32 devices in a mesh: dp: 2 (over x), expert: 16 (over z, y, core).
Axes of the slice: x: 2, y: 2, z: 4, core: 2. Of those that a mesh axis runs over, the one named last changes fastest.
Arguments:
- tokens: bfloat16 [4096, 5120], P(('dp', 'expert')), may hold values from -6 to 6
- cotangent: bfloat16 [4096, 5120], P(('dp', 'expert')), may hold values from -2 to 2
- picks: int32 [32, 16, 4], P(('dp', 'expert')), may hold values from 0 to 127, as said below
- gates: float32 [32, 16, 4], P(('dp', 'expert')), may hold values from 0.05 to 1
- w_gate: bfloat16 [16, 5120, 768], P('expert', 'dp'), may hold values from -0.078125 to 0.078125
- w_up: bfloat16 [16, 5120, 768], P('expert', 'dp'), may hold values from -0.078125 to 0.078125
- w_down: bfloat16 [16, 768, 5120], P('expert', None, 'dp'), may hold values from -0.21875 to 0.21875
Outputs:
- mixed: bfloat16 [4096, 5120], P(('dp', 'expert'))
- token_grad: bfloat16 [4096, 5120], P(('dp', 'expert'))
- gate_grad: float32 [32, 16, 4], P(('dp', 'expert'))
- grad_w_gate: bfloat16 [16, 5120, 768], P('expert', 'dp')
- grad_w_up: bfloat16 [16, 5120, 768], P('expert', 'dp')
- grad_w_down: bfloat16 [16, 768, 5120], P('expert', None, 'dp')
The draws below stay inside these ranges and needn't reach their ends.
Inputs may be any that keep to these rules, and one draw needn't show every extreme that they name: picks[d, e] holds 4 distinct token indices of device d; every expert takes exactly 4 tokens from every device.
All inputs are finite; a program needn't handle non-finite values.
Results may differ from the reference program's by a relative error of at most 0.02.
Values may be sent and summed in bfloat16 or wider, within the bound.
No kernel may reach another device: no remote copies, remote signals or barrier semaphores. Data moves between devices by JAX's collectives and lax.ppermute only.
A program may use at most 64 MiB of HBM per device.

```python
import math
import jax
import jax.numpy as jnp
from jax import lax

D = 5120
FF = 768
TOK_DEV = 128
SLOT = 4
EXPERTS = 16
SOURCES = 32
TOKENS = 4096
N_DP = 2


def draw_picks(key, part):
    subkeys = jax.random.split(jax.random.fold_in(key, 17), SOURCES * EXPERTS)

    def pick_one(subkey):
        return jax.random.permutation(subkey, TOK_DEV)[:SLOT]
    chosen = jax.vmap(pick_one)(subkeys)
    return chosen.reshape(SOURCES, EXPERTS, SLOT).astype(jnp.int32)


def shard_levels(own_key, dims, cuts, low, top_value):
    def one(position, blocks):
        steps = jax.random.uniform(jax.random.fold_in(jax.random.fold_in(own_key, 6), position), (blocks,), jnp.float32, low / len(cuts), top_value / len(cuts))
        return jnp.repeat(jnp.exp(steps), dims[position] // blocks).reshape((-1,) + (1,) * (len(dims) - position - 1))

    gain = one(*cuts[0])
    for cut in cuts[1:]:
        gain = gain * one(*cut)
    return gain


def centred(key, shape, scale, bound, shards=(), held_as=jnp.bfloat16):
    level = shard_levels(key, shape, shards, -0.22, 0.18) if shards else 1.0
    drawn = jax.random.normal(key, shape, jnp.float32) * scale * level
    return jnp.minimum(jnp.maximum(drawn, -bound), bound).astype(held_as)


def setup_inputs(seed: int = 0) -> dict:
    key_list = jax.random.split(jax.random.key(seed), 8)
    return {
        "tokens": centred(key_list[0], (TOKENS, D), 1.0, 6.0, ((0, 32),)),
        "cotangent": centred(key_list[1], (TOKENS, D), 0.25, 2.0, ((0, 32),)),
        "picks": draw_picks(jax.random.fold_in(key_list[7], 71), 0),
        "gates": jnp.clip(jnp.exp(math.log(1.0) - 2.9957323 * jax.random.uniform(key_list[3], (SOURCES, EXPERTS, SLOT), jnp.float32) ** shard_levels(key_list[3], (SOURCES, EXPERTS, SLOT), ((0, 32),), -0.2, 0.2)), 0.05, 1.0),
        "w_gate": centred(key_list[4], (EXPERTS, D, FF), D ** -0.5, 0.078125, ((0, 16), (1, 2))),
        "w_up": centred(key_list[5], (EXPERTS, D, FF), D ** -0.5, 0.078125, ((0, 16), (1, 2))),
        "w_down": centred(key_list[6], (EXPERTS, FF, D), FF ** -0.5, 0.21875, ((0, 16), (2, 2))),
    }


def swiglu_grads(gate_sum, up_sum, back_sum):
    sigmoid_gate = jax.nn.sigmoid(gate_sum)
    silu_gate = gate_sum * sigmoid_gate
    hidden = (silu_gate * up_sum).astype(jnp.bfloat16)
    grad_up = (back_sum * silu_gate).astype(jnp.bfloat16)
    grad_gate = (back_sum * up_sum * sigmoid_gate * (1.0 + gate_sum * (1.0 - sigmoid_gate))).astype(jnp.bfloat16)
    return hidden, grad_gate, grad_up


def blockwise(form, left, right):
    parts = jnp.einsum(form, left, right, precision=lax.Precision.HIGHEST)
    parts = lax.optimization_barrier(parts.astype(jnp.bfloat16)).astype(jnp.float32)
    return jnp.sum(parts, axis=0)


def reference(tokens, cotangent, picks, gates, w_gate, w_up, w_down):
    sources = picks.shape[0]
    expert_count = picks.shape[1]
    slot_count = picks.shape[2]
    model_width = tokens.shape[1]
    per_device = tokens.shape[0] // sources
    hidden_units = w_gate.shape[2]
    slice_width = model_width // N_DP
    row_count = sources * slot_count
    offsets = (jnp.arange(sources, dtype=jnp.int32) * per_device)[:, None, None]
    flat_rows = (picks + offsets).astype(jnp.int32).reshape(-1)
    token_rows = jnp.take(tokens, flat_rows, axis=0).reshape(sources, expert_count, slot_count, model_width)
    grad_rows = jnp.take(cotangent, flat_rows, axis=0).reshape(sources, expert_count, slot_count, model_width)
    scaled = (gates[..., None] * grad_rows.astype(jnp.float32)).astype(jnp.bfloat16)
    by_expert_in = jnp.moveaxis(token_rows, 1, 0).reshape(expert_count, row_count, model_width)
    by_expert_up = jnp.moveaxis(scaled, 1, 0).reshape(expert_count, row_count, model_width)

    def one_expert(operands):
        rows_in, rows_up, gate_w, up_w, down_w = operands
        split_in = rows_in.astype(jnp.float32).reshape(row_count, N_DP, slice_width)
        split_up = rows_up.astype(jnp.float32).reshape(row_count, N_DP, slice_width)
        gate_blocks = gate_w.astype(jnp.float32).reshape(N_DP, slice_width, hidden_units)
        up_blocks = up_w.astype(jnp.float32).reshape(N_DP, slice_width, hidden_units)
        down_blocks = down_w.astype(jnp.float32).reshape(hidden_units, N_DP, slice_width)
        gate_sum = blockwise("rkd,kdf->krf", split_in, gate_blocks)
        up_sum = blockwise("rkd,kdf->krf", split_in, up_blocks)
        back_sum = blockwise("rkd,fkd->krf", split_up, down_blocks)
        hidden, grad_gate, grad_up = swiglu_grads(gate_sum, up_sum, back_sum)
        expert_out = jnp.dot(hidden, down_w, preferred_element_type=jnp.float32).astype(jnp.bfloat16)
        row_grad = (jnp.dot(grad_gate, gate_w.T, preferred_element_type=jnp.float32)
                    + jnp.dot(grad_up, up_w.T, preferred_element_type=jnp.float32)).astype(jnp.bfloat16)
        grad_down = jnp.dot(hidden.T, rows_up, preferred_element_type=jnp.float32).astype(jnp.bfloat16)
        grad_gate_w = jnp.dot(rows_in.T, grad_gate, preferred_element_type=jnp.float32).astype(jnp.bfloat16)
        grad_up_w = jnp.dot(rows_in.T, grad_up, preferred_element_type=jnp.float32).astype(jnp.bfloat16)
        return expert_out, row_grad, grad_gate_w, grad_up_w, grad_down

    expert_out, row_grad, grad_gate_w, grad_up_w, grad_down = lax.map(
        one_expert, (by_expert_in, by_expert_up, w_gate, w_up, w_down))
    out_rows = jnp.moveaxis(expert_out.reshape(expert_count, sources, slot_count, model_width), 0, 1)
    grad_back = jnp.moveaxis(row_grad.reshape(expert_count, sources, slot_count, model_width), 0, 1)
    out_float = out_rows.astype(jnp.float32)
    weighted = (gates[..., None] * out_float).reshape(-1, model_width)
    mixed = jax.ops.segment_sum(weighted, flat_rows, num_segments=tokens.shape[0]).astype(jnp.bfloat16)
    token_grad = jax.ops.segment_sum(grad_back.astype(jnp.float32).reshape(-1, model_width), flat_rows,
                                     num_segments=tokens.shape[0]).astype(jnp.bfloat16)
    gate_grad = jnp.sum(grad_rows.astype(jnp.float32) * out_float, axis=-1)
    return mixed, token_grad, gate_grad, grad_gate_w, grad_up_w, grad_down
```

```python
import functools

import jax
import jax.numpy as jnp
from jax import lax
from jax.experimental import pallas as pl
from jax.experimental.pallas import tpu as pltpu
from jax.sharding import PartitionSpec as P

F32 = jnp.float32
BF16 = jnp.bfloat16
MIB = 1024 * 1024


def dot(left, right, dims=((1,), (0,)), precision=None):
    return lax.dot_general(left, right, (dims, ((), ())), precision=precision, preferred_element_type=F32)


def exact_dot(left, right, dims=((1,), (0,))):
    return dot(left, right, dims, lax.Precision.HIGHEST)


def iota(shape, axis):
    return lax.broadcasted_iota(jnp.int32, shape, axis)


def block_of(width, limit):
    best = 128
    for size in range(128, limit + 1, 128):
        if width % size == 0:
            best = size
    return best


def params(mib):
    return pltpu.CompilerParams(vmem_limit_bytes=mib * MIB)


def spread(values, slots):
    experts = values.shape[0]
    rows = experts * slots * 2
    owner = (iota((rows, experts), 0) // (2 * slots) == iota((rows, experts), 1)).astype(F32)
    wide = exact_dot(owner, values)
    mine = iota((rows, slots), 0) % slots == iota((rows, slots), 1)
    return jnp.sum(jnp.where(mine, wide, 0.0), axis=1, keepdims=True)


def second_half(shape, slots):
    return iota(shape, 0) % (2 * slots) >= slots


def pack_kernel(slots, picks_ref, gates_ref, tokens_ref, cot_ref, out_ref):
    count = tokens_ref.shape[0]
    rows = out_ref.shape[0]
    chosen = spread(picks_ref[0].astype(F32), slots).astype(jnp.int32)
    scale = spread(gates_ref[0], slots)
    late = second_half((rows, count), slots)
    hit = chosen == iota((rows, count), 1)
    from_tokens = jnp.where(hit & ~late, 1.0, 0.0).astype(BF16)
    from_cot = jnp.where(hit & late, 1.0, 0.0).astype(BF16)
    picked = dot(from_tokens, tokens_ref[...]) + dot(from_cot, cot_ref[...])
    factor = jnp.where(second_half((rows, 1), slots), scale, 1.0)
    out_ref[...] = (picked * factor).astype(BF16)


def pack(tokens, cotangent, picks, gates, n_dp):
    experts, slots = picks.shape[1:]
    count, width = tokens.shape
    rows = experts * slots * 2
    part = width // n_dp
    cols = block_of(part, 1280)
    steps = part // cols
    return pl.pallas_call(
        functools.partial(pack_kernel, slots),
        grid=(n_dp, steps),
        in_specs=[
            pl.BlockSpec((1, experts, slots), lambda k, b: (0, 0, 0)),
            pl.BlockSpec((1, experts, slots), lambda k, b: (0, 0, 0)),
            pl.BlockSpec((count, cols), lambda k, b: (0, k * steps + b)),
            pl.BlockSpec((count, cols), lambda k, b: (0, k * steps + b)),
        ],
        out_specs=pl.BlockSpec((rows, cols), lambda k, b: (k, b)),
        out_shape=jax.ShapeDtypeStruct((n_dp * rows, part), BF16),
        compiler_params=params(16),
        name="pack_rows",
    )(picks, gates, tokens, cotangent)


def split_rows(packed, slots, late):
    total = packed.shape[0]
    group = min(total, 256)
    kept = group // 2
    source = iota((kept, group), 0) // slots * (2 * slots) + iota((kept, group), 0) % slots + late * slots
    take = jnp.where(source == iota((kept, group), 1), 1.0, 0.0).astype(BF16)
    parts = [dot(take, packed[g : g + group]).astype(BF16) for g in range(0, total, group)]
    return parts[0] if len(parts) == 1 else jnp.concatenate(parts, axis=0)


def merge_rows(first, second, slots):
    shown = first if first is not None else second
    total = shown.shape[0]
    kept = min(total, 128)
    group = 2 * kept
    result = []
    for g in range(0, total, kept):
        acc = None
        for late, value in enumerate((first, second)):
            if value is None:
                continue
            source = iota((group, kept), 1) // slots * (2 * slots) + iota((group, kept), 1) % slots + late * slots
            put = jnp.where(source == iota((group, kept), 0), 1.0, 0.0).astype(BF16)
            term = dot(put, value[g : g + kept])
            acc = term if acc is None else acc + term
        result.append(acc.astype(BF16))
    return result[0] if len(result) == 1 else jnp.concatenate(result, axis=0)


def terms_kernel(slots, packed_ref, gate_ref, up_ref, down_ref, out_ref, acc_ref):
    hidden = gate_ref.shape[2]
    step = pl.program_id(0)
    packed = packed_ref[...]
    rows_in = split_rows(packed, slots, 0)
    rows_up = split_rows(packed, slots, 1)

    @pl.when(step == 0)
    def _():
        acc_ref[...] = jnp.zeros_like(acc_ref)

    acc_ref[:, :hidden] += dot(rows_in, gate_ref[0])
    acc_ref[:, hidden : 2 * hidden] += dot(rows_in, up_ref[0])
    acc_ref[:, 2 * hidden :] += dot(rows_up, down_ref[0], ((1,), (1,)))

    @pl.when(step == pl.num_programs(0) - 1)
    def _():
        out_ref[...] = acc_ref[...].astype(BF16)


def terms(packed, w_gate, w_up, w_down, slots):
    total, part = packed.shape
    hidden = w_gate.shape[2]
    cols = block_of(part, 640)
    rows = total // 2
    return pl.pallas_call(
        functools.partial(terms_kernel, slots),
        grid=(part // cols,),
        in_specs=[
            pl.BlockSpec((total, cols), lambda b: (0, b)),
            pl.BlockSpec((1, cols, hidden), lambda b: (0, b, 0)),
            pl.BlockSpec((1, cols, hidden), lambda b: (0, b, 0)),
            pl.BlockSpec((1, hidden, cols), lambda b: (0, 0, b)),
        ],
        out_specs=pl.BlockSpec((rows, 3 * hidden), lambda b: (0, 0)),
        out_shape=jax.ShapeDtypeStruct((rows, 3 * hidden), BF16),
        scratch_shapes=[pltpu.VMEM((rows, 3 * hidden), F32)],
        compiler_params=params(48),
        cost_estimate=pl.CostEstimate(
            flops=2 * rows * part * 3 * hidden, bytes_accessed=6 * part * hidden, transcendentals=0
        ),
        name="partial_products",
    )(packed, w_gate, w_up, w_down)


def results_kernel(slots, count, *refs):
    term_refs = refs[:count]
    gate_ref, up_ref, down_ref, out_ref, acts_ref, own_ref = refs[count:]
    hidden = gate_ref.shape[2]

    @pl.when(pl.program_id(0) == 0)
    def _():
        total = term_refs[0][...].astype(F32)
        for ref in term_refs[1:]:
            total = total + ref[...].astype(F32)
        gate_sum = total[:, :hidden]
        up_sum = total[:, hidden : 2 * hidden]
        back_sum = total[:, 2 * hidden :]
        sig = jax.nn.sigmoid(gate_sum)
        silu = gate_sum * sig
        act = (silu * up_sum).astype(BF16)
        grad_up = (back_sum * silu).astype(BF16)
        grad_gate = (back_sum * up_sum * sig * (1.0 + gate_sum * (1.0 - sig))).astype(BF16)
        own_ref[:, :hidden] = act
        own_ref[:, hidden : 2 * hidden] = grad_gate
        own_ref[:, 2 * hidden :] = grad_up
        acts_ref[:, :hidden] = merge_rows(None, act, slots)
        acts_ref[:, hidden : 2 * hidden] = merge_rows(grad_gate, None, slots)
        acts_ref[:, 2 * hidden :] = merge_rows(grad_up, None, slots)

    out = dot(own_ref[:, :hidden], down_ref[0]).astype(BF16)
    grad = (
        dot(own_ref[:, hidden : 2 * hidden], gate_ref[0], ((1,), (1,)))
        + dot(own_ref[:, 2 * hidden :], up_ref[0], ((1,), (1,)))
    ).astype(BF16)
    out_ref[...] = merge_rows(out, grad, slots)


def results(shares, w_gate, w_up, w_down, slots):
    rows = shares[0].shape[0]
    part, hidden = w_gate.shape[1:]
    cols = block_of(part, 640)
    whole = pl.BlockSpec((rows, 3 * hidden), lambda b: (0, 0))
    return pl.pallas_call(
        functools.partial(results_kernel, slots, len(shares)),
        grid=(part // cols,),
        in_specs=[whole] * len(shares)
        + [
            pl.BlockSpec((1, cols, hidden), lambda b: (0, b, 0)),
            pl.BlockSpec((1, cols, hidden), lambda b: (0, b, 0)),
            pl.BlockSpec((1, hidden, cols), lambda b: (0, 0, b)),
        ],
        out_specs=[
            pl.BlockSpec((2 * rows, cols), lambda b: (0, b)),
            pl.BlockSpec((2 * rows, 3 * hidden), lambda b: (0, 0)),
        ],
        out_shape=[
            jax.ShapeDtypeStruct((2 * rows, part), BF16),
            jax.ShapeDtypeStruct((2 * rows, 3 * hidden), BF16),
        ],
        scratch_shapes=[pltpu.VMEM((rows, 3 * hidden), BF16)],
        compiler_params=params(48),
        cost_estimate=pl.CostEstimate(
            flops=2 * rows * part * 3 * hidden, bytes_accessed=6 * part * hidden, transcendentals=rows * hidden
        ),
        name="expert_rows",
    )(*shares, w_gate, w_up, w_down)


def weights_kernel(packed_ref, acts_ref, gate_ref, up_ref, down_ref):
    hidden = gate_ref.shape[2]
    packed = packed_ref[...]
    gate_ref[0] = dot(packed, acts_ref[:, hidden : 2 * hidden], ((0,), (0,))).astype(BF16)
    up_ref[0] = dot(packed, acts_ref[:, 2 * hidden :], ((0,), (0,))).astype(BF16)
    down_ref[0] = dot(acts_ref[:, :hidden], packed, ((0,), (0,))).astype(BF16)


def weight_grads(packed, acts):
    total, part = packed.shape
    hidden = acts.shape[1] // 3
    cols = block_of(part, 640)
    return pl.pallas_call(
        weights_kernel,
        grid=(part // cols,),
        in_specs=[
            pl.BlockSpec((total, cols), lambda b: (0, b)),
            pl.BlockSpec((total, 3 * hidden), lambda b: (0, 0)),
        ],
        out_specs=[
            pl.BlockSpec((1, cols, hidden), lambda b: (0, b, 0)),
            pl.BlockSpec((1, cols, hidden), lambda b: (0, b, 0)),
            pl.BlockSpec((1, hidden, cols), lambda b: (0, 0, b)),
        ],
        out_shape=[
            jax.ShapeDtypeStruct((1, part, hidden), BF16),
            jax.ShapeDtypeStruct((1, part, hidden), BF16),
            jax.ShapeDtypeStruct((1, hidden, part), BF16),
        ],
        compiler_params=params(48),
        cost_estimate=pl.CostEstimate(
            flops=2 * total * part * 3 * hidden, bytes_accessed=6 * part * hidden, transcendentals=0
        ),
        name="weight_grads",
    )(packed, acts)


def combine_kernel(slots, picks_ref, gates_ref, back_ref, cot_ref, mixed_ref, grad_ref, gate_grad_ref, acc_ref):
    count = cot_ref.shape[0]
    rows = back_ref.shape[0]
    experts = picks_ref.shape[1]
    first = (pl.program_id(0) == 0) & (pl.program_id(1) == 0)
    last = (pl.program_id(0) == pl.num_programs(0) - 1) & (pl.program_id(1) == pl.num_programs(1) - 1)
    chosen = spread(picks_ref[0].astype(F32), slots).astype(jnp.int32)
    scale = spread(gates_ref[0], slots)
    late = second_half((rows, count), slots)
    hit = chosen == iota((rows, count), 1)
    back = back_ref[...]
    ones = jnp.where(hit & late, 1.0, 0.0).astype(BF16)
    rest = jnp.where(hit & ~late, scale, 0.0)
    mixed = None
    for _ in range(3):
        piece = rest.astype(BF16)
        rest = rest - piece.astype(F32)
        term = dot(piece, back, ((0,), (0,)))
        mixed = term if mixed is None else mixed + term
    mixed_ref[...] = mixed.astype(BF16)
    grad_ref[...] = dot(ones, back, ((0,), (0,))).astype(BF16)

    @pl.when(first)
    def _():
        acc_ref[...] = jnp.zeros_like(acc_ref)

    acc_ref[...] += dot(back, cot_ref[...], ((1,), (1,)))

    @pl.when(last)
    def _():
        values = jnp.sum(jnp.where(hit & ~late, acc_ref[...], 0.0), axis=1, keepdims=True)
        mine = iota((rows, slots), 0) % slots == iota((rows, slots), 1)
        owner = (iota((rows, experts), 0) // (2 * slots) == iota((rows, experts), 1)).astype(F32)
        gate_grad_ref[0] = exact_dot(owner, jnp.where(mine, values, 0.0), ((0,), (0,)))


def combine(back, cotangent, picks, gates, n_dp):
    experts, slots = picks.shape[1:]
    count, width = cotangent.shape
    rows = experts * slots * 2
    part = width // n_dp
    cols = block_of(part, 1280)
    steps = part // cols
    return pl.pallas_call(
        functools.partial(combine_kernel, slots),
        grid=(n_dp, steps),
        in_specs=[
            pl.BlockSpec((1, experts, slots), lambda k, b: (0, 0, 0)),
            pl.BlockSpec((1, experts, slots), lambda k, b: (0, 0, 0)),
            pl.BlockSpec((rows, cols), lambda k, b: (k, b)),
            pl.BlockSpec((count, cols), lambda k, b: (0, k * steps + b)),
        ],
        out_specs=[
            pl.BlockSpec((count, cols), lambda k, b: (0, k * steps + b)),
            pl.BlockSpec((count, cols), lambda k, b: (0, k * steps + b)),
            pl.BlockSpec((1, experts, slots), lambda k, b: (0, 0, 0)),
        ],
        out_shape=[
            jax.ShapeDtypeStruct((count, width), BF16),
            jax.ShapeDtypeStruct((count, width), BF16),
            jax.ShapeDtypeStruct((1, experts, slots), F32),
        ],
        scratch_shapes=[pltpu.VMEM((rows, count), F32)],
        compiler_params=params(16),
        name="combine_rows",
    )(picks, gates, back, cotangent)


def body(n_dp, tokens, cotangent, picks, gates, w_gate, w_up, w_down):
    slots = picks.shape[2]
    everyone = ("dp", "expert")
    outgoing = pack(tokens, cotangent, picks, gates, n_dp)
    packed = lax.all_to_all(outgoing, everyone, split_axis=0, concat_axis=0, tiled=True)
    own = terms(packed, w_gate, w_up, w_down, slots)
    shares = [own] + [
        lax.ppermute(own, "dp", [(i, (i + shift) % n_dp) for i in range(n_dp)]) for shift in range(1, n_dp)
    ]
    if n_dp > 2:
        shares = [functools.reduce(jnp.add, [share.astype(F32) for share in shares])]
    returning, acts = results(shares, w_gate, w_up, w_down, slots)
    back = lax.all_to_all(returning, everyone, split_axis=0, concat_axis=0, tiled=True)
    grad_gate_w, grad_up_w, grad_down = weight_grads(packed, acts)
    mixed, token_grad, gate_grad = combine(back, cotangent, picks, gates, n_dp)
    return mixed, token_grad, gate_grad, grad_gate_w, grad_up_w, grad_down


def solution(mesh):
    rows = P(("dp", "expert"), None)
    lists = P(("dp", "expert"), None, None)
    tall = P("expert", "dp", None)
    wide = P("expert", None, "dp")
    return jax.shard_map(
        functools.partial(body, mesh.shape["dp"]),
        mesh=mesh,
        in_specs=(rows, rows, lists, lists, tall, tall, wide),
        out_specs=(rows, rows, lists, tall, tall, wide),
        check_vma=False,
    )
```

```python
import functools

import jax
import jax.numpy as jnp
from jax import lax
from jax.experimental import pallas as pl
from jax.experimental.pallas import tpu as pltpu
from jax.sharding import PartitionSpec as P

F32 = jnp.float32
BF16 = jnp.bfloat16
MIB = 1024 * 1024


def dot(left, right, dims=((1,), (0,)), precision=None):
    return lax.dot_general(left, right, (dims, ((), ())), precision=precision, preferred_element_type=F32)


def exact_dot(left, right, dims=((1,), (0,))):
    return dot(left, right, dims, lax.Precision.HIGHEST)


def iota(shape, axis):
    return lax.broadcasted_iota(jnp.int32, shape, axis)


def block_of(width, limit):
    best = 128
    for size in range(128, limit + 1, 128):
        if width % size == 0:
            best = size
    return best


def params(mib):
    return pltpu.CompilerParams(vmem_limit_bytes=mib * MIB)


def spread(values, slots):
    experts = values.shape[0]
    rows = experts * slots * 2
    owner = (iota((rows, experts), 0) // (2 * slots) == iota((rows, experts), 1)).astype(F32)
    wide = exact_dot(owner, values)
    mine = iota((rows, slots), 0) % slots == iota((rows, slots), 1)
    return jnp.sum(jnp.where(mine, wide, 0.0), axis=1, keepdims=True)


def second_half(shape, slots):
    return iota(shape, 0) % (2 * slots) >= slots


def pack_kernel(slots, picks_ref, gates_ref, tokens_ref, cot_ref, out_ref):
    count = tokens_ref.shape[0]
    rows = out_ref.shape[0]
    chosen = spread(picks_ref[0].astype(F32), slots).astype(jnp.int32)
    scale = spread(gates_ref[0], slots)
    late = second_half((rows, count), slots)
    hit = chosen == iota((rows, count), 1)
    from_tokens = jnp.where(hit & ~late, 1.0, 0.0).astype(BF16)
    from_cot = jnp.where(hit & late, 1.0, 0.0).astype(BF16)
    picked = dot(from_tokens, tokens_ref[...]) + dot(from_cot, cot_ref[...])
    factor = jnp.where(second_half((rows, 1), slots), scale, 1.0)
    out_ref[...] = (picked * factor).astype(BF16)


def pack(tokens, cotangent, picks, gates, n_dp):
    experts, slots = picks.shape[1:]
    count, width = tokens.shape
    rows = experts * slots * 2
    part = width // n_dp
    cols = block_of(part, 1280)
    steps = part // cols
    return pl.pallas_call(
        functools.partial(pack_kernel, slots),
        grid=(n_dp, steps),
        in_specs=[
            pl.BlockSpec((1, experts, slots), lambda k, b: (0, 0, 0)),
            pl.BlockSpec((1, experts, slots), lambda k, b: (0, 0, 0)),
            pl.BlockSpec((count, cols), lambda k, b: (0, k * steps + b)),
            pl.BlockSpec((count, cols), lambda k, b: (0, k * steps + b)),
        ],
        out_specs=pl.BlockSpec((rows, cols), lambda k, b: (k, b)),
        out_shape=jax.ShapeDtypeStruct((n_dp * rows, part), BF16),
        compiler_params=params(16),
        name="pack_rows",
    )(picks, gates, tokens, cotangent)


def split_rows(packed, slots, late):
    total = packed.shape[0]
    group = min(total, 256)
    kept = group // 2
    source = iota((kept, group), 0) // slots * (2 * slots) + iota((kept, group), 0) % slots + late * slots
    take = jnp.where(source == iota((kept, group), 1), 1.0, 0.0).astype(BF16)
    parts = [dot(take, packed[g : g + group]).astype(BF16) for g in range(0, total, group)]
    return parts[0] if len(parts) == 1 else jnp.concatenate(parts, axis=0)


def merge_rows(first, second, slots):
    shown = first if first is not None else second
    total = shown.shape[0]
    kept = min(total, 128)
    group = 2 * kept
    result = []
    for g in range(0, total, kept):
        acc = None
        for late, value in enumerate((first, second)):
            if value is None:
                continue
            source = iota((group, kept), 1) // slots * (2 * slots) + iota((group, kept), 1) % slots + late * slots
            put = jnp.where(source == iota((group, kept), 0), 1.0, 0.0).astype(BF16)
            term = dot(put, value[g : g + kept])
            acc = term if acc is None else acc + term
        result.append(acc.astype(BF16))
    return result[0] if len(result) == 1 else jnp.concatenate(result, axis=0)


def terms_kernel(slots, packed_ref, gate_ref, up_ref, down_ref, out_ref, acc_ref):
    hidden = gate_ref.shape[2]
    step = pl.program_id(0)
    packed = packed_ref[...]
    rows_in = split_rows(packed, slots, 0)
    rows_up = split_rows(packed, slots, 1)

    @pl.when(step == 0)
    def _():
        acc_ref[...] = jnp.zeros_like(acc_ref)

    acc_ref[:, :hidden] += dot(rows_in, gate_ref[0])
    acc_ref[:, hidden : 2 * hidden] += dot(rows_in, up_ref[0])
    acc_ref[:, 2 * hidden :] += dot(rows_up, down_ref[0], ((1,), (1,)))

    @pl.when(step == pl.num_programs(0) - 1)
    def _():
        out_ref[...] = acc_ref[...].astype(BF16)


def terms(packed, w_gate, w_up, w_down, slots):
    total, part = packed.shape
    hidden = w_gate.shape[2]
    cols = block_of(part, 640)
    rows = total // 2
    return pl.pallas_call(
        functools.partial(terms_kernel, slots),
        grid=(part // cols,),
        in_specs=[
            pl.BlockSpec((total, cols), lambda b: (0, b)),
            pl.BlockSpec((1, cols, hidden), lambda b: (0, b, 0)),
            pl.BlockSpec((1, cols, hidden), lambda b: (0, b, 0)),
            pl.BlockSpec((1, hidden, cols), lambda b: (0, 0, b)),
        ],
        out_specs=pl.BlockSpec((rows, 3 * hidden), lambda b: (0, 0)),
        out_shape=jax.ShapeDtypeStruct((rows, 3 * hidden), BF16),
        scratch_shapes=[pltpu.VMEM((rows, 3 * hidden), F32)],
        compiler_params=params(48),
        cost_estimate=pl.CostEstimate(
            flops=2 * rows * part * 3 * hidden, bytes_accessed=6 * part * hidden, transcendentals=0
        ),
        name="partial_products",
    )(packed, w_gate, w_up, w_down)


def results_kernel(slots, count, *refs):
    term_refs = refs[:count]
    gate_ref, up_ref, down_ref, out_ref, acts_ref, own_ref = refs[count:]
    hidden = gate_ref.shape[2]

    @pl.when(pl.program_id(0) == 0)
    def _():
        total = term_refs[0][...].astype(F32)
        for ref in term_refs[1:]:
            total = total + ref[...].astype(F32)
        gate_sum = total[:, :hidden]
        up_sum = total[:, hidden : 2 * hidden]
        back_sum = total[:, 2 * hidden :]
        sig = jax.nn.sigmoid(gate_sum)
        silu = gate_sum * sig
        act = (silu * up_sum).astype(BF16)
        grad_up = (back_sum * silu).astype(BF16)
        grad_gate = (back_sum * up_sum * sig * (1.0 + gate_sum * (1.0 - sig))).astype(BF16)
        own_ref[:, :hidden] = act
        own_ref[:, hidden : 2 * hidden] = grad_gate
        own_ref[:, 2 * hidden :] = grad_up
        acts_ref[:, :hidden] = merge_rows(None, act, slots)
        acts_ref[:, hidden : 2 * hidden] = merge_rows(grad_gate, None, slots)
        acts_ref[:, 2 * hidden :] = merge_rows(grad_up, None, slots)

    out = dot(own_ref[:, :hidden], down_ref[0]).astype(BF16)
    grad = (
        dot(own_ref[:, hidden : 2 * hidden], gate_ref[0], ((1,), (1,)))
        + dot(own_ref[:, 2 * hidden :], up_ref[0], ((1,), (1,)))
    ).astype(BF16)
    out_ref[...] = merge_rows(out, grad, slots)


def results(shares, w_gate, w_up, w_down, slots):
    rows = shares[0].shape[0]
    part, hidden = w_gate.shape[1:]
    cols = block_of(part, 640)
    whole = pl.BlockSpec((rows, 3 * hidden), lambda b: (0, 0))
    return pl.pallas_call(
        functools.partial(results_kernel, slots, len(shares)),
        grid=(part // cols,),
        in_specs=[whole] * len(shares)
        + [
            pl.BlockSpec((1, cols, hidden), lambda b: (0, b, 0)),
            pl.BlockSpec((1, cols, hidden), lambda b: (0, b, 0)),
            pl.BlockSpec((1, hidden, cols), lambda b: (0, 0, b)),
        ],
        out_specs=[
            pl.BlockSpec((2 * rows, cols), lambda b: (0, b)),
            pl.BlockSpec((2 * rows, 3 * hidden), lambda b: (0, 0)),
        ],
        out_shape=[
            jax.ShapeDtypeStruct((2 * rows, part), BF16),
            jax.ShapeDtypeStruct((2 * rows, 3 * hidden), BF16),
        ],
        scratch_shapes=[pltpu.VMEM((rows, 3 * hidden), BF16)],
        compiler_params=params(48),
        cost_estimate=pl.CostEstimate(
            flops=2 * rows * part * 3 * hidden, bytes_accessed=6 * part * hidden, transcendentals=rows * hidden
        ),
        name="expert_rows",
    )(*shares, w_gate, w_up, w_down)


def weights_kernel(packed_ref, acts_ref, gate_ref, up_ref, down_ref):
    hidden = gate_ref.shape[2]
    packed = packed_ref[...]
    gate_ref[0] = dot(packed, acts_ref[:, hidden : 2 * hidden], ((0,), (0,))).astype(BF16)
    up_ref[0] = dot(packed, acts_ref[:, 2 * hidden :], ((0,), (0,))).astype(BF16)
    down_ref[0] = dot(acts_ref[:, :hidden], packed, ((0,), (0,))).astype(BF16)


def weight_grads(packed, acts):
    total, part = packed.shape
    hidden = acts.shape[1] // 3
    cols = block_of(part, 640)
    return pl.pallas_call(
        weights_kernel,
        grid=(part // cols,),
        in_specs=[
            pl.BlockSpec((total, cols), lambda b: (0, b)),
            pl.BlockSpec((total, 3 * hidden), lambda b: (0, 0)),
        ],
        out_specs=[
            pl.BlockSpec((1, cols, hidden), lambda b: (0, b, 0)),
            pl.BlockSpec((1, cols, hidden), lambda b: (0, b, 0)),
            pl.BlockSpec((1, hidden, cols), lambda b: (0, 0, b)),
        ],
        out_shape=[
            jax.ShapeDtypeStruct((1, part, hidden), BF16),
            jax.ShapeDtypeStruct((1, part, hidden), BF16),
            jax.ShapeDtypeStruct((1, hidden, part), BF16),
        ],
        compiler_params=params(48),
        cost_estimate=pl.CostEstimate(
            flops=2 * total * part * 3 * hidden, bytes_accessed=6 * part * hidden, transcendentals=0
        ),
        name="weight_grads",
    )(packed, acts)


def combine_kernel(slots, picks_ref, gates_ref, back_ref, cot_ref, mixed_ref, grad_ref, gate_grad_ref, acc_ref):
    count = cot_ref.shape[0]
    rows = back_ref.shape[0]
    experts = picks_ref.shape[1]
    first = (pl.program_id(0) == 0) & (pl.program_id(1) == 0)
    last = (pl.program_id(0) == pl.num_programs(0) - 1) & (pl.program_id(1) == pl.num_programs(1) - 1)
    chosen = spread(picks_ref[0].astype(F32), slots).astype(jnp.int32)
    scale = spread(gates_ref[0], slots)
    late = second_half((rows, count), slots)
    hit = chosen == iota((rows, count), 1)
    back = back_ref[...]
    ones = jnp.where(hit & late, 1.0, 0.0).astype(BF16)
    rest = jnp.where(hit & ~late, scale, 0.0)
    mixed = None
    for _ in range(3):
        piece = rest.astype(BF16)
        rest = rest - piece.astype(F32)
        term = dot(piece, back, ((0,), (0,)))
        mixed = term if mixed is None else mixed + term
    mixed_ref[...] = mixed.astype(BF16)
    grad_ref[...] = dot(ones, back, ((0,), (0,))).astype(BF16)

    @pl.when(first)
    def _():
        acc_ref[...] = jnp.zeros_like(acc_ref)

    acc_ref[...] += dot(back, cot_ref[...], ((1,), (1,)))

    @pl.when(last)
    def _():
        values = jnp.sum(jnp.where(hit & ~late, acc_ref[...], 0.0), axis=1, keepdims=True)
        mine = iota((rows, slots), 0) % slots == iota((rows, slots), 1)
        owner = (iota((rows, experts), 0) // (2 * slots) == iota((rows, experts), 1)).astype(F32)
        gate_grad_ref[0] = exact_dot(owner, jnp.where(mine, values, 0.0), ((0,), (0,)))


def combine(back, cotangent, picks, gates, n_dp):
    experts, slots = picks.shape[1:]
    count, width = cotangent.shape
    rows = experts * slots * 2
    part = width // n_dp
    cols = block_of(part, 1280)
    steps = part // cols
    return pl.pallas_call(
        functools.partial(combine_kernel, slots),
        grid=(n_dp, steps),
        in_specs=[
            pl.BlockSpec((1, experts, slots), lambda k, b: (0, 0, 0)),
            pl.BlockSpec((1, experts, slots), lambda k, b: (0, 0, 0)),
            pl.BlockSpec((rows, cols), lambda k, b: (k, b)),
            pl.BlockSpec((count, cols), lambda k, b: (0, k * steps + b)),
        ],
        out_specs=[
            pl.BlockSpec((count, cols), lambda k, b: (0, k * steps + b)),
            pl.BlockSpec((count, cols), lambda k, b: (0, k * steps + b)),
            pl.BlockSpec((1, experts, slots), lambda k, b: (0, 0, 0)),
        ],
        out_shape=[
            jax.ShapeDtypeStruct((count, width), BF16),
            jax.ShapeDtypeStruct((count, width), BF16),
            jax.ShapeDtypeStruct((1, experts, slots), F32),
        ],
        scratch_shapes=[pltpu.VMEM((rows, count), F32)],
        compiler_params=params(16),
        name="combine_rows",
    )(picks, gates, back, cotangent)


def body(n_dp, tokens, cotangent, picks, gates, w_gate, w_up, w_down):
    slots = picks.shape[2]
    everyone = ("dp", "expert")
    outgoing = pack(tokens, cotangent, picks, gates, n_dp)
    packed = lax.all_to_all(outgoing, everyone, split_axis=0, concat_axis=0, tiled=True)
    own = terms(packed, w_gate, w_up, w_down, slots)
    shares = [own] + [
        lax.ppermute(own, "dp", [(i, (i + shift) % n_dp) for i in range(n_dp)]) for shift in range(1, n_dp)
    ]
    if n_dp > 2:
        shares = [functools.reduce(jnp.add, [share.astype(F32) for share in shares])]
    returning, acts = results(shares, w_gate, w_up, w_down, slots)
    back = lax.all_to_all(returning, everyone, split_axis=0, concat_axis=0, tiled=True)
    grad_gate_w, grad_up_w, grad_down = weight_grads(packed, acts)
    mixed, token_grad, gate_grad = combine(back, cotangent, picks, gates, n_dp)
    return mixed, token_grad, gate_grad, grad_gate_w, grad_up_w, grad_down


def xor_ids(own, shape, axis, group):
    return jnp.bitwise_xor(own, iota(shape, axis) // group)


def spread_column(values, own, slots):
    experts = values.shape[1]
    rows = experts * 4 * slots
    owner = (xor_ids(own, (rows, experts), 0, 4 * slots) == iota((rows, experts), 1)).astype(F32)
    wide = exact_dot(owner, values, ((1,), (1,)))
    mine = iota((rows, slots), 0) % slots == iota((rows, slots), 1)
    return jnp.sum(jnp.where(mine, wide, 0.0), axis=1, keepdims=True)


def spread_row(values, own, slots):
    experts = values.shape[1]
    rows = experts * 4 * slots
    owner = (xor_ids(own, (experts, rows), 1, 4 * slots) == iota((experts, rows), 0)).astype(F32)
    wide = exact_dot(values, owner)
    mine = iota((slots, rows), 1) % slots == iota((slots, rows), 0)
    return jnp.sum(jnp.where(mine, wide, 0.0), axis=0, keepdims=True)


def far_columns(half, part, block, width):
    return pl.ds(pl.multiple_of(half * part + block * width, 128), width)


def send_kernel(slots, picks_ref, gates_ref, tokens_ref, cot_ref, *refs):
    experts = picks_ref.shape[1]
    outs, (held_ref, sems) = refs[: 2 * experts], refs[2 * experts :]
    count, width = tokens_ref.shape
    part = width // 2
    cols = part // 2
    own_half = lax.axis_index("dp")
    own = lax.axis_index("expert")
    copies = {}
    for far in range(2):
        for block in range(2):
            for kind, source in enumerate((tokens_ref, cot_ref)):
                copy = pltpu.make_async_copy(
                    source.at[:, far_columns(jnp.bitwise_xor(own_half, far), part, block, cols)],
                    held_ref.at[far, pl.ds((2 * block + kind) * count, count)],
                    sems.at[far, block, kind],
                )
                copy.start()
                copies[far, block, kind] = copy
    rows = experts * 4 * slots
    chosen = spread_column(picks_ref[...].astype(F32), own, slots).astype(jnp.int32)
    scale = spread_column(gates_ref[...], own, slots)
    place = iota((rows, 1), 0) % (4 * slots)
    late = place % (2 * slots) >= slots
    factor = jnp.where(late, scale, 1.0)
    target = chosen + jnp.where(late, count, 0) + place // (2 * slots) * (2 * count)
    take = jnp.where(target == iota((rows, 4 * count), 1), 1.0, 0.0).astype(BF16)
    for far in range(2):
        for block in range(2):
            for kind in range(2):
                copies[far, block, kind].wait()
        picked = (dot(take, held_ref[far]) * factor).astype(BF16)
        for near in range(experts):
            outs[far * experts + near][...] = picked[near * 4 * slots : (near + 1) * 4 * slots]


def vmem():
    return pl.BlockSpec(memory_space=pltpu.VMEM)


def hbm():
    return pl.BlockSpec(memory_space=pltpu.HBM)


def in_hbm(value):
    return pltpu.with_memory_space_constraint(value, pltpu.HBM)


def send_rows(tokens, cotangent, picks, gates):
    slots, experts = picks.shape
    count, width = tokens.shape
    message = jax.ShapeDtypeStruct((4 * slots, width // 4), BF16)
    return pl.pallas_call(
        functools.partial(send_kernel, slots),
        in_specs=[vmem(), vmem(), hbm(), hbm()],
        out_specs=[vmem()] * (2 * experts),
        out_shape=[message] * (2 * experts),
        scratch_shapes=[pltpu.VMEM((2, 4 * count, width // 4), BF16), pltpu.SemaphoreType.DMA((2, 2, 2))],
        compiler_params=params(24),
        name="send_rows",
    )(picks, gates, in_hbm(tokens), in_hbm(cotangent))


def sort_matrix(slots, experts, back):
    rows = experts * 4 * slots
    a = iota((rows, rows), 1 if back else 0)
    b = iota((rows, rows), 0 if back else 1)
    group = experts * slots
    source = a % group // slots * (4 * slots) + a // group % 2 * (2 * slots) + a // (2 * group) * slots + a % slots
    return jnp.where(source == b, 1.0, 0.0).astype(BF16)


def sums_kernel(slots, experts, *refs):
    messages = refs[: 2 * experts]
    gate_ref, up_ref, down_ref, out_ref, rows_ref = refs[2 * experts :]
    hidden = gate_ref.shape[2]
    cols = messages[0].shape[1]
    group = experts * slots
    order = sort_matrix(slots, experts, False)
    for far in range(2):
        stacked = jnp.concatenate([messages[far * experts + near][...] for near in range(experts)], axis=0)
        ordered = dot(order, stacked).astype(BF16)
        for kind in range(2):
            for block in range(2):
                start = (2 * kind + block) * group
                rows_ref[kind, block, far * group : (far + 1) * group, :] = ordered[start : start + group]
    for place, ref in enumerate((gate_ref, up_ref, down_ref)):
        acc = None
        for block in range(2):
            span = slice(block * cols, (block + 1) * cols)
            if place < 2:
                term = dot(rows_ref[0, block], ref[0, span, :])
            else:
                term = dot(rows_ref[1, block], ref[0, :, span], ((1,), (1,)))
            acc = term if acc is None else acc + term
        out_ref[:, place * hidden : (place + 1) * hidden] = acc.astype(BF16)


def column_sums(messages, w_gate, w_up, w_down, slots):
    experts = len(messages) // 2
    rows = 2 * experts * slots
    part, hidden = w_gate.shape[1:]
    return pl.pallas_call(
        functools.partial(sums_kernel, slots, experts),
        in_specs=[vmem()] * (2 * experts + 3),
        out_specs=[vmem()] * 2,
        out_shape=[
            jax.ShapeDtypeStruct((rows, 3 * hidden), BF16),
            jax.ShapeDtypeStruct((2, 2, rows, part // 2), BF16),
        ],
        compiler_params=params(24),
        cost_estimate=pl.CostEstimate(
            flops=2 * rows * part * 3 * hidden, bytes_accessed=6 * part * hidden, transcendentals=0
        ),
        name="column_sums",
    )(*messages, w_gate, w_up, w_down)


def reply_kernel(slots, experts, own_ref, other_ref, gate_ref, up_ref, down_ref, acts_ref, *outs):
    hidden = gate_ref.shape[2]
    cols = outs[0].shape[1]
    group = experts * slots
    for far in range(2):
        mine = slice(far * group, (far + 1) * group)
        theirs = slice((1 - far) * group, (2 - far) * group)

        def total(place):
            span = slice(place * hidden, (place + 1) * hidden)
            return own_ref[mine, span].astype(F32) + other_ref[theirs, span].astype(F32)

        gate_sum, up_sum, back_sum = total(0), total(1), total(2)
        sig = jax.nn.sigmoid(gate_sum)
        silu = gate_sum * sig
        acts_ref[mine, :hidden] = (silu * up_sum).astype(BF16)
        acts_ref[mine, hidden : 2 * hidden] = (back_sum * up_sum * sig * (1.0 + gate_sum * (1.0 - sig))).astype(BF16)
        acts_ref[mine, 2 * hidden :] = (back_sum * silu).astype(BF16)
    made = {}
    for block in range(2):
        span = slice(block * cols, (block + 1) * cols)
        made[0, block] = dot(acts_ref[:, :hidden], down_ref[0, :, span]).astype(BF16)
        made[1, block] = (
            dot(acts_ref[:, hidden : 2 * hidden], gate_ref[0, span, :], ((1,), (1,)))
            + dot(acts_ref[:, 2 * hidden :], up_ref[0, span, :], ((1,), (1,)))
        ).astype(BF16)
    order = sort_matrix(slots, experts, True)
    for far in range(2):
        mine = slice(far * group, (far + 1) * group)
        stacked = jnp.concatenate([made[kind, block][mine] for kind in range(2) for block in range(2)], axis=0)
        ordered = dot(order, stacked).astype(BF16)
        for near in range(experts):
            outs[far * experts + near][...] = ordered[near * 4 * slots : (near + 1) * 4 * slots]


def reply_rows(own, other, w_gate, w_up, w_down, slots):
    rows = own.shape[0]
    part, hidden = w_gate.shape[1:]
    experts = rows // (2 * slots)
    return pl.pallas_call(
        functools.partial(reply_kernel, slots, experts),
        in_specs=[vmem()] * 5,
        out_specs=[vmem()] * (2 * experts + 1),
        out_shape=[jax.ShapeDtypeStruct((rows, 3 * hidden), BF16)]
        + [jax.ShapeDtypeStruct((4 * slots, part // 2), BF16)] * (2 * experts),
        compiler_params=params(24),
        cost_estimate=pl.CostEstimate(
            flops=2 * rows * part * 3 * hidden, bytes_accessed=6 * part * hidden, transcendentals=rows * hidden
        ),
        name="reply_rows",
    )(own, other, w_gate, w_up, w_down)


def ordered_weights_kernel(rows_ref, acts_ref, gate_ref, up_ref, down_ref):
    hidden = gate_ref.shape[2]
    rows_in = rows_ref[0, 0]
    gate_ref[0] = dot(rows_in, acts_ref[:, hidden : 2 * hidden], ((0,), (0,))).astype(BF16)
    up_ref[0] = dot(rows_in, acts_ref[:, 2 * hidden :], ((0,), (0,))).astype(BF16)
    down_ref[0] = dot(acts_ref[:, :hidden], rows_ref[1, 0], ((0,), (0,))).astype(BF16)


def ordered_weight_grads(rows, acts):
    total, width = rows.shape[2:]
    part = 2 * width
    hidden = acts.shape[1] // 3
    cols = block_of(width, 640)
    steps = width // cols
    return pl.pallas_call(
        ordered_weights_kernel,
        grid=(2, steps),
        in_specs=[
            pl.BlockSpec((2, 1, total, cols), lambda k, b: (0, k, 0, b)),
            pl.BlockSpec((total, 3 * hidden), lambda k, b: (0, 0)),
        ],
        out_specs=[
            pl.BlockSpec((1, cols, hidden), lambda k, b: (0, k * steps + b, 0)),
            pl.BlockSpec((1, cols, hidden), lambda k, b: (0, k * steps + b, 0)),
            pl.BlockSpec((1, hidden, cols), lambda k, b: (0, 0, k * steps + b)),
        ],
        out_shape=[
            jax.ShapeDtypeStruct((1, part, hidden), BF16),
            jax.ShapeDtypeStruct((1, part, hidden), BF16),
            jax.ShapeDtypeStruct((1, hidden, part), BF16),
        ],
        compiler_params=params(24),
        cost_estimate=pl.CostEstimate(
            flops=2 * total * part * 3 * hidden, bytes_accessed=6 * part * hidden, transcendentals=0
        ),
        name="weight_grads",
    )(rows, acts)


def take_kernel(slots, picks_ref, gates_ref, cot_ref, *refs):
    experts = picks_ref.shape[1]
    messages = refs[: 2 * experts]
    mixed_ref, grad_ref, gate_grad_ref, held_ref, sems = refs[2 * experts :]
    count, width = cot_ref.shape
    part = width // 2
    cols = part // 2
    rows = experts * 4 * slots
    own_half = lax.axis_index("dp")
    own = lax.axis_index("expert")
    chosen = spread_row(picks_ref[...].astype(F32), own, slots).astype(jnp.int32)
    scale = spread_row(gates_ref[...], own, slots)
    place = iota((1, rows), 1) % (4 * slots)
    late = place % (2 * slots) >= slots
    hit = chosen == iota((count, rows), 0)
    copies = []
    products = None
    for far in range(2):
        stacked = jnp.concatenate([messages[far * experts + near][...] for near in range(experts)], axis=0)
        half = jnp.bitwise_xor(own_half, far)
        for block in range(2):
            inside = hit & (place // (2 * slots) == block)
            span = far_columns(half, part, block, cols)
            rest = jnp.where(inside & ~late, scale, 0.0)
            mixed = None
            for _ in range(3):
                piece = rest.astype(BF16)
                rest = rest - piece.astype(F32)
                term = dot(piece, stacked)
                mixed = term if mixed is None else mixed + term
            held_ref[0, far, block] = mixed.astype(BF16)
            held_ref[1, far, block] = dot(jnp.where(inside & late, 1.0, 0.0).astype(BF16), stacked).astype(BF16)
            for kind, target in enumerate((mixed_ref, grad_ref)):
                copy = pltpu.make_async_copy(held_ref.at[kind, far, block], target.at[:, span], sems.at[kind, far, block])
                copy.start()
                copies.append(copy)
            product = dot(cot_ref[:, span], stacked, ((1,), (1,)))
            product = jnp.where(inside & ~late, product, 0.0)
            products = product if products is None else products + product
    values = jnp.sum(products, axis=0, keepdims=True)
    mine = iota((slots, rows), 1) % slots == iota((slots, rows), 0)
    owner = (xor_ids(own, (rows, experts), 0, 4 * slots) == iota((rows, experts), 1)).astype(F32)
    gate_grad_ref[...] = exact_dot(jnp.where(mine, values, 0.0), owner)
    for copy in copies:
        copy.wait()


def take_rows(messages, cotangent, picks, gates):
    slots, experts = picks.shape
    count, width = cotangent.shape
    return pl.pallas_call(
        functools.partial(take_kernel, slots),
        in_specs=[vmem()] * (3 + 2 * experts),
        out_specs=[hbm(), hbm(), vmem()],
        out_shape=[
            jax.ShapeDtypeStruct((count, width), BF16),
            jax.ShapeDtypeStruct((count, width), BF16),
            jax.ShapeDtypeStruct((slots, experts), F32),
        ],
        scratch_shapes=[pltpu.VMEM((2, 2, 2, count, width // 4), BF16), pltpu.SemaphoreType.DMA((2, 2, 2))],
        compiler_params=params(24),
        name="take_rows",
    )(picks, gates, cotangent, *messages)


EVERYONE = ("dp", "expert")


def exchange(messages):
    total = len(messages)
    result = list(messages)
    for mask in sorted(range(1, total), key=lambda m: (-(m % (total // 2)), -m)):
        result[mask] = lax.ppermute(messages[mask], EVERYONE, [(i, i ^ mask) for i in range(total)])
    return result


def xor_body(tokens, cotangent, picks, gates, w_gate, w_up, w_down):
    experts, slots = picks.shape[1:]
    picks_t = picks[0].T
    gates_t = gates[0].T
    arrived = exchange(send_rows(tokens, cotangent, picks_t, gates_t))
    own, rows = column_sums(arrived, w_gate, w_up, w_down, slots)
    other = lax.ppermute(own, EVERYONE, [(i, i ^ experts) for i in range(2 * experts)])
    acts, *replies = reply_rows(own, other, w_gate, w_up, w_down, slots)
    back = exchange(replies)
    grad_gate_w, grad_up_w, grad_down = ordered_weight_grads(rows, acts)
    mixed, token_grad, gate_grad = take_rows(back, cotangent, picks_t, gates_t)
    return mixed, token_grad, gate_grad.T[None], grad_gate_w, grad_up_w, grad_down


def pick_body(n_dp, tokens, cotangent, picks, *rest):
    experts, slots = picks.shape[1:]
    fits = n_dp == 2 and experts & (experts - 1) == 0 and experts <= 16
    fits = fits and 4 * slots == 16 and tokens.shape[1] % 512 == 0
    if fits:
        return xor_body(tokens, cotangent, picks, *rest)
    return body(n_dp, tokens, cotangent, picks, *rest)


def solution(mesh):
    rows = P(("dp", "expert"), None)
    lists = P(("dp", "expert"), None, None)
    tall = P("expert", "dp", None)
    wide = P("expert", None, "dp")
    return jax.shard_map(
        functools.partial(pick_body, mesh.shape["dp"]),
        mesh=mesh,
        in_specs=(rows, rows, lists, lists, tall, tall, wide),
        out_specs=(rows, rows, lists, tall, tall, wide),
        check_vma=False,
    )
```

```python
import functools

import jax
import jax.numpy as jnp
from jax import lax
from jax.experimental import pallas as pl
from jax.experimental.pallas import tpu as pltpu
from jax.sharding import PartitionSpec as P

F32 = jnp.float32
BF16 = jnp.bfloat16
MIB = 1024 * 1024
EVERYONE = ("dp", "expert")


def dot(left, right, dims=((1,), (0,)), precision=None):
    return lax.dot_general(left, right, (dims, ((), ())), precision=precision, preferred_element_type=F32)


def exact_dot(left, right, dims=((1,), (0,))):
    return dot(left, right, dims, lax.Precision.HIGHEST)


def iota(shape, axis):
    return lax.broadcasted_iota(jnp.int32, shape, axis)


def one_hot(condition):
    return jnp.where(condition, 1.0, 0.0).astype(BF16)


def vmem():
    return pl.BlockSpec(memory_space=pltpu.VMEM)


def hbm():
    return pl.BlockSpec(memory_space=pltpu.HBM)


def in_hbm(value):
    return pltpu.with_memory_space_constraint(value, pltpu.HBM)


def shape_of(*sizes, dtype=BF16):
    return jax.ShapeDtypeStruct(sizes, dtype)


def params(mib=24):
    return pltpu.CompilerParams(vmem_limit_bytes=mib * MIB)


def cost(flops, moved):
    return pl.CostEstimate(flops=flops, bytes_accessed=moved, transcendentals=0)


def block_of(width, limit):
    best = 128
    for size in range(128, limit + 1, 128):
        if width % size == 0:
            best = size
    return best


def spread_column(values, blocks):
    slots, experts = values.shape
    rows = experts * blocks * slots
    owner = (iota((rows, experts), 0) // (blocks * slots) == iota((rows, experts), 1)).astype(F32)
    wide = exact_dot(owner, values, ((1,), (1,)))
    mine = iota((rows, slots), 0) % slots == iota((rows, slots), 1)
    return jnp.sum(jnp.where(mine, wide, 0.0), axis=1, keepdims=True)


def spread_row(values, blocks):
    slots, experts = values.shape
    rows = experts * blocks * slots
    owner = (iota((experts, rows), 1) // (blocks * slots) == iota((experts, rows), 0)).astype(F32)
    wide = exact_dot(values, owner)
    mine = iota((slots, rows), 1) % slots == iota((slots, rows), 0)
    return jnp.sum(jnp.where(mine, wide, 0.0), axis=0, keepdims=True)


def send_kernel(halves, blocks, scaled, *refs):
    count = 2 if scaled else 1
    lists, source_ref, out_ref = refs[:count], refs[count], refs[count + 1]
    held_ref, sems, list_sems = refs[count + 2 : count + 5]
    list_refs = refs[count + 5 :]
    rows, cols = out_ref.shape
    rows = rows // halves
    tokens = source_ref.shape[0]
    list_copies = [
        pltpu.make_async_copy(ref, target, list_sems.at[i]) for i, (ref, target) in enumerate(zip(lists, list_refs))
    ]
    copies = []
    for copy in list_copies:
        copy.start()
    for half in range(halves):
        for block in range(blocks):
            place = half * blocks + block
            copies.append(
                pltpu.make_async_copy(
                    source_ref.at[:, place * cols : (place + 1) * cols],
                    held_ref.at[half, block * tokens : (block + 1) * tokens],
                    sems.at[half, block],
                )
            )
            copies[-1].start()
    for copy in list_copies:
        copy.wait()
    slots = list_refs[0].shape[0]
    chosen = spread_column(list_refs[0][...].astype(F32), blocks).astype(jnp.int32)
    target = chosen + iota((rows, 1), 0) % (blocks * slots) // slots * tokens
    take = one_hot(target == iota((rows, blocks * tokens), 1))
    scale = spread_column(list_refs[1][...], blocks) if scaled else None
    for half in range(halves):
        for block in range(blocks):
            copies[half * blocks + block].wait()
        picked = dot(take, held_ref[half])
        if scaled:
            picked = picked * scale
        out_ref[half * rows : (half + 1) * rows] = picked.astype(BF16)


def send_rows(source, lists, halves, blocks):
    slots, experts = lists[0].shape
    tokens, width = source.shape
    cols = width // (halves * blocks)
    rows = halves * experts * blocks * slots
    return pl.pallas_call(
        functools.partial(send_kernel, halves, blocks, len(lists) == 2),
        in_specs=[hbm()] * (len(lists) + 1),
        out_specs=vmem(),
        out_shape=shape_of(rows, cols),
        scratch_shapes=[
            pltpu.VMEM((halves, blocks * tokens, cols), BF16),
            pltpu.SemaphoreType.DMA((halves, blocks)),
            pltpu.SemaphoreType.DMA((2,)),
        ]
        + [pltpu.VMEM((slots, experts), value.dtype) for value in lists],
        compiler_params=params(16),
        cost_estimate=cost(2 * rows * cols * tokens * blocks, 2 * tokens * width + 2 * rows * cols),
        name="send_rows",
    )(*[in_hbm(value) for value in lists], in_hbm(source))


def sort_matrix(rows, blocks, slots, back):
    a = iota((rows, rows), 1 if back else 0)
    b = iota((rows, rows), 0 if back else 1)
    group = rows // blocks
    return one_hot(a % group // slots * (blocks * slots) + a // group * slots + a % slots == b)


def sort_rows(messages_ref, rows_ref, slots):
    blocks, total = rows_ref.shape[:2]
    if blocks == 1:
        rows_ref[0] = messages_ref[...]
        return
    size = min(blocks * total, 256)
    group = size // blocks
    order = sort_matrix(size, blocks, slots, False)
    for part in range(total // group):
        ordered = dot(order, messages_ref[part * size : (part + 1) * size]).astype(BF16)
        for block in range(blocks):
            rows_ref[block, part * group : (part + 1) * group] = ordered[block * group : (block + 1) * group]


def unsort_rows(made, out_ref, slots):
    blocks, total = len(made), made[0].shape[0]
    if blocks == 1:
        out_ref[...] = made[0]
        return
    size = min(blocks * total, 256)
    group = size // blocks
    order = sort_matrix(size, blocks, slots, True)
    for part in range(total // group):
        stacked = jnp.concatenate([value[part * group : (part + 1) * group] for value in made], axis=0)
        out_ref[part * size : (part + 1) * size] = dot(order, stacked).astype(BF16)


def spans(ref, blocks):
    cols = ref // blocks
    return [slice(block * cols, (block + 1) * cols) for block in range(blocks)]


def added(terms):
    return functools.reduce(jnp.add, terms)


def in_sums_kernel(slots, messages_ref, gate_ref, up_ref, out_ref, rows_ref):
    blocks = rows_ref.shape[0]
    part, hidden = gate_ref.shape[1:]
    sort_rows(messages_ref, rows_ref, slots)
    for place, ref in enumerate((gate_ref, up_ref)):
        total = added([dot(rows_ref[b], ref[0, span, :]) for b, span in enumerate(spans(part, blocks))])
        out_ref[:, place * hidden : (place + 1) * hidden] = total.astype(BF16)


def in_sums(messages, w_gate, w_up, blocks, slots):
    part, hidden = w_gate.shape[1:]
    rows = messages.shape[0] // blocks
    return pl.pallas_call(
        functools.partial(in_sums_kernel, slots),
        in_specs=[vmem()] * 3,
        out_specs=[vmem()] * 2,
        out_shape=[shape_of(rows, 2 * hidden), shape_of(blocks, rows, part // blocks)],
        compiler_params=params(),
        cost_estimate=cost(4 * rows * part * hidden, 4 * part * hidden),
        name="gate_up_sums",
    )(messages, w_gate, w_up)


def up_sums_kernel(slots, messages_ref, down_ref, out_ref, rows_ref):
    blocks = rows_ref.shape[0]
    part = down_ref.shape[2]
    sort_rows(messages_ref, rows_ref, slots)
    total = added(
        [dot(rows_ref[b], down_ref[0, :, span], ((1,), (1,))) for b, span in enumerate(spans(part, blocks))]
    )
    out_ref[...] = total.astype(BF16)


def up_sums(messages, w_down, blocks, slots):
    hidden, part = w_down.shape[1:]
    rows = messages.shape[0] // blocks
    return pl.pallas_call(
        functools.partial(up_sums_kernel, slots),
        in_specs=[vmem()] * 2,
        out_specs=[vmem()] * 2,
        out_shape=[shape_of(rows, hidden), shape_of(blocks, rows, part // blocks)],
        compiler_params=params(),
        cost_estimate=cost(2 * rows * part * hidden, 2 * part * hidden),
        name="back_sums",
    )(messages, w_down)


def row_parts(total):
    size = min(total, 128)
    return [slice(start, start + size) for start in range(0, total, size)]


def summed(refs, rows, span):
    return added([ref[rows, span].astype(F32) for ref in refs])


def out_rows_kernel(slots, blocks, count, *refs):
    shares, (down_ref, act_ref, out_ref) = refs[:count], refs[count:]
    hidden, part = down_ref.shape[1:]
    for rows in row_parts(act_ref.shape[0]):
        gate_sum = summed(shares, rows, slice(0, hidden))
        up_sum = summed(shares, rows, slice(hidden, 2 * hidden))
        act_ref[rows] = (gate_sum * jax.nn.sigmoid(gate_sum) * up_sum).astype(BF16)
    unsort_rows([dot(act_ref[...], down_ref[0, :, span]).astype(BF16) for span in spans(part, blocks)], out_ref, slots)


def out_rows(shares, w_down, blocks, slots):
    hidden, part = w_down.shape[1:]
    rows = shares[0].shape[0]
    return pl.pallas_call(
        functools.partial(out_rows_kernel, slots, blocks, len(shares)),
        in_specs=[vmem()] * (len(shares) + 1),
        out_specs=[vmem()] * 2,
        out_shape=[shape_of(rows, hidden), shape_of(blocks * rows, part // blocks)],
        compiler_params=params(),
        cost_estimate=cost(2 * rows * part * hidden, 2 * part * hidden),
        name="output_rows",
    )(*shares, w_down)


def grad_rows_kernel(slots, blocks, count, *refs):
    shares, backs = refs[:count], refs[count : 2 * count]
    gate_ref, up_ref, act_ref, out_ref = refs[2 * count :]
    part, hidden = gate_ref.shape[1:]
    for rows in row_parts(act_ref.shape[0]):
        gate_sum = summed(shares, rows, slice(0, hidden))
        up_sum = summed(shares, rows, slice(hidden, 2 * hidden))
        back_sum = summed(backs, rows, slice(0, hidden))
        sig = jax.nn.sigmoid(gate_sum)
        act_ref[rows, :hidden] = (back_sum * up_sum * sig * (1.0 + gate_sum * (1.0 - sig))).astype(BF16)
        act_ref[rows, hidden:] = (back_sum * (gate_sum * sig)).astype(BF16)
    made = []
    for span in spans(part, blocks):
        total = dot(act_ref[:, :hidden], gate_ref[0, span, :], ((1,), (1,)))
        total = total + dot(act_ref[:, hidden:], up_ref[0, span, :], ((1,), (1,)))
        made.append(total.astype(BF16))
    unsort_rows(made, out_ref, slots)


def grad_rows(shares, backs, w_gate, w_up, blocks, slots):
    part, hidden = w_gate.shape[1:]
    rows = shares[0].shape[0]
    return pl.pallas_call(
        functools.partial(grad_rows_kernel, slots, blocks, len(shares)),
        in_specs=[vmem()] * (2 * len(shares) + 2),
        out_specs=[vmem()] * 2,
        out_shape=[shape_of(rows, 2 * hidden), shape_of(blocks * rows, part // blocks)],
        compiler_params=params(32),
        cost_estimate=cost(4 * rows * part * hidden, 4 * part * hidden),
        name="gradient_rows",
    )(*shares, *backs, w_gate, w_up)


def weights_kernel(rows_in_ref, rows_up_ref, act_ref, grad_act_ref, gate_ref, up_ref, down_ref):
    hidden = gate_ref.shape[2]
    rows_in = rows_in_ref[0]
    gate_ref[0] = dot(rows_in, grad_act_ref[:, :hidden], ((0,), (0,))).astype(BF16)
    up_ref[0] = dot(rows_in, grad_act_ref[:, hidden:], ((0,), (0,))).astype(BF16)
    down_ref[0] = dot(act_ref[...], rows_up_ref[0], ((0,), (0,))).astype(BF16)


def weight_grads(rows_in, rows_up, act, grad_act):
    blocks, total, width = rows_in.shape
    part = blocks * width
    hidden = act.shape[1]
    cols = block_of(width, 640)
    steps = width // cols
    chunk = pl.BlockSpec((1, total, cols), lambda k, b: (k, 0, b))
    tall = pl.BlockSpec((1, cols, hidden), lambda k, b: (0, k * steps + b, 0))
    return pl.pallas_call(
        weights_kernel,
        grid=(blocks, steps),
        in_specs=[
            chunk,
            chunk,
            pl.BlockSpec((total, hidden), lambda k, b: (0, 0)),
            pl.BlockSpec((total, 2 * hidden), lambda k, b: (0, 0)),
        ],
        out_specs=[tall, tall, pl.BlockSpec((1, hidden, cols), lambda k, b: (0, 0, k * steps + b))],
        out_shape=[shape_of(1, part, hidden), shape_of(1, part, hidden), shape_of(1, hidden, part)],
        compiler_params=params(),
        cost_estimate=cost(6 * total * part * hidden, 6 * part * hidden),
        name="weight_grads",
    )(rows_in, rows_up, act, grad_act)


def put_columns(held_ref, target_ref, sems, half, block):
    blocks, _, cols = held_ref.shape[1:]
    place = half * blocks + block
    copy = pltpu.make_async_copy(
        held_ref.at[half, block], target_ref.at[:, place * cols : (place + 1) * cols], sems.at[half, block]
    )
    copy.start()
    return copy


def mixed_kernel(picks_ref, gates_ref, cot_ref, back_ref, mixed_ref, gate_grad_ref, put_ref, held_ref, sems):
    slots, experts = picks_ref.shape
    halves, blocks, tokens, cols = held_ref.shape
    rows = experts * blocks * slots
    hit = spread_row(picks_ref[...].astype(F32), blocks).astype(jnp.int32) == iota((tokens, rows), 0)
    scale = spread_row(gates_ref[...], blocks)
    of_block = iota((tokens, rows), 1) % (blocks * slots) // slots
    copies = []
    products = None
    for block in range(blocks):
        inside = hit & (of_block == block)
        put_ref[block] = one_hot(inside)
        rest = jnp.where(inside, scale, 0.0)
        pieces = []
        for _ in range(3):
            pieces.append(rest.astype(BF16))
            rest = rest - pieces[-1].astype(F32)
        for half in range(halves):
            back = back_ref[half * rows : (half + 1) * rows]
            held_ref[half, block] = added([dot(piece, back) for piece in pieces]).astype(BF16)
            copies.append(put_columns(held_ref, mixed_ref, sems, half, block))
            place = half * blocks + block
            product = dot(cot_ref[:, place * cols : (place + 1) * cols], back, ((1,), (1,)))
            product = jnp.where(inside, product, 0.0)
            products = product if products is None else products + product
    values = jnp.sum(products, axis=0, keepdims=True)
    mine = iota((slots, rows), 1) % slots == iota((slots, rows), 0)
    owner = (iota((rows, experts), 0) // (blocks * slots) == iota((rows, experts), 1)).astype(F32)
    gate_grad_ref[...] = exact_dot(jnp.where(mine, values, 0.0), owner)
    for copy in copies:
        copy.wait()


def mix_rows(back, cotangent, picks, gates, halves, blocks):
    slots, experts = picks.shape
    tokens, width = cotangent.shape
    cols = width // (halves * blocks)
    rows = experts * blocks * slots
    return pl.pallas_call(
        mixed_kernel,
        in_specs=[vmem()] * 4,
        out_specs=[hbm(), vmem(), vmem()],
        out_shape=[shape_of(tokens, width), shape_of(slots, experts, dtype=F32), shape_of(blocks, tokens, rows)],
        scratch_shapes=[pltpu.VMEM((halves, blocks, tokens, cols), BF16), pltpu.SemaphoreType.DMA((halves, blocks))],
        compiler_params=params(16),
        cost_estimate=cost(8 * rows * tokens * width, 4 * tokens * width),
        name="mixed_rows",
    )(picks, gates, cotangent, back)


def token_grad_kernel(put_ref, back_ref, grad_ref, held_ref, sems):
    halves, blocks = held_ref.shape[:2]
    rows = back_ref.shape[0] // halves
    copies = []
    for half in range(halves):
        for block in range(blocks):
            back = back_ref[half * rows : (half + 1) * rows]
            held_ref[half, block] = dot(put_ref[block], back).astype(BF16)
            copies.append(put_columns(held_ref, grad_ref, sems, half, block))
    for copy in copies:
        copy.wait()


def token_grads(back, put, halves):
    blocks, tokens, rows = put.shape
    cols = back.shape[1]
    width = halves * blocks * cols
    return pl.pallas_call(
        token_grad_kernel,
        in_specs=[vmem()] * 2,
        out_specs=hbm(),
        out_shape=shape_of(tokens, width),
        scratch_shapes=[pltpu.VMEM((halves, blocks, tokens, cols), BF16), pltpu.SemaphoreType.DMA((halves, blocks))],
        compiler_params=params(16),
        cost_estimate=cost(2 * rows * tokens * width, 2 * tokens * width),
        name="token_grads",
    )(put, back)


def scatter(messages):
    return lax.all_to_all(messages, EVERYONE, split_axis=0, concat_axis=0, tiled=True)


def dp_shares(own, halves):
    shares = [own] + [
        lax.ppermute(own, "dp", [(i, (i + shift) % halves) for i in range(halves)]) for shift in range(1, halves)
    ]
    return shares if halves <= 2 else [added([share.astype(F32) for share in shares])]


def body(halves, tokens, cotangent, picks, gates, w_gate, w_up, w_down):
    slots = picks.shape[2]
    blocks = 2 if tokens.shape[1] // halves % 256 == 0 else 1
    picks_t = picks[0].T
    gates_t = gates[0].T
    arrived_in = scatter(send_rows(tokens, (picks_t,), halves, blocks))
    arrived_up = scatter(send_rows(cotangent, (picks_t, gates_t), halves, blocks))
    own_sums, rows_in = in_sums(arrived_in, w_gate, w_up, blocks, slots)
    shares = dp_shares(own_sums, halves)
    act, outputs = out_rows(shares, w_down, blocks, slots)
    back_out = scatter(outputs)
    own_back, rows_up = up_sums(arrived_up, w_down, blocks, slots)
    backs = dp_shares(own_back, halves)
    grad_act, gradients = grad_rows(shares, backs, w_gate, w_up, blocks, slots)
    back_grad = scatter(gradients)
    grad_gate_w, grad_up_w, grad_down = weight_grads(rows_in, rows_up, act, grad_act)
    mixed, gate_grad, put = mix_rows(back_out, cotangent, picks_t, gates_t, halves, blocks)
    token_grad = token_grads(back_grad, put, halves)
    return mixed, token_grad, gate_grad.T[None], grad_gate_w, grad_up_w, grad_down


def solution(mesh):
    rows = P(("dp", "expert"), None)
    lists = P(("dp", "expert"), None, None)
    tall = P("expert", "dp", None)
    wide = P("expert", None, "dp")
    return jax.shard_map(
        functools.partial(body, mesh.shape["dp"]),
        mesh=mesh,
        in_specs=(rows, rows, lists, lists, tall, tall, wide),
        out_specs=(rows, rows, lists, tall, tall, wide),
        check_vma=False,
    )
```

```python
import functools

import jax
import jax.numpy as jnp
from jax import lax
from jax.experimental import pallas as pl
from jax.experimental.pallas import tpu as pltpu
from jax.sharding import PartitionSpec as P

F32 = jnp.float32
BF16 = jnp.bfloat16
MIB = 1024 * 1024
EVERYONE = ("dp", "expert")


def dot(left, right, dims=((1,), (0,)), precision=None):
    return lax.dot_general(left, right, (dims, ((), ())), precision=precision, preferred_element_type=F32)


def exact_dot(left, right, dims=((1,), (0,))):
    return dot(left, right, dims, lax.Precision.HIGHEST)


def iota(shape, axis):
    return lax.broadcasted_iota(jnp.int32, shape, axis)


def one_hot(condition):
    return jnp.where(condition, 1.0, 0.0).astype(BF16)


def vmem():
    return pl.BlockSpec(memory_space=pltpu.VMEM)


def hbm():
    return pl.BlockSpec(memory_space=pltpu.HBM)


def in_hbm(value):
    return pltpu.with_memory_space_constraint(value, pltpu.HBM)


def shape_of(*sizes, dtype=BF16):
    return jax.ShapeDtypeStruct(sizes, dtype)


def params(mib=24):
    return pltpu.CompilerParams(vmem_limit_bytes=mib * MIB)


def cost(flops, moved):
    return pl.CostEstimate(flops=flops, bytes_accessed=moved, transcendentals=0)


def block_of(width, limit):
    best = 128
    for size in range(128, limit + 1, 128):
        if width % size == 0:
            best = size
    return best


def spread_column(values, blocks):
    slots, experts = values.shape
    rows = experts * blocks * slots
    owner = (iota((rows, experts), 0) // (blocks * slots) == iota((rows, experts), 1)).astype(F32)
    wide = exact_dot(owner, values, ((1,), (1,)))
    mine = iota((rows, slots), 0) % slots == iota((rows, slots), 1)
    return jnp.sum(jnp.where(mine, wide, 0.0), axis=1, keepdims=True)


def spread_row(values, blocks):
    slots, experts = values.shape
    rows = experts * blocks * slots
    owner = (iota((experts, rows), 1) // (blocks * slots) == iota((experts, rows), 0)).astype(F32)
    wide = exact_dot(values, owner)
    mine = iota((slots, rows), 1) % slots == iota((slots, rows), 0)
    return jnp.sum(jnp.where(mine, wide, 0.0), axis=0, keepdims=True)


def send_kernel(halves, blocks, scaled, extra, *refs):
    count = 2 if scaled else 1
    lists, source_ref, refs = refs[:count], refs[count], refs[count + 1 :]
    kept, out_ref, refs = refs[:extra], refs[extra], refs[extra + 1 :]
    kept_refs, refs = refs[:extra], refs[extra:]
    held_ref, sems, list_sems, kept_sems = refs[:4]
    list_refs = refs[4:]
    rows, cols = out_ref.shape
    rows = rows // halves
    tokens = source_ref.shape[0]
    list_copies = [
        pltpu.make_async_copy(ref, target, list_sems.at[i]) for i, (ref, target) in enumerate(zip(lists, list_refs))
    ]
    copies = []
    for copy in list_copies:
        copy.start()
    for half in range(halves):
        for block in range(blocks):
            place = half * blocks + block
            copies.append(
                pltpu.make_async_copy(
                    source_ref.at[:, place * cols : (place + 1) * cols],
                    held_ref.at[half, block * tokens : (block + 1) * tokens],
                    sems.at[half, block],
                )
            )
            copies[-1].start()
    kept_copies = [
        pltpu.make_async_copy(ref, target, kept_sems.at[i]) for i, (ref, target) in enumerate(zip(kept, kept_refs))
    ]
    for copy in kept_copies:
        copy.start()
    for copy in list_copies:
        copy.wait()
    slots = list_refs[0].shape[0]
    chosen = spread_column(list_refs[0][...].astype(F32), blocks).astype(jnp.int32)
    target = chosen + iota((rows, 1), 0) % (blocks * slots) // slots * tokens
    take = one_hot(target == iota((rows, blocks * tokens), 1))
    scale = spread_column(list_refs[1][...], blocks) if scaled else None
    for half in range(halves):
        for block in range(blocks):
            copies[half * blocks + block].wait()
        picked = dot(take, held_ref[half])
        if scaled:
            picked = picked * scale
        out_ref[half * rows : (half + 1) * rows] = picked.astype(BF16)
    for copy in kept_copies:
        copy.wait()


def send_rows(source, lists, halves, blocks, kept=()):
    slots, experts = lists[0].shape
    tokens, width = source.shape
    cols = width // (halves * blocks)
    rows = halves * experts * blocks * slots
    return pl.pallas_call(
        functools.partial(send_kernel, halves, blocks, len(lists) == 2, len(kept)),
        in_specs=[hbm()] * (len(lists) + 1 + len(kept)),
        out_specs=[vmem()] * (1 + len(kept)),
        out_shape=[shape_of(rows, cols)] + [shape_of(*value.shape) for value in kept],
        scratch_shapes=[
            pltpu.VMEM((halves, blocks * tokens, cols), BF16),
            pltpu.SemaphoreType.DMA((halves, blocks)),
            pltpu.SemaphoreType.DMA((2,)),
            pltpu.SemaphoreType.DMA((3,)),
        ]
        + [pltpu.VMEM((slots, experts), value.dtype) for value in lists],
        compiler_params=params(20),
        cost_estimate=cost(2 * rows * cols * tokens * blocks, 2 * tokens * width + 2 * sum(v.size for v in kept)),
        name="send_rows",
    )(*[in_hbm(value) for value in lists], in_hbm(source), *[in_hbm(value) for value in kept])


def sort_matrix(rows, blocks, slots, back):
    a = iota((rows, rows), 1 if back else 0)
    b = iota((rows, rows), 0 if back else 1)
    group = rows // blocks
    return one_hot(a % group // slots * (blocks * slots) + a // group * slots + a % slots == b)


def sort_rows(messages_ref, rows_ref, slots):
    blocks, total = rows_ref.shape[:2]
    if blocks == 1:
        rows_ref[0] = messages_ref[...]
        return
    size = min(blocks * total, 256)
    group = size // blocks
    order = sort_matrix(size, blocks, slots, False)
    for part in range(total // group):
        ordered = dot(order, messages_ref[part * size : (part + 1) * size]).astype(BF16)
        for block in range(blocks):
            rows_ref[block, part * group : (part + 1) * group] = ordered[block * group : (block + 1) * group]


def unsort_rows(made, out_ref, slots):
    blocks, total = len(made), made[0].shape[0]
    if blocks == 1:
        out_ref[...] = made[0]
        return
    size = min(blocks * total, 256)
    group = size // blocks
    order = sort_matrix(size, blocks, slots, True)
    for part in range(total // group):
        stacked = jnp.concatenate([value[part * group : (part + 1) * group] for value in made], axis=0)
        out_ref[part * size : (part + 1) * size] = dot(order, stacked).astype(BF16)


def spans(ref, blocks):
    cols = ref // blocks
    return [slice(block * cols, (block + 1) * cols) for block in range(blocks)]


def added(terms):
    return functools.reduce(jnp.add, terms)


def in_sums_kernel(slots, messages_ref, gate_ref, up_ref, out_ref, rows_ref):
    blocks = rows_ref.shape[0]
    part, hidden = gate_ref.shape[1:]
    sort_rows(messages_ref, rows_ref, slots)
    for place, ref in enumerate((gate_ref, up_ref)):
        total = added([dot(rows_ref[b], ref[0, span, :]) for b, span in enumerate(spans(part, blocks))])
        out_ref[:, place * hidden : (place + 1) * hidden] = total.astype(BF16)


def in_sums(messages, w_gate, w_up, blocks, slots):
    part, hidden = w_gate.shape[1:]
    rows = messages.shape[0] // blocks
    return pl.pallas_call(
        functools.partial(in_sums_kernel, slots),
        in_specs=[vmem()] * 3,
        out_specs=[vmem()] * 2,
        out_shape=[shape_of(rows, 2 * hidden), shape_of(blocks, rows, part // blocks)],
        compiler_params=params(),
        cost_estimate=cost(4 * rows * part * hidden, 4 * part * hidden),
        name="gate_up_sums",
    )(messages, w_gate, w_up)


def up_sums_kernel(slots, messages_ref, down_ref, out_ref, rows_ref):
    blocks = rows_ref.shape[0]
    part = down_ref.shape[2]
    sort_rows(messages_ref, rows_ref, slots)
    total = added(
        [dot(rows_ref[b], down_ref[0, :, span], ((1,), (1,))) for b, span in enumerate(spans(part, blocks))]
    )
    out_ref[...] = total.astype(BF16)


def up_sums(messages, w_down, blocks, slots):
    hidden, part = w_down.shape[1:]
    rows = messages.shape[0] // blocks
    return pl.pallas_call(
        functools.partial(up_sums_kernel, slots),
        in_specs=[vmem()] * 2,
        out_specs=[vmem()] * 2,
        out_shape=[shape_of(rows, hidden), shape_of(blocks, rows, part // blocks)],
        compiler_params=params(),
        cost_estimate=cost(2 * rows * part * hidden, 2 * part * hidden),
        name="back_sums",
    )(messages, w_down)


def row_parts(total):
    size = min(total, 128)
    return [slice(start, start + size) for start in range(0, total, size)]


def summed(refs, rows, span):
    return added([ref[rows, span].astype(F32) for ref in refs])


def out_rows_kernel(slots, blocks, count, *refs):
    shares, (down_ref, act_ref, out_ref) = refs[:count], refs[count:]
    hidden, part = down_ref.shape[1:]
    for rows in row_parts(act_ref.shape[0]):
        gate_sum = summed(shares, rows, slice(0, hidden))
        up_sum = summed(shares, rows, slice(hidden, 2 * hidden))
        act_ref[rows] = (gate_sum * jax.nn.sigmoid(gate_sum) * up_sum).astype(BF16)
    unsort_rows([dot(act_ref[...], down_ref[0, :, span]).astype(BF16) for span in spans(part, blocks)], out_ref, slots)


def out_rows(shares, w_down, blocks, slots):
    hidden, part = w_down.shape[1:]
    rows = shares[0].shape[0]
    return pl.pallas_call(
        functools.partial(out_rows_kernel, slots, blocks, len(shares)),
        in_specs=[vmem()] * (len(shares) + 1),
        out_specs=[vmem()] * 2,
        out_shape=[shape_of(rows, hidden), shape_of(blocks * rows, part // blocks)],
        compiler_params=params(),
        cost_estimate=cost(2 * rows * part * hidden, 2 * part * hidden),
        name="output_rows",
    )(*shares, w_down)


def grad_rows_kernel(slots, blocks, count, *refs):
    shares, backs = refs[:count], refs[count : 2 * count]
    gate_ref, up_ref, act_ref, out_ref = refs[2 * count :]
    part, hidden = gate_ref.shape[1:]
    for rows in row_parts(act_ref.shape[0]):
        gate_sum = summed(shares, rows, slice(0, hidden))
        up_sum = summed(shares, rows, slice(hidden, 2 * hidden))
        back_sum = summed(backs, rows, slice(0, hidden))
        sig = jax.nn.sigmoid(gate_sum)
        act_ref[rows, :hidden] = (back_sum * up_sum * sig * (1.0 + gate_sum * (1.0 - sig))).astype(BF16)
        act_ref[rows, hidden:] = (back_sum * (gate_sum * sig)).astype(BF16)
    made = []
    for span in spans(part, blocks):
        total = dot(act_ref[:, :hidden], gate_ref[0, span, :], ((1,), (1,)))
        total = total + dot(act_ref[:, hidden:], up_ref[0, span, :], ((1,), (1,)))
        made.append(total.astype(BF16))
    unsort_rows(made, out_ref, slots)


def grad_rows(shares, backs, w_gate, w_up, blocks, slots):
    part, hidden = w_gate.shape[1:]
    rows = shares[0].shape[0]
    return pl.pallas_call(
        functools.partial(grad_rows_kernel, slots, blocks, len(shares)),
        in_specs=[vmem()] * (2 * len(shares) + 2),
        out_specs=[vmem()] * 2,
        out_shape=[shape_of(rows, 2 * hidden), shape_of(blocks * rows, part // blocks)],
        compiler_params=params(32),
        cost_estimate=cost(4 * rows * part * hidden, 4 * part * hidden),
        name="gradient_rows",
    )(*shares, *backs, w_gate, w_up)


def weights_kernel(rows_in_ref, rows_up_ref, act_ref, grad_act_ref, gate_ref, up_ref, down_ref):
    hidden = gate_ref.shape[2]
    rows_in = rows_in_ref[0]
    gate_ref[0] = dot(rows_in, grad_act_ref[:, :hidden], ((0,), (0,))).astype(BF16)
    up_ref[0] = dot(rows_in, grad_act_ref[:, hidden:], ((0,), (0,))).astype(BF16)
    down_ref[0] = dot(act_ref[...], rows_up_ref[0], ((0,), (0,))).astype(BF16)


def weight_grads(rows_in, rows_up, act, grad_act):
    blocks, total, width = rows_in.shape
    part = blocks * width
    hidden = act.shape[1]
    cols = block_of(width, 640)
    steps = width // cols
    chunk = pl.BlockSpec((1, total, cols), lambda k, b: (k, 0, b))
    tall = pl.BlockSpec((1, cols, hidden), lambda k, b: (0, k * steps + b, 0))
    return pl.pallas_call(
        weights_kernel,
        grid=(blocks, steps),
        in_specs=[
            chunk,
            chunk,
            pl.BlockSpec((total, hidden), lambda k, b: (0, 0)),
            pl.BlockSpec((total, 2 * hidden), lambda k, b: (0, 0)),
        ],
        out_specs=[tall, tall, pl.BlockSpec((1, hidden, cols), lambda k, b: (0, 0, k * steps + b))],
        out_shape=[shape_of(1, part, hidden), shape_of(1, part, hidden), shape_of(1, hidden, part)],
        compiler_params=params(),
        cost_estimate=cost(6 * total * part * hidden, 6 * part * hidden),
        name="weight_grads",
    )(rows_in, rows_up, act, grad_act)


def put_columns(held_ref, target_ref, sems, half, block):
    blocks, _, cols = held_ref.shape[1:]
    place = half * blocks + block
    copy = pltpu.make_async_copy(
        held_ref.at[half, block], target_ref.at[:, place * cols : (place + 1) * cols], sems.at[half, block]
    )
    copy.start()
    return copy


def mixed_kernel(picks_ref, gates_ref, cot_ref, back_ref, mixed_ref, gate_grad_ref, put_ref, held_ref, sems):
    slots, experts = picks_ref.shape
    halves, blocks, tokens, cols = held_ref.shape
    rows = experts * blocks * slots
    hit = spread_row(picks_ref[...].astype(F32), blocks).astype(jnp.int32) == iota((tokens, rows), 0)
    scale = spread_row(gates_ref[...], blocks)
    of_block = iota((tokens, rows), 1) % (blocks * slots) // slots
    copies = []
    products = None
    for block in range(blocks):
        inside = hit & (of_block == block)
        put_ref[block] = one_hot(inside)
        rest = jnp.where(inside, scale, 0.0)
        pieces = []
        for _ in range(3):
            pieces.append(rest.astype(BF16))
            rest = rest - pieces[-1].astype(F32)
        for half in range(halves):
            back = back_ref[half * rows : (half + 1) * rows]
            held_ref[half, block] = added([dot(piece, back) for piece in pieces]).astype(BF16)
            copies.append(put_columns(held_ref, mixed_ref, sems, half, block))
            place = half * blocks + block
            product = dot(cot_ref[:, place * cols : (place + 1) * cols], back, ((1,), (1,)))
            product = jnp.where(inside, product, 0.0)
            products = product if products is None else products + product
    values = jnp.sum(products, axis=0, keepdims=True)
    mine = iota((slots, rows), 1) % slots == iota((slots, rows), 0)
    owner = (iota((rows, experts), 0) // (blocks * slots) == iota((rows, experts), 1)).astype(F32)
    gate_grad_ref[...] = exact_dot(jnp.where(mine, values, 0.0), owner)
    for copy in copies:
        copy.wait()


def mix_rows(back, cotangent, picks, gates, halves, blocks):
    slots, experts = picks.shape
    tokens, width = cotangent.shape
    cols = width // (halves * blocks)
    rows = experts * blocks * slots
    return pl.pallas_call(
        mixed_kernel,
        in_specs=[vmem()] * 4,
        out_specs=[hbm(), vmem(), vmem()],
        out_shape=[shape_of(tokens, width), shape_of(slots, experts, dtype=F32), shape_of(blocks, tokens, rows)],
        scratch_shapes=[pltpu.VMEM((halves, blocks, tokens, cols), BF16), pltpu.SemaphoreType.DMA((halves, blocks))],
        compiler_params=params(16),
        cost_estimate=cost(8 * rows * tokens * width, 4 * tokens * width),
        name="mixed_rows",
    )(picks, gates, cotangent, back)


def token_grad_kernel(put_ref, back_ref, grad_ref, held_ref, sems):
    halves, blocks = held_ref.shape[:2]
    rows = back_ref.shape[0] // halves
    copies = []
    for half in range(halves):
        for block in range(blocks):
            back = back_ref[half * rows : (half + 1) * rows]
            held_ref[half, block] = dot(put_ref[block], back).astype(BF16)
            copies.append(put_columns(held_ref, grad_ref, sems, half, block))
    for copy in copies:
        copy.wait()


def token_grads(back, put, halves):
    blocks, tokens, rows = put.shape
    cols = back.shape[1]
    width = halves * blocks * cols
    return pl.pallas_call(
        token_grad_kernel,
        in_specs=[vmem()] * 2,
        out_specs=hbm(),
        out_shape=shape_of(tokens, width),
        scratch_shapes=[pltpu.VMEM((halves, blocks, tokens, cols), BF16), pltpu.SemaphoreType.DMA((halves, blocks))],
        compiler_params=params(16),
        cost_estimate=cost(2 * rows * tokens * width, 2 * tokens * width),
        name="token_grads",
    )(put, back)


def scatter(messages):
    return lax.all_to_all(messages, EVERYONE, split_axis=0, concat_axis=0, tiled=True)


def dp_shares(own, halves):
    shares = [own] + [
        lax.ppermute(own, "dp", [(i, (i + shift) % halves) for i in range(halves)]) for shift in range(1, halves)
    ]
    return shares if halves <= 2 else [added([share.astype(F32) for share in shares])]


def body(halves, tokens, cotangent, picks, gates, w_gate, w_up, w_down):
    slots = picks.shape[2]
    blocks = 2 if tokens.shape[1] // halves % 256 == 0 else 1
    picks_t = picks[0].T
    gates_t = gates[0].T
    arrived_in = scatter(send_rows(tokens, (picks_t,), halves, blocks)[0])
    weights = (w_gate, w_up, w_down)
    messages_up, w_gate, w_up, w_down = send_rows(cotangent, (picks_t, gates_t), halves, blocks, weights)
    arrived_up = scatter(messages_up)
    own_sums, rows_in = in_sums(arrived_in, w_gate, w_up, blocks, slots)
    shares = dp_shares(own_sums, halves)
    act, outputs = out_rows(shares, w_down, blocks, slots)
    back_out = scatter(outputs)
    own_back, rows_up = up_sums(arrived_up, w_down, blocks, slots)
    backs = dp_shares(own_back, halves)
    grad_act, gradients = grad_rows(shares, backs, w_gate, w_up, blocks, slots)
    back_grad = scatter(gradients)
    grad_gate_w, grad_up_w, grad_down = weight_grads(rows_in, rows_up, act, grad_act)
    mixed, gate_grad, put = mix_rows(back_out, cotangent, picks_t, gates_t, halves, blocks)
    token_grad = token_grads(back_grad, put, halves)
    return mixed, token_grad, gate_grad.T[None], grad_gate_w, grad_up_w, grad_down


def solution(mesh):
    rows = P(("dp", "expert"), None)
    lists = P(("dp", "expert"), None, None)
    tall = P("expert", "dp", None)
    wide = P("expert", None, "dp")
    return jax.shard_map(
        functools.partial(body, mesh.shape["dp"]),
        mesh=mesh,
        in_specs=(rows, rows, lists, lists, tall, tall, wide),
        out_specs=(rows, rows, lists, tall, tall, wide),
        check_vma=False,
    )
```

```python
import functools

import jax
import jax.numpy as jnp
from jax import lax
from jax.experimental import pallas as pl
from jax.experimental.pallas import tpu as pltpu
from jax.sharding import PartitionSpec as P

F32 = jnp.float32
BF16 = jnp.bfloat16
MIB = 1024 * 1024
EVERYONE = ("dp", "expert")


def dot(left, right, dims=((1,), (0,)), precision=None):
    return lax.dot_general(left, right, (dims, ((), ())), precision=precision, preferred_element_type=F32)


def exact_dot(left, right, dims=((1,), (0,))):
    return dot(left, right, dims, lax.Precision.HIGHEST)


def iota(shape, axis):
    return lax.broadcasted_iota(jnp.int32, shape, axis)


def planes_of(experts):
    return experts // 4 if experts % 4 == 0 else 1


def expert_at(place, experts):
    planes = planes_of(experts)
    return place % planes * (experts // planes) + place // planes


def one_hot(condition):
    return jnp.where(condition, 1.0, 0.0).astype(BF16)


def vmem():
    return pl.BlockSpec(memory_space=pltpu.VMEM)


def hbm():
    return pl.BlockSpec(memory_space=pltpu.HBM)


def in_hbm(value):
    return pltpu.with_memory_space_constraint(value, pltpu.HBM)


def shape_of(*sizes, dtype=BF16):
    return jax.ShapeDtypeStruct(sizes, dtype)


def hbm_shape(*sizes):
    return pltpu.HBM(sizes, BF16)


def params(mib=24):
    return pltpu.CompilerParams(vmem_limit_bytes=mib * MIB)


def cost(flops, moved):
    return pl.CostEstimate(flops=flops, bytes_accessed=moved, transcendentals=0)


def block_of(width, limit):
    best = 128
    for size in range(128, limit + 1, 128):
        if width % size == 0:
            best = size
    return best


def spread_column(values, blocks):
    slots, experts = values.shape
    rows = experts * blocks * slots
    owner = (expert_at(iota((rows, experts), 0) // (blocks * slots), experts) == iota((rows, experts), 1)).astype(F32)
    wide = exact_dot(owner, values, ((1,), (1,)))
    mine = iota((rows, slots), 0) % slots == iota((rows, slots), 1)
    return jnp.sum(jnp.where(mine, wide, 0.0), axis=1, keepdims=True)


def spread_row(values, blocks):
    slots, experts = values.shape
    rows = experts * blocks * slots
    owner = (expert_at(iota((experts, rows), 1) // (blocks * slots), experts) == iota((experts, rows), 0)).astype(F32)
    wide = exact_dot(values, owner)
    mine = iota((slots, rows), 1) % slots == iota((slots, rows), 0)
    return jnp.sum(jnp.where(mine, wide, 0.0), axis=0, keepdims=True)


def send_kernel(halves, blocks, scaled, *refs):
    count = 2 if scaled else 1
    lists, source_ref, out_ref = refs[:count], refs[count], refs[count + 1]
    held_ref, sems, list_sems = refs[count + 2 : count + 5]
    list_refs = refs[count + 5 :]
    rows, cols = out_ref.shape
    rows = rows // halves
    tokens = source_ref.shape[0]
    list_copies = [
        pltpu.make_async_copy(ref, target, list_sems.at[i]) for i, (ref, target) in enumerate(zip(lists, list_refs))
    ]
    copies = []
    for copy in list_copies:
        copy.start()
    for half in range(halves):
        for block in range(blocks):
            place = half * blocks + block
            copies.append(
                pltpu.make_async_copy(
                    source_ref.at[:, place * cols : (place + 1) * cols],
                    held_ref.at[half, block * tokens : (block + 1) * tokens],
                    sems.at[half, block],
                )
            )
            copies[-1].start()
    for copy in list_copies:
        copy.wait()
    slots, experts = list_refs[0].shape
    run = planes_of(experts) * blocks * slots
    chosen = spread_column(list_refs[0][...].astype(F32), blocks).astype(jnp.int32)
    target = chosen + iota((rows, 1), 0) % (blocks * slots) // slots * tokens
    take = one_hot(target == iota((rows, blocks * tokens), 1))
    scale = spread_column(list_refs[1][...], blocks) if scaled else None
    for half in range(halves):
        for block in range(blocks):
            copies[half * blocks + block].wait()
        picked = dot(take, held_ref[half])
        if scaled:
            picked = picked * scale
        picked = picked.astype(BF16)
        for place in range(rows // run):
            start = (place * halves + half) * run
            out_ref[start : start + run] = picked[place * run : (place + 1) * run]


def send_rows(source, lists, halves, blocks):
    slots, experts = lists[0].shape
    tokens, width = source.shape
    cols = width // (halves * blocks)
    rows = halves * experts * blocks * slots
    return pl.pallas_call(
        functools.partial(send_kernel, halves, blocks, len(lists) == 2),
        in_specs=[hbm()] * (len(lists) + 1),
        out_specs=vmem(),
        out_shape=shape_of(rows, cols),
        scratch_shapes=[
            pltpu.VMEM((halves, blocks * tokens, cols), BF16),
            pltpu.SemaphoreType.DMA((halves, blocks)),
            pltpu.SemaphoreType.DMA((2,)),
        ]
        + [pltpu.VMEM((slots, experts), value.dtype) for value in lists],
        compiler_params=params(16),
        cost_estimate=cost(2 * rows * cols * tokens * blocks, 2 * tokens * width + 2 * rows * cols),
        name="send_rows",
    )(*[in_hbm(value) for value in lists], in_hbm(source))


def sort_matrix(rows, blocks, slots, back):
    a = iota((rows, rows), 1 if back else 0)
    b = iota((rows, rows), 0 if back else 1)
    group = rows // blocks
    return one_hot(a % group // slots * (blocks * slots) + a // group * slots + a % slots == b)


def sort_rows(messages_ref, rows_ref, slots):
    blocks, total = rows_ref.shape[:2]
    if blocks == 1:
        rows_ref[0] = messages_ref[...]
        return
    size = min(blocks * total, 256)
    group = size // blocks
    order = sort_matrix(size, blocks, slots, False)
    for part in range(total // group):
        ordered = dot(order, messages_ref[part * size : (part + 1) * size]).astype(BF16)
        for block in range(blocks):
            rows_ref[block, part * group : (part + 1) * group] = ordered[block * group : (block + 1) * group]


def unsort_rows(made, out_ref, slots, span=slice(None)):
    blocks, total = len(made), made[0].shape[0]
    if blocks == 1:
        out_ref[:, span] = made[0]
        return
    size = min(blocks * total, 256)
    group = size // blocks
    order = sort_matrix(size, blocks, slots, True)
    for part in range(total // group):
        stacked = jnp.concatenate([value[part * group : (part + 1) * group] for value in made], axis=0)
        out_ref[part * size : (part + 1) * size, span] = dot(order, stacked).astype(BF16)


def spans(ref, blocks):
    cols = ref // blocks
    return [slice(block * cols, (block + 1) * cols) for block in range(blocks)]


def added(terms):
    return functools.reduce(jnp.add, terms)


def pieces_of(width):
    if width % 256 or width <= 768:
        return [(0, width)]
    first = width // 2 // 256 * 256
    return [(0, first), (first, width - first)]


class Stream:
    def __init__(self, sems):
        self.sems, self.copies = sems, []

    def start(self, source, target):
        copy = pltpu.make_async_copy(source, target, self.sems.at[len(self.copies)])
        copy.start()
        self.copies.append(copy)
        return copy


def in_sums_kernel(slots, messages_ref, gate_ref, up_ref, out_ref, kept_ref, rows_ref, held_ref, acc_ref, sems):
    blocks, _, cols = rows_ref.shape
    hidden = gate_ref.shape[2]
    stream = Stream(sems)
    cuts = [(block, start, size) for block in range(blocks) for start, size in pieces_of(cols)]
    copies = []
    for block, start, size in cuts:
        span = slice(block * cols + start, block * cols + start + size)
        copies += [stream.start(ref.at[0, span], held_ref.at[i, span]) for i, ref in enumerate((gate_ref, up_ref))]
    sort_rows(messages_ref, rows_ref, slots)
    kept = stream.start(rows_ref, kept_ref)
    for number, (block, start, size) in enumerate(cuts):
        span = slice(block * cols + start, block * cols + start + size)
        for i in range(2):
            copies[2 * number + i].wait()
            term = dot(rows_ref[block, :, start : start + size], held_ref[i, span])
            acc_ref[i] = term if number == 0 else acc_ref[i] + term
    for i in range(2):
        out_ref[:, i * hidden : (i + 1) * hidden] = acc_ref[i].astype(BF16)
    kept.wait()


def in_sums(messages, w_gate, w_up, blocks, slots):
    part, hidden = w_gate.shape[1:]
    rows = messages.shape[0] // blocks
    cols = part // blocks
    return pl.pallas_call(
        functools.partial(in_sums_kernel, slots),
        in_specs=[vmem(), hbm(), hbm()],
        out_specs=[vmem(), hbm()],
        out_shape=[shape_of(rows, 2 * hidden), hbm_shape(blocks, rows, cols)],
        scratch_shapes=[
            pltpu.VMEM((blocks, rows, cols), BF16),
            pltpu.VMEM((2, part, hidden), BF16),
            pltpu.VMEM((2, rows, hidden), F32),
            pltpu.SemaphoreType.DMA((2 * blocks * len(pieces_of(cols)) + 1,)),
        ],
        compiler_params=params(),
        cost_estimate=cost(4 * rows * part * hidden, 4 * part * hidden),
        name="gate_up_sums",
    )(messages, in_hbm(w_gate), in_hbm(w_up))


def up_sums_kernel(slots, messages_ref, down_ref, out_ref, kept_ref, rows_ref, held_ref, acc_ref, sems):
    blocks, _, cols = rows_ref.shape
    stream = Stream(sems)
    cuts = [(block, start, size) for block in range(blocks) for start, size in pieces_of(cols)]
    copies = []
    for block, start, size in cuts:
        span = slice(block * cols + start, block * cols + start + size)
        copies.append(stream.start(down_ref.at[0, :, span], held_ref.at[:, span]))
    sort_rows(messages_ref, rows_ref, slots)
    kept = stream.start(rows_ref, kept_ref)
    for number, (block, start, size) in enumerate(cuts):
        span = slice(block * cols + start, block * cols + start + size)
        copies[number].wait()
        term = dot(rows_ref[block, :, start : start + size], held_ref[:, span], ((1,), (1,)))
        acc_ref[...] = term if number == 0 else acc_ref[...] + term
    out_ref[...] = acc_ref[...].astype(BF16)
    kept.wait()


def up_sums(messages, w_down, blocks, slots):
    hidden, part = w_down.shape[1:]
    rows = messages.shape[0] // blocks
    cols = part // blocks
    return pl.pallas_call(
        functools.partial(up_sums_kernel, slots),
        in_specs=[vmem(), hbm()],
        out_specs=[vmem(), hbm()],
        out_shape=[shape_of(rows, hidden), hbm_shape(blocks, rows, cols)],
        scratch_shapes=[
            pltpu.VMEM((blocks, rows, cols), BF16),
            pltpu.VMEM((hidden, part), BF16),
            pltpu.VMEM((rows, hidden), F32),
            pltpu.SemaphoreType.DMA((blocks * len(pieces_of(cols)) + 1,)),
        ],
        compiler_params=params(),
        cost_estimate=cost(2 * rows * part * hidden, 2 * part * hidden),
        name="back_sums",
    )(messages, in_hbm(w_down))


def row_parts(total):
    size = min(total, 128)
    return [slice(start, start + size) for start in range(0, total, size)]


def summed(refs, rows, span):
    return added([ref[rows, span].astype(F32) for ref in refs])


def out_rows_kernel(slots, blocks, count, *refs):
    shares, (down_ref, act_ref, out_ref) = refs[:count], refs[count:]
    hidden, part = down_ref.shape[1:]
    for rows in row_parts(act_ref.shape[0]):
        gate_sum = summed(shares, rows, slice(0, hidden))
        up_sum = summed(shares, rows, slice(hidden, 2 * hidden))
        act_ref[rows] = (gate_sum * jax.nn.sigmoid(gate_sum) * up_sum).astype(BF16)
    unsort_rows([dot(act_ref[...], down_ref[0, :, span]).astype(BF16) for span in spans(part, blocks)], out_ref, slots)


def out_rows(shares, w_down, blocks, slots):
    hidden, part = w_down.shape[1:]
    rows = shares[0].shape[0]
    return pl.pallas_call(
        functools.partial(out_rows_kernel, slots, blocks, len(shares)),
        in_specs=[vmem()] * (len(shares) + 1),
        out_specs=[vmem()] * 2,
        out_shape=[shape_of(rows, hidden), shape_of(blocks * rows, part // blocks)],
        compiler_params=params(),
        cost_estimate=cost(2 * rows * part * hidden, 2 * part * hidden),
        name="output_rows",
    )(*shares, w_down)


def grad_rows_kernel(slots, blocks, count, *refs):
    shares, backs = refs[:count], refs[count : 2 * count]
    gate_ref, up_ref, kept_ref, out_ref, act_ref, held_ref, sems = refs[2 * count :]
    part, hidden = gate_ref.shape[1:]
    cols = part // blocks
    stream = Stream(sems)
    cuts = [(start, size, block) for start, size in pieces_of(cols) for block in range(blocks)]
    copies = []
    for start, size, block in cuts:
        span = slice(block * cols + start, block * cols + start + size)
        copies.append([stream.start(r.at[0, span], held_ref.at[i, span]) for i, r in enumerate((gate_ref, up_ref))])
    for rows in row_parts(act_ref.shape[0]):
        gate_sum = summed(shares, rows, slice(0, hidden))
        up_sum = summed(shares, rows, slice(hidden, 2 * hidden))
        back_sum = summed(backs, rows, slice(0, hidden))
        sig = jax.nn.sigmoid(gate_sum)
        act_ref[rows, :hidden] = (back_sum * up_sum * sig * (1.0 + gate_sum * (1.0 - sig))).astype(BF16)
        act_ref[rows, hidden:] = (back_sum * (gate_sum * sig)).astype(BF16)
    kept = stream.start(act_ref, kept_ref)
    made = []
    for (start, size, block), pair in zip(cuts, copies):
        span = slice(block * cols + start, block * cols + start + size)
        terms = []
        for i in range(2):
            pair[i].wait()
            terms.append(dot(act_ref[:, i * hidden : (i + 1) * hidden], held_ref[i, span], ((1,), (1,))))
        made.append(added(terms).astype(BF16))
        if block == blocks - 1:
            unsort_rows(made, out_ref, slots, slice(start, start + size))
            made = []
    kept.wait()


def grad_rows(shares, backs, w_gate, w_up, blocks, slots):
    part, hidden = w_gate.shape[1:]
    rows = shares[0].shape[0]
    cols = part // blocks
    return pl.pallas_call(
        functools.partial(grad_rows_kernel, slots, blocks, len(shares)),
        in_specs=[vmem()] * (2 * len(shares)) + [hbm()] * 2,
        out_specs=[hbm(), vmem()],
        out_shape=[hbm_shape(rows, 2 * hidden), shape_of(blocks * rows, cols)],
        scratch_shapes=[
            pltpu.VMEM((rows, 2 * hidden), BF16),
            pltpu.VMEM((2, part, hidden), BF16),
            pltpu.SemaphoreType.DMA((2 * blocks * len(pieces_of(cols)) + 1,)),
        ],
        compiler_params=params(40),
        cost_estimate=cost(4 * rows * part * hidden, 4 * part * hidden),
        name="gradient_rows",
    )(*shares, *backs, in_hbm(w_gate), in_hbm(w_up))


def weights_kernel(rows_in_ref, rows_up_ref, act_ref, grad_act_ref, gate_ref, up_ref, down_ref):
    hidden = gate_ref.shape[2]
    rows_in = rows_in_ref[0]
    gate_ref[0] = dot(rows_in, grad_act_ref[:, :hidden], ((0,), (0,))).astype(BF16)
    up_ref[0] = dot(rows_in, grad_act_ref[:, hidden:], ((0,), (0,))).astype(BF16)
    down_ref[0] = dot(act_ref[...], rows_up_ref[0], ((0,), (0,))).astype(BF16)


def weight_grads(rows_in, rows_up, act, grad_act):
    blocks, total, width = rows_in.shape
    part = blocks * width
    hidden = act.shape[1]
    cols = block_of(width, 640)
    steps = width // cols
    chunk = pl.BlockSpec((1, total, cols), lambda k, b: (k, 0, b))
    tall = pl.BlockSpec((1, cols, hidden), lambda k, b: (0, k * steps + b, 0))
    return pl.pallas_call(
        weights_kernel,
        grid=(blocks, steps),
        in_specs=[
            chunk,
            chunk,
            pl.BlockSpec((total, hidden), lambda k, b: (0, 0)),
            pl.BlockSpec((total, 2 * hidden), lambda k, b: (0, 0)),
        ],
        out_specs=[tall, tall, pl.BlockSpec((1, hidden, cols), lambda k, b: (0, 0, k * steps + b))],
        out_shape=[shape_of(1, part, hidden), shape_of(1, part, hidden), shape_of(1, hidden, part)],
        compiler_params=params(),
        cost_estimate=cost(6 * total * part * hidden, 6 * part * hidden),
        name="weight_grads",
    )(rows_in, rows_up, act, grad_act)


def back_rows(back_ref, half, halves, run):
    total = back_ref.shape[0]
    return jnp.concatenate([back_ref[start : start + run] for start in range(half * run, total, halves * run)], axis=0)


def put_columns(held_ref, target_ref, sems, half, block):
    blocks, _, cols = held_ref.shape[1:]
    place = half * blocks + block
    copy = pltpu.make_async_copy(
        held_ref.at[half, block], target_ref.at[:, place * cols : (place + 1) * cols], sems.at[half, block]
    )
    copy.start()
    return copy


def mixed_kernel(picks_ref, gates_ref, cot_ref, back_ref, mixed_ref, gate_grad_ref, put_ref, held_ref, sems):
    slots, experts = picks_ref.shape
    halves, blocks, tokens, cols = held_ref.shape
    rows = experts * blocks * slots
    hit = spread_row(picks_ref[...].astype(F32), blocks).astype(jnp.int32) == iota((tokens, rows), 0)
    scale = spread_row(gates_ref[...], blocks)
    of_block = iota((tokens, rows), 1) % (blocks * slots) // slots
    run = planes_of(experts) * blocks * slots
    backs = [back_rows(back_ref, half, halves, run) for half in range(halves)]
    copies = []
    products = None
    for block in range(blocks):
        inside = hit & (of_block == block)
        put_ref[block] = one_hot(inside)
        rest = jnp.where(inside, scale, 0.0)
        pieces = []
        for _ in range(3):
            pieces.append(rest.astype(BF16))
            rest = rest - pieces[-1].astype(F32)
        for half in range(halves):
            back = backs[half]
            held_ref[half, block] = added([dot(piece, back) for piece in pieces]).astype(BF16)
            copies.append(put_columns(held_ref, mixed_ref, sems, half, block))
            place = half * blocks + block
            product = dot(cot_ref[:, place * cols : (place + 1) * cols], back, ((1,), (1,)))
            product = jnp.where(inside, product, 0.0)
            products = product if products is None else products + product
    values = jnp.sum(products, axis=0, keepdims=True)
    mine = iota((slots, rows), 1) % slots == iota((slots, rows), 0)
    owner = (expert_at(iota((rows, experts), 0) // (blocks * slots), experts) == iota((rows, experts), 1)).astype(F32)
    gate_grad_ref[...] = exact_dot(jnp.where(mine, values, 0.0), owner)
    for copy in copies:
        copy.wait()


def mix_rows(back, cotangent, picks, gates, halves, blocks):
    slots, experts = picks.shape
    tokens, width = cotangent.shape
    cols = width // (halves * blocks)
    rows = experts * blocks * slots
    return pl.pallas_call(
        mixed_kernel,
        in_specs=[vmem()] * 4,
        out_specs=[hbm(), vmem(), vmem()],
        out_shape=[shape_of(tokens, width), shape_of(slots, experts, dtype=F32), shape_of(blocks, tokens, rows)],
        scratch_shapes=[pltpu.VMEM((halves, blocks, tokens, cols), BF16), pltpu.SemaphoreType.DMA((halves, blocks))],
        compiler_params=params(16),
        cost_estimate=cost(8 * rows * tokens * width, 4 * tokens * width),
        name="mixed_rows",
    )(picks, gates, cotangent, back)


def token_grad_kernel(run, put_ref, back_ref, grad_ref, held_ref, sems):
    halves, blocks = held_ref.shape[:2]
    copies = []
    for half in range(halves):
        back = back_rows(back_ref, half, halves, run)
        for block in range(blocks):
            held_ref[half, block] = dot(put_ref[block], back).astype(BF16)
            copies.append(put_columns(held_ref, grad_ref, sems, half, block))
    for copy in copies:
        copy.wait()


def token_grads(back, put, halves, run):
    blocks, tokens, rows = put.shape
    cols = back.shape[1]
    width = halves * blocks * cols
    return pl.pallas_call(
        functools.partial(token_grad_kernel, run),
        in_specs=[vmem()] * 2,
        out_specs=hbm(),
        out_shape=shape_of(tokens, width),
        scratch_shapes=[pltpu.VMEM((halves, blocks, tokens, cols), BF16), pltpu.SemaphoreType.DMA((halves, blocks))],
        compiler_params=params(16),
        cost_estimate=cost(2 * rows * tokens * width, 2 * tokens * width),
        name="token_grads",
    )(put, back)


def to_owners(halves, experts, messages):
    planes = planes_of(experts)
    order = [
        half * experts + plane * (experts // planes) + place
        for place in range(experts // planes)
        for half in range(halves)
        for plane in range(planes)
    ]
    return lax.all_to_all(
        messages, EVERYONE, split_axis=0, concat_axis=0, tiled=True, axis_index_groups=[order]
    )


def dp_shares(own, halves):
    shares = [own] + [
        lax.ppermute(own, "dp", [(i, (i + shift) % halves) for i in range(halves)]) for shift in range(1, halves)
    ]
    return shares if halves <= 2 else [added([share.astype(F32) for share in shares])]


def body(halves, tokens, cotangent, picks, gates, w_gate, w_up, w_down):
    experts, slots = picks.shape[1:]
    scatter = functools.partial(to_owners, halves, experts)
    blocks = 2 if tokens.shape[1] // halves % 256 == 0 else 1
    picks_t = picks[0].T
    gates_t = gates[0].T
    arrived_in = scatter(send_rows(tokens, (picks_t,), halves, blocks))
    arrived_up = scatter(send_rows(cotangent, (picks_t, gates_t), halves, blocks))
    own_sums, rows_in = in_sums(arrived_in, w_gate, w_up, blocks, slots)
    shares = dp_shares(own_sums, halves)
    act, outputs = out_rows(shares, w_down, blocks, slots)
    back_out = scatter(outputs)
    own_back, rows_up = up_sums(arrived_up, w_down, blocks, slots)
    backs = dp_shares(own_back, halves)
    grad_act, gradients = grad_rows(shares, backs, w_gate, w_up, blocks, slots)
    back_grad = scatter(gradients)
    grad_gate_w, grad_up_w, grad_down = weight_grads(rows_in, rows_up, act, grad_act)
    mixed, gate_grad, put = mix_rows(back_out, cotangent, picks_t, gates_t, halves, blocks)
    token_grad = token_grads(back_grad, put, halves, planes_of(experts) * blocks * slots)
    return mixed, token_grad, gate_grad.T[None], grad_gate_w, grad_up_w, grad_down


def solution(mesh):
    rows = P(("dp", "expert"), None)
    lists = P(("dp", "expert"), None, None)
    tall = P("expert", "dp", None)
    wide = P("expert", None, "dp")
    return jax.shard_map(
        functools.partial(body, mesh.shape["dp"]),
        mesh=mesh,
        in_specs=(rows, rows, lists, lists, tall, tall, wide),
        out_specs=(rows, rows, lists, tall, tall, wide),
        check_vma=False,
    )
```

```python
import functools

import jax
import jax.numpy as jnp
from jax import lax
from jax.experimental import pallas as pl
from jax.experimental.pallas import tpu as pltpu
from jax.sharding import PartitionSpec as P

F32 = jnp.float32
BF16 = jnp.bfloat16
MIB = 1024 * 1024
EVERYONE = ("dp", "expert")


def dot(left, right, dims=((1,), (0,)), precision=None):
    return lax.dot_general(left, right, (dims, ((), ())), precision=precision, preferred_element_type=F32)


def exact_dot(left, right, dims=((1,), (0,))):
    return dot(left, right, dims, lax.Precision.HIGHEST)


def iota(shape, axis):
    return lax.broadcasted_iota(jnp.int32, shape, axis)


def planes_of(experts):
    return experts // 4 if experts % 4 == 0 else 1


def expert_at(place, experts):
    planes = planes_of(experts)
    return place % planes * (experts // planes) + place // planes


def one_hot(condition):
    return jnp.where(condition, 1.0, 0.0).astype(BF16)


def vmem():
    return pl.BlockSpec(memory_space=pltpu.VMEM)


def hbm():
    return pl.BlockSpec(memory_space=pltpu.HBM)


def in_hbm(value):
    return pltpu.with_memory_space_constraint(value, pltpu.HBM)


def shape_of(*sizes, dtype=BF16):
    return jax.ShapeDtypeStruct(sizes, dtype)


def hbm_shape(*sizes):
    return pltpu.HBM(sizes, BF16)


def params(mib=24):
    return pltpu.CompilerParams(vmem_limit_bytes=mib * MIB)


def cost(flops, moved):
    return pl.CostEstimate(flops=flops, bytes_accessed=moved, transcendentals=0)


def block_of(width, limit):
    best = 128
    for size in range(128, limit + 1, 128):
        if width % size == 0:
            best = size
    return best


def spread_column(values, blocks):
    slots, experts = values.shape
    rows = experts * blocks * slots
    owner = (expert_at(iota((rows, experts), 0) // (blocks * slots), experts) == iota((rows, experts), 1)).astype(F32)
    wide = exact_dot(owner, values, ((1,), (1,)))
    mine = iota((rows, slots), 0) % slots == iota((rows, slots), 1)
    return jnp.sum(jnp.where(mine, wide, 0.0), axis=1, keepdims=True)


def spread_row(values, blocks):
    slots, experts = values.shape
    rows = experts * blocks * slots
    owner = (expert_at(iota((experts, rows), 1) // (blocks * slots), experts) == iota((experts, rows), 0)).astype(F32)
    wide = exact_dot(values, owner)
    mine = iota((slots, rows), 1) % slots == iota((slots, rows), 0)
    return jnp.sum(jnp.where(mine, wide, 0.0), axis=0, keepdims=True)


def send_kernel(halves, blocks, scaled, extra, *refs):
    count = 2 if scaled else 1
    lists, source_ref, refs = refs[:count], refs[count], refs[count + 1 :]
    kept, out_ref, refs = refs[:extra], refs[extra], refs[extra + 1 :]
    kept_refs, refs = refs[:extra], refs[extra:]
    held_ref, sems, list_sems, kept_sems = refs[:4]
    list_refs = refs[4:]
    rows, cols = out_ref.shape
    rows = rows // halves
    tokens = source_ref.shape[0]
    list_copies = [
        pltpu.make_async_copy(ref, target, list_sems.at[i]) for i, (ref, target) in enumerate(zip(lists, list_refs))
    ]
    copies = []
    for copy in list_copies:
        copy.start()
    for half in range(halves):
        for block in range(blocks):
            place = half * blocks + block
            copies.append(
                pltpu.make_async_copy(
                    source_ref.at[:, place * cols : (place + 1) * cols],
                    held_ref.at[half, block * tokens : (block + 1) * tokens],
                    sems.at[half, block],
                )
            )
            copies[-1].start()
    kept_copies = [
        pltpu.make_async_copy(ref, target, kept_sems.at[i]) for i, (ref, target) in enumerate(zip(kept, kept_refs))
    ]
    for copy in kept_copies:
        copy.start()
    for copy in list_copies:
        copy.wait()
    slots, experts = list_refs[0].shape
    run = planes_of(experts) * blocks * slots
    chosen = spread_column(list_refs[0][...].astype(F32), blocks).astype(jnp.int32)
    target = chosen + iota((rows, 1), 0) % (blocks * slots) // slots * tokens
    take = one_hot(target == iota((rows, blocks * tokens), 1))
    scale = spread_column(list_refs[1][...], blocks) if scaled else None
    for half in range(halves):
        for block in range(blocks):
            copies[half * blocks + block].wait()
        picked = dot(take, held_ref[half])
        if scaled:
            picked = picked * scale
        picked = picked.astype(BF16)
        for place in range(rows // run):
            start = (place * halves + half) * run
            out_ref[start : start + run] = picked[place * run : (place + 1) * run]
    for copy in kept_copies:
        copy.wait()


def send_rows(source, lists, halves, blocks, kept=()):
    slots, experts = lists[0].shape
    tokens, width = source.shape
    cols = width // (halves * blocks)
    rows = halves * experts * blocks * slots
    return pl.pallas_call(
        functools.partial(send_kernel, halves, blocks, len(lists) == 2, len(kept)),
        in_specs=[hbm()] * (len(lists) + 1 + len(kept)),
        out_specs=[vmem()] * (1 + len(kept)),
        out_shape=[shape_of(rows, cols)] + [shape_of(*value.shape) for value in kept],
        scratch_shapes=[
            pltpu.VMEM((halves, blocks * tokens, cols), BF16),
            pltpu.SemaphoreType.DMA((halves, blocks)),
            pltpu.SemaphoreType.DMA((2,)),
            pltpu.SemaphoreType.DMA((2,)),
        ]
        + [pltpu.VMEM((slots, experts), value.dtype) for value in lists],
        compiler_params=params(16),
        cost_estimate=cost(2 * rows * cols * tokens * blocks, 2 * tokens * width + 2 * sum(v.size for v in kept)),
        name="send_rows",
    )(*[in_hbm(value) for value in lists], in_hbm(source), *[in_hbm(value) for value in kept])


def sort_matrix(rows, blocks, slots, back):
    a = iota((rows, rows), 1 if back else 0)
    b = iota((rows, rows), 0 if back else 1)
    group = rows // blocks
    return one_hot(a % group // slots * (blocks * slots) + a // group * slots + a % slots == b)


def sort_rows(messages_ref, rows_ref, slots):
    blocks, total = rows_ref.shape[:2]
    if blocks == 1:
        rows_ref[0] = messages_ref[...]
        return
    size = min(blocks * total, 256)
    group = size // blocks
    order = sort_matrix(size, blocks, slots, False)
    for part in range(total // group):
        ordered = dot(order, messages_ref[part * size : (part + 1) * size]).astype(BF16)
        for block in range(blocks):
            rows_ref[block, part * group : (part + 1) * group] = ordered[block * group : (block + 1) * group]


def unsort_rows(made, out_ref, slots, span=slice(None)):
    blocks, total = len(made), made[0].shape[0]
    if blocks == 1:
        out_ref[:, span] = made[0]
        return
    size = min(blocks * total, 256)
    group = size // blocks
    order = sort_matrix(size, blocks, slots, True)
    for part in range(total // group):
        stacked = jnp.concatenate([value[part * group : (part + 1) * group] for value in made], axis=0)
        out_ref[part * size : (part + 1) * size, span] = dot(order, stacked).astype(BF16)


def spans(ref, blocks):
    cols = ref // blocks
    return [slice(block * cols, (block + 1) * cols) for block in range(blocks)]


def added(terms):
    return functools.reduce(jnp.add, terms)


def pieces_of(width):
    if width % 256 or width <= 768:
        return [(0, width)]
    first = width // 2 // 256 * 256
    return [(0, first), (first, width - first)]


class Stream:
    def __init__(self, sems):
        self.sems, self.copies = sems, []

    def start(self, source, target):
        copy = pltpu.make_async_copy(source, target, self.sems.at[len(self.copies)])
        copy.start()
        self.copies.append(copy)
        return copy


def sums_kernel(slots, back, messages_ref, *refs):
    count = 1 if back else 2
    weights, (_, out_ref, kept_ref, _, rows_ref, sem) = refs[:count], refs[count:]
    blocks, _, cols = rows_ref.shape
    hidden = out_ref.shape[1] // count
    sort_rows(messages_ref, rows_ref, slots)
    kept = pltpu.make_async_copy(rows_ref, kept_ref, sem)
    kept.start()
    for place, ref in enumerate(weights):
        terms = []
        for block, span in enumerate(spans(blocks * cols, blocks)):
            if back:
                terms.append(dot(rows_ref[block], ref[0, :, span], ((1,), (1,))))
            else:
                terms.append(dot(rows_ref[block], ref[0, span, :]))
        out_ref[:, place * hidden : (place + 1) * hidden] = added(terms).astype(BF16)
    kept.wait()


def column_sums(messages, weights, following, hidden, blocks, slots):
    rows = messages.shape[0] // blocks
    cols = messages.shape[1]
    back = len(weights) == 1
    return pl.pallas_call(
        functools.partial(sums_kernel, slots, back),
        in_specs=[vmem()] * (1 + len(weights)) + [hbm()],
        out_specs=[vmem(), hbm(), hbm()],
        out_shape=[
            shape_of(rows, len(weights) * hidden),
            hbm_shape(blocks, rows, cols),
            hbm_shape(*following.shape),
        ],
        scratch_shapes=[pltpu.VMEM((blocks, rows, cols), BF16), pltpu.SemaphoreType.DMA],
        input_output_aliases={1 + len(weights): 2},
        compiler_params=params(),
        cost_estimate=cost(
            2 * len(weights) * rows * blocks * cols * hidden, 2 * len(weights) * blocks * cols * hidden
        ),
        name="back_sums" if back else "gate_up_sums",
    )(messages, *weights, in_hbm(following))


def row_parts(total):
    size = min(total, 128)
    return [slice(start, start + size) for start in range(0, total, size)]


def summed(refs, rows, span):
    return added([ref[rows, span].astype(F32) for ref in refs])


def out_rows_kernel(slots, blocks, count, *refs):
    shares, (down_ref, act_ref, out_ref) = refs[:count], refs[count:]
    hidden, part = down_ref.shape[1:]
    for rows in row_parts(act_ref.shape[0]):
        gate_sum = summed(shares, rows, slice(0, hidden))
        up_sum = summed(shares, rows, slice(hidden, 2 * hidden))
        act_ref[rows] = (gate_sum * jax.nn.sigmoid(gate_sum) * up_sum).astype(BF16)
    unsort_rows([dot(act_ref[...], down_ref[0, :, span]).astype(BF16) for span in spans(part, blocks)], out_ref, slots)


def out_rows(shares, w_down, blocks, slots):
    hidden, part = w_down.shape[1:]
    rows = shares[0].shape[0]
    return pl.pallas_call(
        functools.partial(out_rows_kernel, slots, blocks, len(shares)),
        in_specs=[vmem()] * (len(shares) + 1),
        out_specs=[vmem()] * 2,
        out_shape=[shape_of(rows, hidden), shape_of(blocks * rows, part // blocks)],
        compiler_params=params(),
        cost_estimate=cost(2 * rows * part * hidden, 2 * part * hidden),
        name="output_rows",
    )(*shares, w_down)


def grad_rows_kernel(slots, blocks, count, *refs):
    shares, backs = refs[:count], refs[count : 2 * count]
    gate_ref, up_ref, kept_ref, out_ref, act_ref, held_ref, sems = refs[2 * count :]
    part, hidden = gate_ref.shape[1:]
    cols = part // blocks
    stream = Stream(sems)
    cuts = [(start, size, block) for start, size in pieces_of(cols) for block in range(blocks)]
    copies = []
    for start, size, block in cuts:
        span = slice(block * cols + start, block * cols + start + size)
        copies.append([stream.start(r.at[0, span], held_ref.at[i, span]) for i, r in enumerate((gate_ref, up_ref))])
    for rows in row_parts(act_ref.shape[0]):
        gate_sum = summed(shares, rows, slice(0, hidden))
        up_sum = summed(shares, rows, slice(hidden, 2 * hidden))
        back_sum = summed(backs, rows, slice(0, hidden))
        sig = jax.nn.sigmoid(gate_sum)
        act_ref[rows, :hidden] = (back_sum * up_sum * sig * (1.0 + gate_sum * (1.0 - sig))).astype(BF16)
        act_ref[rows, hidden:] = (back_sum * (gate_sum * sig)).astype(BF16)
    kept = stream.start(act_ref, kept_ref)
    made = []
    for (start, size, block), pair in zip(cuts, copies):
        span = slice(block * cols + start, block * cols + start + size)
        terms = []
        for i in range(2):
            pair[i].wait()
            terms.append(dot(act_ref[:, i * hidden : (i + 1) * hidden], held_ref[i, span], ((1,), (1,))))
        made.append(added(terms).astype(BF16))
        if block == blocks - 1:
            unsort_rows(made, out_ref, slots, slice(start, start + size))
            made = []
    kept.wait()


def grad_rows(shares, backs, w_gate, w_up, blocks, slots):
    part, hidden = w_gate.shape[1:]
    rows = shares[0].shape[0]
    cols = part // blocks
    return pl.pallas_call(
        functools.partial(grad_rows_kernel, slots, blocks, len(shares)),
        in_specs=[vmem()] * (2 * len(shares)) + [hbm()] * 2,
        out_specs=[hbm(), vmem()],
        out_shape=[hbm_shape(rows, 2 * hidden), shape_of(blocks * rows, cols)],
        scratch_shapes=[
            pltpu.VMEM((rows, 2 * hidden), BF16),
            pltpu.VMEM((2, part, hidden), BF16),
            pltpu.SemaphoreType.DMA((2 * blocks * len(pieces_of(cols)) + 1,)),
        ],
        compiler_params=params(40),
        cost_estimate=cost(4 * rows * part * hidden, 4 * part * hidden),
        name="gradient_rows",
    )(*shares, *backs, in_hbm(w_gate), in_hbm(w_up))


def weights_kernel(rows_in_ref, rows_up_ref, act_ref, grad_act_ref, gate_ref, up_ref, down_ref):
    hidden = gate_ref.shape[2]
    rows_in = rows_in_ref[0]
    gate_ref[0] = dot(rows_in, grad_act_ref[:, :hidden], ((0,), (0,))).astype(BF16)
    up_ref[0] = dot(rows_in, grad_act_ref[:, hidden:], ((0,), (0,))).astype(BF16)
    down_ref[0] = dot(act_ref[...], rows_up_ref[0], ((0,), (0,))).astype(BF16)


def weight_grads(rows_in, rows_up, act, grad_act):
    blocks, total, width = rows_in.shape
    part = blocks * width
    hidden = act.shape[1]
    cols = block_of(width, 640)
    steps = width // cols
    chunk = pl.BlockSpec((1, total, cols), lambda k, b: (k, 0, b))
    tall = pl.BlockSpec((1, cols, hidden), lambda k, b: (0, k * steps + b, 0))
    return pl.pallas_call(
        weights_kernel,
        grid=(blocks, steps),
        in_specs=[
            chunk,
            chunk,
            pl.BlockSpec((total, hidden), lambda k, b: (0, 0)),
            pl.BlockSpec((total, 2 * hidden), lambda k, b: (0, 0)),
        ],
        out_specs=[tall, tall, pl.BlockSpec((1, hidden, cols), lambda k, b: (0, 0, k * steps + b))],
        out_shape=[shape_of(1, part, hidden), shape_of(1, part, hidden), shape_of(1, hidden, part)],
        compiler_params=params(),
        cost_estimate=cost(6 * total * part * hidden, 6 * part * hidden),
        name="weight_grads",
    )(rows_in, rows_up, act, grad_act)


def back_rows(back_ref, half, halves, run):
    total = back_ref.shape[0]
    return jnp.concatenate([back_ref[start : start + run] for start in range(half * run, total, halves * run)], axis=0)


def put_columns(held_ref, target_ref, sems, half, block):
    blocks, _, cols = held_ref.shape[1:]
    place = half * blocks + block
    copy = pltpu.make_async_copy(
        held_ref.at[half, block], target_ref.at[:, place * cols : (place + 1) * cols], sems.at[half, block]
    )
    copy.start()
    return copy


def mixed_kernel(picks_ref, gates_ref, cot_ref, back_ref, mixed_ref, gate_grad_ref, put_ref, held_ref, sems):
    slots, experts = picks_ref.shape
    halves, blocks, tokens, cols = held_ref.shape
    rows = experts * blocks * slots
    hit = spread_row(picks_ref[...].astype(F32), blocks).astype(jnp.int32) == iota((tokens, rows), 0)
    scale = spread_row(gates_ref[...], blocks)
    of_block = iota((tokens, rows), 1) % (blocks * slots) // slots
    run = planes_of(experts) * blocks * slots
    backs = [back_rows(back_ref, half, halves, run) for half in range(halves)]
    copies = []
    products = None
    for block in range(blocks):
        inside = hit & (of_block == block)
        put_ref[block] = one_hot(inside)
        rest = jnp.where(inside, scale, 0.0)
        pieces = []
        for _ in range(3):
            pieces.append(rest.astype(BF16))
            rest = rest - pieces[-1].astype(F32)
        for half in range(halves):
            back = backs[half]
            held_ref[half, block] = added([dot(piece, back) for piece in pieces]).astype(BF16)
            copies.append(put_columns(held_ref, mixed_ref, sems, half, block))
            place = half * blocks + block
            product = dot(cot_ref[:, place * cols : (place + 1) * cols], back, ((1,), (1,)))
            product = jnp.where(inside, product, 0.0)
            products = product if products is None else products + product
    values = jnp.sum(products, axis=0, keepdims=True)
    mine = iota((slots, rows), 1) % slots == iota((slots, rows), 0)
    owner = (expert_at(iota((rows, experts), 0) // (blocks * slots), experts) == iota((rows, experts), 1)).astype(F32)
    gate_grad_ref[...] = exact_dot(jnp.where(mine, values, 0.0), owner)
    for copy in copies:
        copy.wait()


def mix_rows(back, cotangent, picks, gates, halves, blocks):
    slots, experts = picks.shape
    tokens, width = cotangent.shape
    cols = width // (halves * blocks)
    rows = experts * blocks * slots
    return pl.pallas_call(
        mixed_kernel,
        in_specs=[vmem()] * 4,
        out_specs=[hbm(), vmem(), vmem()],
        out_shape=[shape_of(tokens, width), shape_of(slots, experts, dtype=F32), shape_of(blocks, tokens, rows)],
        scratch_shapes=[pltpu.VMEM((halves, blocks, tokens, cols), BF16), pltpu.SemaphoreType.DMA((halves, blocks))],
        compiler_params=params(16),
        cost_estimate=cost(8 * rows * tokens * width, 4 * tokens * width),
        name="mixed_rows",
    )(picks, gates, cotangent, back)


def token_grad_kernel(run, put_ref, back_ref, grad_ref, held_ref, sems):
    halves, blocks = held_ref.shape[:2]
    copies = []
    for half in range(halves):
        back = back_rows(back_ref, half, halves, run)
        for block in range(blocks):
            held_ref[half, block] = dot(put_ref[block], back).astype(BF16)
            copies.append(put_columns(held_ref, grad_ref, sems, half, block))
    for copy in copies:
        copy.wait()


def token_grads(back, put, halves, run):
    blocks, tokens, rows = put.shape
    cols = back.shape[1]
    width = halves * blocks * cols
    return pl.pallas_call(
        functools.partial(token_grad_kernel, run),
        in_specs=[vmem()] * 2,
        out_specs=hbm(),
        out_shape=shape_of(tokens, width),
        scratch_shapes=[pltpu.VMEM((halves, blocks, tokens, cols), BF16), pltpu.SemaphoreType.DMA((halves, blocks))],
        compiler_params=params(16),
        cost_estimate=cost(2 * rows * tokens * width, 2 * tokens * width),
        name="token_grads",
    )(put, back)


def to_owners(halves, experts, messages):
    planes = planes_of(experts)
    order = [
        half * experts + plane * (experts // planes) + place
        for place in range(experts // planes)
        for half in range(halves)
        for plane in range(planes)
    ]
    return lax.all_to_all(
        messages, EVERYONE, split_axis=0, concat_axis=0, tiled=True, axis_index_groups=[order]
    )


def dp_shares(own, halves):
    shares = [own] + [
        lax.ppermute(own, "dp", [(i, (i + shift) % halves) for i in range(halves)]) for shift in range(1, halves)
    ]
    return shares if halves <= 2 else [added([share.astype(F32) for share in shares])]


def body(halves, tokens, cotangent, picks, gates, w_gate, w_up, w_down):
    experts, slots = picks.shape[1:]
    scatter = functools.partial(to_owners, halves, experts)
    blocks = 2 if tokens.shape[1] // halves % 256 == 0 else 1
    picks_t = picks[0].T
    gates_t = gates[0].T
    hidden = w_gate.shape[2]
    arrived_in = scatter(send_rows(tokens, (picks_t,), halves, blocks)[0])
    messages_up, near_gate, near_up = send_rows(cotangent, (picks_t, gates_t), halves, blocks, (w_gate, w_up))
    own_sums, rows_in, messages_up = column_sums(arrived_in, (near_gate, near_up), messages_up, hidden, blocks, slots)
    shares = dp_shares(own_sums, halves)
    arrived_up = scatter(messages_up)
    act, outputs = out_rows(shares, w_down, blocks, slots)
    own_back, rows_up, outputs = column_sums(arrived_up, (w_down,), outputs, hidden, blocks, slots)
    backs = dp_shares(own_back, halves)
    back_out = scatter(outputs)
    grad_act, gradients = grad_rows(shares, backs, w_gate, w_up, blocks, slots)
    back_grad = scatter(gradients)
    grad_gate_w, grad_up_w, grad_down = weight_grads(rows_in, rows_up, act, grad_act)
    mixed, gate_grad, put = mix_rows(back_out, cotangent, picks_t, gates_t, halves, blocks)
    token_grad = token_grads(back_grad, put, halves, planes_of(experts) * blocks * slots)
    return mixed, token_grad, gate_grad.T[None], grad_gate_w, grad_up_w, grad_down


def solution(mesh):
    rows = P(("dp", "expert"), None)
    lists = P(("dp", "expert"), None, None)
    tall = P("expert", "dp", None)
    wide = P("expert", None, "dp")
    return jax.shard_map(
        functools.partial(body, mesh.shape["dp"]),
        mesh=mesh,
        in_specs=(rows, rows, lists, lists, tall, tall, wide),
        out_specs=(rows, rows, lists, tall, tall, wide),
        check_vma=False,
    )
```

```python
import functools

import jax
import jax.numpy as jnp
from jax import lax
from jax.experimental import pallas as pl
from jax.experimental.pallas import tpu as pltpu
from jax.sharding import PartitionSpec as P

F32 = jnp.float32
BF16 = jnp.bfloat16
MIB = 1024 * 1024
EVERYONE = ("dp", "expert")


def dot(left, right, dims=((1,), (0,)), precision=None):
    return lax.dot_general(left, right, (dims, ((), ())), precision=precision, preferred_element_type=F32)


def exact_dot(left, right, dims=((1,), (0,))):
    return dot(left, right, dims, lax.Precision.HIGHEST)


def iota(shape, axis):
    return lax.broadcasted_iota(jnp.int32, shape, axis)


def planes_of(experts):
    return experts // 4 if experts % 4 == 0 else 1


def expert_at(place, experts):
    planes = planes_of(experts)
    return place % planes * (experts // planes) + place // planes


def one_hot(condition):
    return jnp.where(condition, 1.0, 0.0).astype(BF16)


def vmem():
    return pl.BlockSpec(memory_space=pltpu.VMEM)


def hbm():
    return pl.BlockSpec(memory_space=pltpu.HBM)


def in_hbm(value):
    return pltpu.with_memory_space_constraint(value, pltpu.HBM)


def shape_of(*sizes, dtype=BF16):
    return jax.ShapeDtypeStruct(sizes, dtype)


def hbm_shape(*sizes):
    return pltpu.HBM(sizes, BF16)


def params(mib=24):
    return pltpu.CompilerParams(vmem_limit_bytes=mib * MIB)


def cost(flops, moved):
    return pl.CostEstimate(flops=flops, bytes_accessed=moved, transcendentals=0)


def block_of(width, limit):
    best = 128
    for size in range(128, limit + 1, 128):
        if width % size == 0:
            best = size
    return best


def spread_column(values, blocks):
    slots, experts = values.shape
    rows = experts * blocks * slots
    owner = (expert_at(iota((rows, experts), 0) // (blocks * slots), experts) == iota((rows, experts), 1)).astype(F32)
    wide = exact_dot(owner, values, ((1,), (1,)))
    mine = iota((rows, slots), 0) % slots == iota((rows, slots), 1)
    return jnp.sum(jnp.where(mine, wide, 0.0), axis=1, keepdims=True)


def spread_row(values, blocks):
    slots, experts = values.shape
    rows = experts * blocks * slots
    owner = (expert_at(iota((experts, rows), 1) // (blocks * slots), experts) == iota((experts, rows), 0)).astype(F32)
    wide = exact_dot(values, owner)
    mine = iota((slots, rows), 1) % slots == iota((slots, rows), 0)
    return jnp.sum(jnp.where(mine, wide, 0.0), axis=0, keepdims=True)


def send_kernel(halves, blocks, scaled, *refs):
    count = 2 if scaled else 1
    lists, source_ref, out_ref = refs[:count], refs[count], refs[count + 1]
    held_ref, sems, list_sems = refs[count + 2 : count + 5]
    list_refs = refs[count + 5 :]
    rows, cols = out_ref.shape
    rows = rows // halves
    tokens = source_ref.shape[0]
    list_copies = [
        pltpu.make_async_copy(ref, target, list_sems.at[i]) for i, (ref, target) in enumerate(zip(lists, list_refs))
    ]
    copies = []
    for copy in list_copies:
        copy.start()
    for half in range(halves):
        for block in range(blocks):
            place = half * blocks + block
            copies.append(
                pltpu.make_async_copy(
                    source_ref.at[:, place * cols : (place + 1) * cols],
                    held_ref.at[half, block * tokens : (block + 1) * tokens],
                    sems.at[half, block],
                )
            )
            copies[-1].start()
    for copy in list_copies:
        copy.wait()
    slots, experts = list_refs[0].shape
    run = planes_of(experts) * blocks * slots
    chosen = spread_column(list_refs[0][...].astype(F32), blocks).astype(jnp.int32)
    target = chosen + iota((rows, 1), 0) % (blocks * slots) // slots * tokens
    take = one_hot(target == iota((rows, blocks * tokens), 1))
    scale = spread_column(list_refs[1][...], blocks) if scaled else None
    for half in range(halves):
        for block in range(blocks):
            copies[half * blocks + block].wait()
        picked = dot(take, held_ref[half])
        if scaled:
            picked = picked * scale
        picked = picked.astype(BF16)
        for place in range(rows // run):
            start = (place * halves + half) * run
            out_ref[start : start + run] = picked[place * run : (place + 1) * run]


def send_rows(source, lists, halves, blocks):
    slots, experts = lists[0].shape
    tokens, width = source.shape
    cols = width // (halves * blocks)
    rows = halves * experts * blocks * slots
    return pl.pallas_call(
        functools.partial(send_kernel, halves, blocks, len(lists) == 2),
        in_specs=[hbm()] * (len(lists) + 1),
        out_specs=vmem(),
        out_shape=shape_of(rows, cols),
        scratch_shapes=[
            pltpu.VMEM((halves, blocks * tokens, cols), BF16),
            pltpu.SemaphoreType.DMA((halves, blocks)),
            pltpu.SemaphoreType.DMA((2,)),
        ]
        + [pltpu.VMEM((slots, experts), value.dtype) for value in lists],
        compiler_params=params(16),
        cost_estimate=cost(2 * rows * cols * tokens * blocks, 2 * tokens * width + 2 * rows * cols),
        name="send_rows",
    )(*[in_hbm(value) for value in lists], in_hbm(source))


def sort_matrix(rows, blocks, slots, back):
    a = iota((rows, rows), 1 if back else 0)
    b = iota((rows, rows), 0 if back else 1)
    group = rows // blocks
    return one_hot(a % group // slots * (blocks * slots) + a // group * slots + a % slots == b)


def sort_rows(messages_ref, rows_ref, slots):
    blocks, total = rows_ref.shape[:2]
    if blocks == 1:
        rows_ref[0] = messages_ref[...]
        return
    size = min(blocks * total, 256)
    group = size // blocks
    order = sort_matrix(size, blocks, slots, False)
    for part in range(total // group):
        ordered = dot(order, messages_ref[part * size : (part + 1) * size]).astype(BF16)
        for block in range(blocks):
            rows_ref[block, part * group : (part + 1) * group] = ordered[block * group : (block + 1) * group]


def unsort_rows(made, out_ref, slots, span=slice(None)):
    blocks, total = len(made), made[0].shape[0]
    if blocks == 1:
        out_ref[:, span] = made[0]
        return
    size = min(blocks * total, 256)
    group = size // blocks
    order = sort_matrix(size, blocks, slots, True)
    for part in range(total // group):
        stacked = jnp.concatenate([value[part * group : (part + 1) * group] for value in made], axis=0)
        out_ref[part * size : (part + 1) * size, span] = dot(order, stacked).astype(BF16)


def spans(ref, blocks):
    cols = ref // blocks
    return [slice(block * cols, (block + 1) * cols) for block in range(blocks)]


def added(terms):
    return functools.reduce(jnp.add, terms)


def pieces_of(width):
    if width % 256 or width <= 768:
        return [(0, width)]
    first = width // 2 // 256 * 256
    return [(0, first), (first, width - first)]


def thirds_of(height):
    size = height // 3 if height % 384 == 0 else height
    return [(start, size) for start in range(0, height, size)]


class Stream:
    def __init__(self, sems):
        self.sems, self.copies = sems, []

    def start(self, source, target):
        copy = pltpu.make_async_copy(source, target, self.sems.at[len(self.copies)])
        copy.start()
        self.copies.append(copy)
        return copy


def in_sums_kernel(slots, sort, source_ref, weight_ref, out_ref, *refs):
    held_ref, acc_ref, sems = refs[-3:]
    part, hidden = weight_ref.shape[1:]
    stream = Stream(sems)
    if sort:
        rows_ref, kept_ref = refs[:2]
    else:
        rows_ref = source_ref
    blocks, _, cols = rows_ref.shape
    cuts = [(block, start, size) for block in range(blocks) for start, size in pieces_of(cols)]
    spots = [slice(block * cols + start, block * cols + start + size) for block, start, size in cuts]
    copies = [stream.start(weight_ref.at[0, spot], held_ref.at[spot]) for spot in spots]
    if sort:
        sort_rows(source_ref, rows_ref, slots)
        kept = stream.start(rows_ref, kept_ref)
    for number, (block, start, size) in enumerate(cuts):
        copies[number].wait()
        term = dot(rows_ref[block, :, start : start + size], held_ref[spots[number]])
        if number < len(cuts) - 1:
            acc_ref[...] = term if number == 0 else acc_ref[...] + term
        else:
            out_ref[...] = (term if number == 0 else acc_ref[...] + term).astype(BF16)
    if sort:
        kept.wait()


def in_sums(source, weight, blocks, slots):
    part, hidden = weight.shape[1:]
    cols = part // blocks
    sort = len(source.shape) == 2
    rows = source.shape[0] // blocks if sort else source.shape[1]
    more = [shape_of(blocks, rows, cols), hbm_shape(blocks, rows, cols)] if sort else []
    return pl.pallas_call(
        functools.partial(in_sums_kernel, slots, sort),
        in_specs=[vmem(), hbm()],
        out_specs=[vmem()] + ([vmem(), hbm()] if sort else []),
        out_shape=[shape_of(rows, hidden)] + more,
        scratch_shapes=[
            pltpu.VMEM((part, hidden), BF16),
            pltpu.VMEM((rows, hidden), F32),
            pltpu.SemaphoreType.DMA((blocks * len(pieces_of(cols)) + 1,)),
        ],
        compiler_params=params(),
        cost_estimate=cost(2 * rows * part * hidden, 2 * part * hidden),
        name="gate_sums" if sort else "up_sums",
    )(source, in_hbm(weight))


def back_sums_kernel(slots, messages_ref, down_ref, out_ref, kept_ref, rows_ref, held_ref, sems):
    blocks, _, cols = rows_ref.shape
    stream = Stream(sems)
    spots = [slice(start, start + size) for start, size in thirds_of(down_ref.shape[1])]
    copies = [stream.start(down_ref.at[0, spot], held_ref.at[spot]) for spot in spots]
    sort_rows(messages_ref, rows_ref, slots)
    kept = stream.start(rows_ref, kept_ref)
    for spot, copy in zip(spots, copies):
        copy.wait()
        terms = [
            dot(rows_ref[b], held_ref[spot, span], ((1,), (1,))) for b, span in enumerate(spans(blocks * cols, blocks))
        ]
        out_ref[:, spot] = added(terms).astype(BF16)
    kept.wait()


def back_sums(messages, w_down, blocks, slots):
    hidden, part = w_down.shape[1:]
    rows = messages.shape[0] // blocks
    cols = part // blocks
    return pl.pallas_call(
        functools.partial(back_sums_kernel, slots),
        in_specs=[vmem(), hbm()],
        out_specs=[vmem(), hbm()],
        out_shape=[shape_of(rows, hidden), hbm_shape(blocks, rows, cols)],
        scratch_shapes=[
            pltpu.VMEM((blocks, rows, cols), BF16),
            pltpu.VMEM((hidden, part), BF16),
            pltpu.SemaphoreType.DMA((len(thirds_of(hidden)) + 1,)),
        ],
        compiler_params=params(),
        cost_estimate=cost(2 * rows * part * hidden, 2 * part * hidden),
        name="back_sums",
    )(messages, in_hbm(w_down))


def bring_kernel(count, *refs):
    sources, targets, sems = refs[1 : count + 1], refs[count + 1 : 2 * count + 1], refs[-1]
    copies = [pltpu.make_async_copy(s, t, sems.at[i]) for i, (s, t) in enumerate(zip(sources, targets))]
    for copy in copies:
        copy.start()
    for copy in copies:
        copy.wait()


def bring(values, after):
    return pl.pallas_call(
        functools.partial(bring_kernel, len(values)),
        in_specs=[pl.BlockSpec(memory_space=pl.ANY)] + [hbm()] * len(values),
        out_specs=[vmem()] * len(values),
        out_shape=[shape_of(*value.shape) for value in values],
        scratch_shapes=[pltpu.SemaphoreType.DMA((len(values),))],
        compiler_params=params(16),
        cost_estimate=cost(0, 2 * sum(value.size for value in values)),
        name="bring_weights",
    )(after, *[in_hbm(value) for value in values])


def row_parts(total):
    size = min(total, 128)
    return [slice(start, start + size) for start in range(0, total, size)]


def summed(refs, rows):
    return added([ref[rows].astype(F32) for ref in refs])


def out_rows_kernel(slots, blocks, count, *refs):
    gates, ups, (down_ref, act_ref, out_ref) = refs[:count], refs[count : 2 * count], refs[2 * count :]
    part = down_ref.shape[2]
    for rows in row_parts(act_ref.shape[0]):
        gate_sum = summed(gates, rows)
        act_ref[rows] = (gate_sum * jax.nn.sigmoid(gate_sum) * summed(ups, rows)).astype(BF16)
    unsort_rows([dot(act_ref[...], down_ref[0, :, span]).astype(BF16) for span in spans(part, blocks)], out_ref, slots)


def out_rows(gates, ups, w_down, blocks, slots):
    hidden, part = w_down.shape[1:]
    rows = gates[0].shape[0]
    return pl.pallas_call(
        functools.partial(out_rows_kernel, slots, blocks, len(gates)),
        in_specs=[vmem()] * (2 * len(gates) + 1),
        out_specs=[vmem()] * 2,
        out_shape=[shape_of(rows, hidden), shape_of(blocks * rows, part // blocks)],
        compiler_params=params(),
        cost_estimate=cost(2 * rows * part * hidden, 2 * part * hidden),
        name="output_rows",
    )(*gates, *ups, w_down)


def grad_rows_kernel(slots, blocks, count, *refs):
    gates, ups, backs = refs[:count], refs[count : 2 * count], refs[2 * count : 3 * count]
    gate_ref, up_ref, kept_ref, out_ref, act_ref, sem = refs[3 * count :]
    part, hidden = gate_ref.shape[1:]
    cols = part // blocks
    for rows in row_parts(act_ref.shape[0]):
        gate_sum, up_sum, back_sum = summed(gates, rows), summed(ups, rows), summed(backs, rows)
        sig = jax.nn.sigmoid(gate_sum)
        act_ref[rows, :hidden] = (back_sum * up_sum * sig * (1.0 + gate_sum * (1.0 - sig))).astype(BF16)
        act_ref[rows, hidden:] = (back_sum * (gate_sum * sig)).astype(BF16)
    kept = pltpu.make_async_copy(act_ref, kept_ref, sem)
    kept.start()
    for start, size in pieces_of(cols):
        made = []
        for block in range(blocks):
            span = slice(block * cols + start, block * cols + start + size)
            total = dot(act_ref[:, :hidden], gate_ref[0, span, :], ((1,), (1,)))
            total = total + dot(act_ref[:, hidden:], up_ref[0, span, :], ((1,), (1,)))
            made.append(total.astype(BF16))
        unsort_rows(made, out_ref, slots, slice(start, start + size))
    kept.wait()


def grad_rows(gates, ups, backs, w_gate, w_up, blocks, slots):
    part, hidden = w_gate.shape[1:]
    rows = gates[0].shape[0]
    cols = part // blocks
    return pl.pallas_call(
        functools.partial(grad_rows_kernel, slots, blocks, len(gates)),
        in_specs=[vmem()] * (3 * len(gates) + 2),
        out_specs=[hbm(), vmem()],
        out_shape=[hbm_shape(rows, 2 * hidden), shape_of(blocks * rows, cols)],
        scratch_shapes=[pltpu.VMEM((rows, 2 * hidden), BF16), pltpu.SemaphoreType.DMA],
        compiler_params=params(32),
        cost_estimate=cost(4 * rows * part * hidden, 4 * part * hidden),
        name="gradient_rows",
    )(*gates, *ups, *backs, w_gate, w_up)


def weights_kernel(rows_in_ref, rows_up_ref, act_ref, grad_act_ref, gate_ref, up_ref, down_ref):
    hidden = gate_ref.shape[2]
    rows_in = rows_in_ref[0]
    gate_ref[0] = dot(rows_in, grad_act_ref[:, :hidden], ((0,), (0,))).astype(BF16)
    up_ref[0] = dot(rows_in, grad_act_ref[:, hidden:], ((0,), (0,))).astype(BF16)
    down_ref[0] = dot(act_ref[...], rows_up_ref[0], ((0,), (0,))).astype(BF16)


def weight_grads(rows_in, rows_up, act, grad_act):
    blocks, total, width = rows_in.shape
    part = blocks * width
    hidden = act.shape[1]
    cols = block_of(width, 640)
    steps = width // cols
    chunk = pl.BlockSpec((1, total, cols), lambda k, b: (k, 0, b))
    tall = pl.BlockSpec((1, cols, hidden), lambda k, b: (0, k * steps + b, 0))
    return pl.pallas_call(
        weights_kernel,
        grid=(blocks, steps),
        in_specs=[
            chunk,
            chunk,
            pl.BlockSpec((total, hidden), lambda k, b: (0, 0)),
            pl.BlockSpec((total, 2 * hidden), lambda k, b: (0, 0)),
        ],
        out_specs=[tall, tall, pl.BlockSpec((1, hidden, cols), lambda k, b: (0, 0, k * steps + b))],
        out_shape=[shape_of(1, part, hidden), shape_of(1, part, hidden), shape_of(1, hidden, part)],
        compiler_params=params(),
        cost_estimate=cost(6 * total * part * hidden, 6 * part * hidden),
        name="weight_grads",
    )(rows_in, rows_up, act, grad_act)


def back_rows(back_ref, half, halves, run):
    total = back_ref.shape[0]
    return jnp.concatenate([back_ref[start : start + run] for start in range(half * run, total, halves * run)], axis=0)


def put_columns(held_ref, target_ref, sems, half, block):
    blocks, _, cols = held_ref.shape[1:]
    place = half * blocks + block
    copy = pltpu.make_async_copy(
        held_ref.at[half, block], target_ref.at[:, place * cols : (place + 1) * cols], sems.at[half, block]
    )
    copy.start()
    return copy


def mixed_kernel(picks_ref, gates_ref, cot_ref, back_ref, mixed_ref, gate_grad_ref, put_ref, held_ref, sems):
    slots, experts = picks_ref.shape
    halves, blocks, tokens, cols = held_ref.shape
    rows = experts * blocks * slots
    hit = spread_row(picks_ref[...].astype(F32), blocks).astype(jnp.int32) == iota((tokens, rows), 0)
    scale = spread_row(gates_ref[...], blocks)
    of_block = iota((tokens, rows), 1) % (blocks * slots) // slots
    run = planes_of(experts) * blocks * slots
    backs = [back_rows(back_ref, half, halves, run) for half in range(halves)]
    copies = []
    products = None
    for block in range(blocks):
        inside = hit & (of_block == block)
        put_ref[block] = one_hot(inside)
        rest = jnp.where(inside, scale, 0.0)
        pieces = []
        for _ in range(3):
            pieces.append(rest.astype(BF16))
            rest = rest - pieces[-1].astype(F32)
        for half in range(halves):
            back = backs[half]
            held_ref[half, block] = added([dot(piece, back) for piece in pieces]).astype(BF16)
            copies.append(put_columns(held_ref, mixed_ref, sems, half, block))
            place = half * blocks + block
            product = dot(cot_ref[:, place * cols : (place + 1) * cols], back, ((1,), (1,)))
            product = jnp.where(inside, product, 0.0)
            products = product if products is None else products + product
    values = jnp.sum(products, axis=0, keepdims=True)
    mine = iota((slots, rows), 1) % slots == iota((slots, rows), 0)
    owner = (expert_at(iota((rows, experts), 0) // (blocks * slots), experts) == iota((rows, experts), 1)).astype(F32)
    gate_grad_ref[...] = exact_dot(jnp.where(mine, values, 0.0), owner)
    for copy in copies:
        copy.wait()


def mix_rows(back, cotangent, picks, gates, halves, blocks):
    slots, experts = picks.shape
    tokens, width = cotangent.shape
    cols = width // (halves * blocks)
    rows = experts * blocks * slots
    return pl.pallas_call(
        mixed_kernel,
        in_specs=[vmem()] * 4,
        out_specs=[hbm(), vmem(), vmem()],
        out_shape=[shape_of(tokens, width), shape_of(slots, experts, dtype=F32), shape_of(blocks, tokens, rows)],
        scratch_shapes=[pltpu.VMEM((halves, blocks, tokens, cols), BF16), pltpu.SemaphoreType.DMA((halves, blocks))],
        compiler_params=params(16),
        cost_estimate=cost(8 * rows * tokens * width, 4 * tokens * width),
        name="mixed_rows",
    )(picks, gates, cotangent, back)


def token_grad_kernel(run, put_ref, back_ref, grad_ref, held_ref, sems):
    halves, blocks = held_ref.shape[:2]
    copies = []
    for half in range(halves):
        back = back_rows(back_ref, half, halves, run)
        for block in range(blocks):
            held_ref[half, block] = dot(put_ref[block], back).astype(BF16)
            copies.append(put_columns(held_ref, grad_ref, sems, half, block))
    for copy in copies:
        copy.wait()


def token_grads(back, put, halves, run):
    blocks, tokens, rows = put.shape
    cols = back.shape[1]
    width = halves * blocks * cols
    return pl.pallas_call(
        functools.partial(token_grad_kernel, run),
        in_specs=[vmem()] * 2,
        out_specs=hbm(),
        out_shape=shape_of(tokens, width),
        scratch_shapes=[pltpu.VMEM((halves, blocks, tokens, cols), BF16), pltpu.SemaphoreType.DMA((halves, blocks))],
        compiler_params=params(16),
        cost_estimate=cost(2 * rows * tokens * width, 2 * tokens * width),
        name="token_grads",
    )(put, back)


def to_owners(halves, experts, messages):
    planes = planes_of(experts)
    order = [
        half * experts + plane * (experts // planes) + place
        for place in range(experts // planes)
        for half in range(halves)
        for plane in range(planes)
    ]
    return lax.all_to_all(
        messages, EVERYONE, split_axis=0, concat_axis=0, tiled=True, axis_index_groups=[order]
    )


def dp_shares(own, halves):
    shares = [own] + [
        lax.ppermute(own, "dp", [(i, (i + shift) % halves) for i in range(halves)]) for shift in range(1, halves)
    ]
    return shares if halves <= 2 else [added([share.astype(F32) for share in shares])]


def body(halves, tokens, cotangent, picks, gates, w_gate, w_up, w_down):
    experts, slots = picks.shape[1:]
    scatter = functools.partial(to_owners, halves, experts)
    blocks = 2 if tokens.shape[1] // halves % 256 == 0 else 1
    picks_t = picks[0].T
    gates_t = gates[0].T
    arrived_in = scatter(send_rows(tokens, (picks_t,), halves, blocks))
    arrived_up = scatter(send_rows(cotangent, (picks_t, gates_t), halves, blocks))
    own_gate, near_rows, rows_in = in_sums(arrived_in, w_gate, blocks, slots)
    gates_sum = dp_shares(own_gate, halves)
    (own_up,) = in_sums(near_rows, w_up, blocks, slots)
    ups_sum = dp_shares(own_up, halves)
    act, outputs = out_rows(gates_sum, ups_sum, w_down, blocks, slots)
    back_out = scatter(outputs)
    own_back, rows_up = back_sums(arrived_up, w_down, blocks, slots)
    backs_sum = dp_shares(own_back, halves)
    near_gate, near_up = bring((w_gate, w_up), own_back)
    grad_act, gradients = grad_rows(gates_sum, ups_sum, backs_sum, near_gate, near_up, blocks, slots)
    back_grad = scatter(gradients)
    grad_gate_w, grad_up_w, grad_down = weight_grads(rows_in, rows_up, act, grad_act)
    mixed, gate_grad, put = mix_rows(back_out, cotangent, picks_t, gates_t, halves, blocks)
    token_grad = token_grads(back_grad, put, halves, planes_of(experts) * blocks * slots)
    return mixed, token_grad, gate_grad.T[None], grad_gate_w, grad_up_w, grad_down


def solution(mesh):
    rows = P(("dp", "expert"), None)
    lists = P(("dp", "expert"), None, None)
    tall = P("expert", "dp", None)
    wide = P("expert", None, "dp")
    return jax.shard_map(
        functools.partial(body, mesh.shape["dp"]),
        mesh=mesh,
        in_specs=(rows, rows, lists, lists, tall, tall, wide),
        out_specs=(rows, rows, lists, tall, tall, wide),
        check_vma=False,
    )
```

```python
import functools

import jax
import jax.numpy as jnp
from jax import lax
from jax.experimental import pallas as pl
from jax.experimental.pallas import tpu as pltpu
from jax.sharding import PartitionSpec as P

F32 = jnp.float32
BF16 = jnp.bfloat16
MIB = 1024 * 1024
EVERYONE = ("dp", "expert")


def dot(left, right, dims=((1,), (0,)), precision=None):
    return lax.dot_general(left, right, (dims, ((), ())), precision=precision, preferred_element_type=F32)


def exact_dot(left, right, dims=((1,), (0,))):
    return dot(left, right, dims, lax.Precision.HIGHEST)


def iota(shape, axis):
    return lax.broadcasted_iota(jnp.int32, shape, axis)


def planes_of(experts):
    return experts // 4 if experts % 4 == 0 else 1


def expert_at(place, experts):
    planes = planes_of(experts)
    return place % planes * (experts // planes) + place // planes


def split_place(place, halves, planes):
    return (place // (halves * planes) * planes + place % planes) * halves + place // planes % halves


def one_hot(condition):
    return jnp.where(condition, 1.0, 0.0).astype(BF16)


def vmem():
    return pl.BlockSpec(memory_space=pltpu.VMEM)


def hbm():
    return pl.BlockSpec(memory_space=pltpu.HBM)


def in_hbm(value):
    return pltpu.with_memory_space_constraint(value, pltpu.HBM)


def shape_of(*sizes, dtype=BF16):
    return jax.ShapeDtypeStruct(sizes, dtype)


def hbm_shape(*sizes):
    return pltpu.HBM(sizes, BF16)


def params(mib=24):
    return pltpu.CompilerParams(vmem_limit_bytes=mib * MIB)


def cost(flops, moved):
    return pl.CostEstimate(flops=flops, bytes_accessed=moved, transcendentals=0)


def block_of(width, limit):
    best = 128
    for size in range(128, limit + 1, 128):
        if width % size == 0:
            best = size
    return best


def spread_column(values, blocks):
    slots, experts = values.shape
    rows = experts * blocks * slots
    owner = (expert_at(iota((rows, experts), 0) // (blocks * slots), experts) == iota((rows, experts), 1)).astype(F32)
    wide = exact_dot(owner, values, ((1,), (1,)))
    mine = iota((rows, slots), 0) % slots == iota((rows, slots), 1)
    return jnp.sum(jnp.where(mine, wide, 0.0), axis=1, keepdims=True)


def spread_row(values, blocks):
    slots, experts = values.shape
    rows = experts * blocks * slots
    owner = (expert_at(iota((experts, rows), 1) // (blocks * slots), experts) == iota((experts, rows), 0)).astype(F32)
    wide = exact_dot(values, owner)
    mine = iota((slots, rows), 1) % slots == iota((slots, rows), 0)
    return jnp.sum(jnp.where(mine, wide, 0.0), axis=0, keepdims=True)


def send_kernel(halves, blocks, scaled, *refs):
    count = 2 if scaled else 1
    lists, source_ref, out_ref = refs[:count], refs[count], refs[count + 1]
    held_ref, sems, list_sems = refs[count + 2 : count + 5]
    list_refs = refs[count + 5 :]
    rows, cols = out_ref.shape
    rows = rows // halves
    tokens = source_ref.shape[0]
    list_copies = [
        pltpu.make_async_copy(ref, target, list_sems.at[i]) for i, (ref, target) in enumerate(zip(lists, list_refs))
    ]
    copies = []
    for copy in list_copies:
        copy.start()
    for half in range(halves):
        for block in range(blocks):
            place = half * blocks + block
            copies.append(
                pltpu.make_async_copy(
                    source_ref.at[:, place * cols : (place + 1) * cols],
                    held_ref.at[half, block * tokens : (block + 1) * tokens],
                    sems.at[half, block],
                )
            )
            copies[-1].start()
    for copy in list_copies:
        copy.wait()
    slots, experts = list_refs[0].shape
    run = planes_of(experts) * blocks * slots
    chosen = spread_column(list_refs[0][...].astype(F32), blocks).astype(jnp.int32)
    target = chosen + iota((rows, 1), 0) % (blocks * slots) // slots * tokens
    take = one_hot(target == iota((rows, blocks * tokens), 1))
    scale = spread_column(list_refs[1][...], blocks) if scaled else None
    for half in range(halves):
        for block in range(blocks):
            copies[half * blocks + block].wait()
        picked = dot(take, held_ref[half])
        if scaled:
            picked = picked * scale
        picked = picked.astype(BF16)
        for place in range(rows // run):
            start = (place * halves + half) * run
            out_ref[start : start + run] = picked[place * run : (place + 1) * run]


def pair_kernel(blocks, _, picks_ref, gates_ref, source_ref, own_ref, other_ref, held_ref, sems):
    slots, experts = picks_ref.shape
    tokens = source_ref.shape[0]
    rows, cols = own_ref.shape
    half = lax.axis_index("dp")
    copies = []
    for far in range(2):
        for block in range(blocks):
            start = (jnp.bitwise_xor(half, far) * blocks + block) * cols
            copies.append(
                pltpu.make_async_copy(
                    source_ref.at[:, pl.ds(pl.multiple_of(start, 128), cols)],
                    held_ref.at[far, block * tokens : (block + 1) * tokens],
                    sems.at[far, block],
                )
            )
            copies[-1].start()
    chosen = spread_column(picks_ref[...].astype(F32), blocks).astype(jnp.int32)
    target = chosen + iota((rows, 1), 0) % (blocks * slots) // slots * tokens
    take = one_hot(target == iota((rows, blocks * tokens), 1))
    scale = spread_column(gates_ref[...], blocks)
    for far, out_ref in enumerate((own_ref, other_ref)):
        for block in range(blocks):
            copies[far * blocks + block].wait()
        out_ref[...] = (dot(take, held_ref[far]) * scale).astype(BF16)


def pair_rows(source, picks, gates, blocks, after):
    slots, experts = picks.shape
    tokens, width = source.shape
    cols = width // (2 * blocks)
    rows = experts * blocks * slots
    return pl.pallas_call(
        functools.partial(pair_kernel, blocks),
        in_specs=[pl.BlockSpec(memory_space=pl.ANY), vmem(), vmem(), hbm()],
        out_specs=[vmem()] * 2,
        out_shape=[shape_of(rows, cols)] * 2,
        scratch_shapes=[pltpu.VMEM((2, blocks * tokens, cols), BF16), pltpu.SemaphoreType.DMA((2, blocks))],
        compiler_params=params(16),
        cost_estimate=cost(4 * rows * cols * tokens * blocks, 2 * tokens * width),
        name="pair_rows",
    )(after, picks, gates, in_hbm(source))


def join_kernel(own_ref, other_ref, out_ref, sems):
    half = lax.axis_index("dp")
    copies = [
        pltpu.make_async_copy(own_ref, out_ref.at[:, half], sems.at[0]),
        pltpu.make_async_copy(other_ref, out_ref.at[:, 1 - half], sems.at[1]),
    ]
    for copy in copies:
        copy.start()
    for copy in copies:
        copy.wait()


def join_rows(own, other, experts):
    rows, cols = own.shape
    shape = (experts, rows // experts, cols)
    joined = pl.pallas_call(
        join_kernel,
        in_specs=[pl.BlockSpec(memory_space=pl.ANY)] * 2,
        out_specs=hbm(),
        out_shape=hbm_shape(experts, 2, *shape[1:]),
        scratch_shapes=[pltpu.SemaphoreType.DMA((2,))],
        compiler_params=params(16),
        cost_estimate=cost(0, 8 * rows * cols),
        name="join_rows",
    )(own.reshape(shape), other.reshape(shape))
    return joined.reshape(2 * rows, cols)


def send_rows(source, lists, halves, blocks):
    slots, experts = lists[0].shape
    tokens, width = source.shape
    cols = width // (halves * blocks)
    rows = halves * experts * blocks * slots
    return pl.pallas_call(
        functools.partial(send_kernel, halves, blocks, len(lists) == 2),
        in_specs=[hbm()] * (len(lists) + 1),
        out_specs=vmem(),
        out_shape=shape_of(rows, cols),
        scratch_shapes=[
            pltpu.VMEM((halves, blocks * tokens, cols), BF16),
            pltpu.SemaphoreType.DMA((halves, blocks)),
            pltpu.SemaphoreType.DMA((2,)),
        ]
        + [pltpu.VMEM((slots, experts), value.dtype) for value in lists],
        compiler_params=params(16),
        cost_estimate=cost(2 * rows * cols * tokens * blocks, 2 * tokens * width + 2 * rows * cols),
        name="send_rows",
    )(*[in_hbm(value) for value in lists], in_hbm(source))


def sort_matrix(rows, blocks, slots, back, place=lambda device: device):
    a = iota((rows, rows), 1 if back else 0)
    b = iota((rows, rows), 0 if back else 1)
    group = rows // blocks
    return one_hot(place(a % group // slots) * (blocks * slots) + a // group * slots + a % slots == b)


def sort_rows(messages_ref, rows_ref, slots, place=None):
    blocks, total = rows_ref.shape[:2]
    if blocks == 1 and place is None:
        rows_ref[0] = messages_ref[...]
        return
    size = min(blocks * total, 256)
    group = size // blocks
    order = sort_matrix(size, blocks, slots, False, place or (lambda device: device))
    for part in range(total // group):
        ordered = dot(order, messages_ref[part * size : (part + 1) * size]).astype(BF16)
        for block in range(blocks):
            rows_ref[block, part * group : (part + 1) * group] = ordered[block * group : (block + 1) * group]


def unsort_rows(made, out_ref, slots, span=slice(None)):
    blocks, total = len(made), made[0].shape[0]
    if blocks == 1:
        out_ref[:, span] = made[0]
        return
    size = min(blocks * total, 256)
    group = size // blocks
    order = sort_matrix(size, blocks, slots, True)
    for part in range(total // group):
        stacked = jnp.concatenate([value[part * group : (part + 1) * group] for value in made], axis=0)
        out_ref[part * size : (part + 1) * size, span] = dot(order, stacked).astype(BF16)


def spans(ref, blocks):
    cols = ref // blocks
    return [slice(block * cols, (block + 1) * cols) for block in range(blocks)]


def added(terms):
    return functools.reduce(jnp.add, terms)


def pieces_of(width):
    if width % 256 or width <= 768:
        return [(0, width)]
    first = width // 2 // 256 * 256
    return [(0, first), (first, width - first)]


def thirds_of(height):
    size = height // 3 if height % 384 == 0 else height
    return [(start, size) for start in range(0, height, size)]


class Stream:
    def __init__(self, sems):
        self.sems, self.copies = sems, []

    def start(self, source, target):
        copy = pltpu.make_async_copy(source, target, self.sems.at[len(self.copies)])
        copy.start()
        self.copies.append(copy)
        return copy


def in_sums_kernel(slots, sort, source_ref, weight_ref, out_ref, *refs):
    held_ref, acc_ref, sems = refs[-3:]
    part, hidden = weight_ref.shape[1:]
    stream = Stream(sems)
    if sort:
        rows_ref, kept_ref = refs[:2]
    else:
        rows_ref = source_ref
    blocks, _, cols = rows_ref.shape
    cuts = [(block, start, size) for block in range(blocks) for start, size in pieces_of(cols)]
    spots = [slice(block * cols + start, block * cols + start + size) for block, start, size in cuts]
    copies = [stream.start(weight_ref.at[0, spot], held_ref.at[spot]) for spot in spots]
    if sort:
        sort_rows(source_ref, rows_ref, slots)
        kept = stream.start(rows_ref, kept_ref)
    for number, (block, start, size) in enumerate(cuts):
        copies[number].wait()
        term = dot(rows_ref[block, :, start : start + size], held_ref[spots[number]])
        if number < len(cuts) - 1:
            acc_ref[...] = term if number == 0 else acc_ref[...] + term
        else:
            out_ref[...] = (term if number == 0 else acc_ref[...] + term).astype(BF16)
    if sort:
        kept.wait()


def in_sums(source, weight, blocks, slots):
    part, hidden = weight.shape[1:]
    cols = part // blocks
    sort = len(source.shape) == 2
    rows = source.shape[0] // blocks if sort else source.shape[1]
    more = [shape_of(blocks, rows, cols), hbm_shape(blocks, rows, cols)] if sort else []
    return pl.pallas_call(
        functools.partial(in_sums_kernel, slots, sort),
        in_specs=[vmem(), hbm()],
        out_specs=[vmem()] + ([vmem(), hbm()] if sort else []),
        out_shape=[shape_of(rows, hidden)] + more,
        scratch_shapes=[
            pltpu.VMEM((part, hidden), BF16),
            pltpu.VMEM((rows, hidden), F32),
            pltpu.SemaphoreType.DMA((blocks * len(pieces_of(cols)) + 1,)),
        ],
        compiler_params=params(),
        cost_estimate=cost(2 * rows * part * hidden, 2 * part * hidden),
        name="gate_sums" if sort else "up_sums",
    )(source, in_hbm(weight))


def back_sums_kernel(slots, place, messages_ref, down_ref, out_ref, kept_ref, rows_ref, held_ref, sems):
    blocks, _, cols = rows_ref.shape
    stream = Stream(sems)
    spots = [slice(start, start + size) for start, size in thirds_of(down_ref.shape[1])]
    copies = [stream.start(down_ref.at[0, spot], held_ref.at[spot]) for spot in spots]
    sort_rows(messages_ref, rows_ref, slots, place)
    kept = stream.start(rows_ref, kept_ref)
    for spot, copy in zip(spots, copies):
        copy.wait()
        terms = [
            dot(rows_ref[b], held_ref[spot, span], ((1,), (1,))) for b, span in enumerate(spans(blocks * cols, blocks))
        ]
        out_ref[:, spot] = added(terms).astype(BF16)
    kept.wait()


def back_sums(messages, w_down, blocks, slots, place):
    hidden, part = w_down.shape[1:]
    rows = messages.shape[0] // blocks
    cols = part // blocks
    return pl.pallas_call(
        functools.partial(back_sums_kernel, slots, place),
        in_specs=[vmem(), hbm()],
        out_specs=[vmem(), hbm()],
        out_shape=[shape_of(rows, hidden), hbm_shape(blocks, rows, cols)],
        scratch_shapes=[
            pltpu.VMEM((blocks, rows, cols), BF16),
            pltpu.VMEM((hidden, part), BF16),
            pltpu.SemaphoreType.DMA((len(thirds_of(hidden)) + 1,)),
        ],
        compiler_params=params(),
        cost_estimate=cost(2 * rows * part * hidden, 2 * part * hidden),
        name="back_sums",
    )(messages, in_hbm(w_down))


def bring_kernel(count, *refs):
    sources, targets, sems = refs[1 : count + 1], refs[count + 1 : 2 * count + 1], refs[-1]
    copies = [pltpu.make_async_copy(s, t, sems.at[i]) for i, (s, t) in enumerate(zip(sources, targets))]
    for copy in copies:
        copy.start()
    for copy in copies:
        copy.wait()


def bring(values, after):
    return pl.pallas_call(
        functools.partial(bring_kernel, len(values)),
        in_specs=[pl.BlockSpec(memory_space=pl.ANY)] + [hbm()] * len(values),
        out_specs=[vmem()] * len(values),
        out_shape=[shape_of(*value.shape) for value in values],
        scratch_shapes=[pltpu.SemaphoreType.DMA((len(values),))],
        compiler_params=params(16),
        cost_estimate=cost(0, 2 * sum(value.size for value in values)),
        name="bring_weights",
    )(after, *[in_hbm(value) for value in values])


def row_parts(total):
    size = min(total, 128)
    return [slice(start, start + size) for start in range(0, total, size)]


def summed(refs, rows):
    return added([ref[rows].astype(F32) for ref in refs])


def out_rows_kernel(slots, blocks, count, *refs):
    gates, ups, (down_ref, act_ref, out_ref) = refs[:count], refs[count : 2 * count], refs[2 * count :]
    part = down_ref.shape[2]
    for rows in row_parts(act_ref.shape[0]):
        gate_sum = summed(gates, rows)
        act_ref[rows] = (gate_sum * jax.nn.sigmoid(gate_sum) * summed(ups, rows)).astype(BF16)
    unsort_rows([dot(act_ref[...], down_ref[0, :, span]).astype(BF16) for span in spans(part, blocks)], out_ref, slots)


def out_rows(gates, ups, w_down, blocks, slots):
    hidden, part = w_down.shape[1:]
    rows = gates[0].shape[0]
    return pl.pallas_call(
        functools.partial(out_rows_kernel, slots, blocks, len(gates)),
        in_specs=[vmem()] * (2 * len(gates) + 1),
        out_specs=[vmem()] * 2,
        out_shape=[shape_of(rows, hidden), shape_of(blocks * rows, part // blocks)],
        compiler_params=params(),
        cost_estimate=cost(2 * rows * part * hidden, 2 * part * hidden),
        name="output_rows",
    )(*gates, *ups, w_down)


def grad_rows_kernel(slots, blocks, count, *refs):
    gates, ups, backs = refs[:count], refs[count : 2 * count], refs[2 * count : 3 * count]
    gate_ref, up_ref, kept_ref, out_ref, act_ref, sem = refs[3 * count :]
    part, hidden = gate_ref.shape[1:]
    cols = part // blocks
    for rows in row_parts(act_ref.shape[0]):
        gate_sum, up_sum, back_sum = summed(gates, rows), summed(ups, rows), summed(backs, rows)
        sig = jax.nn.sigmoid(gate_sum)
        act_ref[rows, :hidden] = (back_sum * up_sum * sig * (1.0 + gate_sum * (1.0 - sig))).astype(BF16)
        act_ref[rows, hidden:] = (back_sum * (gate_sum * sig)).astype(BF16)
    kept = pltpu.make_async_copy(act_ref, kept_ref, sem)
    kept.start()
    for start, size in pieces_of(cols):
        made = []
        for block in range(blocks):
            span = slice(block * cols + start, block * cols + start + size)
            total = dot(act_ref[:, :hidden], gate_ref[0, span, :], ((1,), (1,)))
            total = total + dot(act_ref[:, hidden:], up_ref[0, span, :], ((1,), (1,)))
            made.append(total.astype(BF16))
        unsort_rows(made, out_ref, slots, slice(start, start + size))
    kept.wait()


def grad_rows(gates, ups, backs, w_gate, w_up, blocks, slots):
    part, hidden = w_gate.shape[1:]
    rows = gates[0].shape[0]
    cols = part // blocks
    return pl.pallas_call(
        functools.partial(grad_rows_kernel, slots, blocks, len(gates)),
        in_specs=[vmem()] * (3 * len(gates) + 2),
        out_specs=[hbm(), vmem()],
        out_shape=[hbm_shape(rows, 2 * hidden), shape_of(blocks * rows, cols)],
        scratch_shapes=[pltpu.VMEM((rows, 2 * hidden), BF16), pltpu.SemaphoreType.DMA],
        compiler_params=params(32),
        cost_estimate=cost(4 * rows * part * hidden, 4 * part * hidden),
        name="gradient_rows",
    )(*gates, *ups, *backs, w_gate, w_up)


def weights_kernel(rows_in_ref, rows_up_ref, act_ref, grad_act_ref, gate_ref, up_ref, down_ref):
    hidden = gate_ref.shape[2]
    rows_in = rows_in_ref[0]
    gate_ref[0] = dot(rows_in, grad_act_ref[:, :hidden], ((0,), (0,))).astype(BF16)
    up_ref[0] = dot(rows_in, grad_act_ref[:, hidden:], ((0,), (0,))).astype(BF16)
    down_ref[0] = dot(act_ref[...], rows_up_ref[0], ((0,), (0,))).astype(BF16)


def weight_grads(rows_in, rows_up, act, grad_act):
    blocks, total, width = rows_in.shape
    part = blocks * width
    hidden = act.shape[1]
    cols = block_of(width, 640)
    steps = width // cols
    chunk = pl.BlockSpec((1, total, cols), lambda k, b: (k, 0, b))
    tall = pl.BlockSpec((1, cols, hidden), lambda k, b: (0, k * steps + b, 0))
    return pl.pallas_call(
        weights_kernel,
        grid=(blocks, steps),
        in_specs=[
            chunk,
            chunk,
            pl.BlockSpec((total, hidden), lambda k, b: (0, 0)),
            pl.BlockSpec((total, 2 * hidden), lambda k, b: (0, 0)),
        ],
        out_specs=[tall, tall, pl.BlockSpec((1, hidden, cols), lambda k, b: (0, 0, k * steps + b))],
        out_shape=[shape_of(1, part, hidden), shape_of(1, part, hidden), shape_of(1, hidden, part)],
        compiler_params=params(),
        cost_estimate=cost(6 * total * part * hidden, 6 * part * hidden),
        name="weight_grads",
    )(rows_in, rows_up, act, grad_act)


def back_rows(back_ref, half, halves, run):
    total = back_ref.shape[0]
    return jnp.concatenate([back_ref[start : start + run] for start in range(half * run, total, halves * run)], axis=0)


def put_columns(held_ref, target_ref, sems, half, block):
    blocks, _, cols = held_ref.shape[1:]
    place = half * blocks + block
    copy = pltpu.make_async_copy(
        held_ref.at[half, block], target_ref.at[:, place * cols : (place + 1) * cols], sems.at[half, block]
    )
    copy.start()
    return copy


def mixed_kernel(picks_ref, gates_ref, cot_ref, back_ref, mixed_ref, gate_grad_ref, put_ref, held_ref, sems):
    slots, experts = picks_ref.shape
    halves, blocks, tokens, cols = held_ref.shape
    rows = experts * blocks * slots
    hit = spread_row(picks_ref[...].astype(F32), blocks).astype(jnp.int32) == iota((tokens, rows), 0)
    scale = spread_row(gates_ref[...], blocks)
    of_block = iota((tokens, rows), 1) % (blocks * slots) // slots
    run = planes_of(experts) * blocks * slots
    backs = [back_rows(back_ref, half, halves, run) for half in range(halves)]
    copies = []
    products = None
    for block in range(blocks):
        inside = hit & (of_block == block)
        put_ref[block] = one_hot(inside)
        rest = jnp.where(inside, scale, 0.0)
        pieces = []
        for _ in range(3):
            pieces.append(rest.astype(BF16))
            rest = rest - pieces[-1].astype(F32)
        for half in range(halves):
            back = backs[half]
            held_ref[half, block] = added([dot(piece, back) for piece in pieces]).astype(BF16)
            copies.append(put_columns(held_ref, mixed_ref, sems, half, block))
            place = half * blocks + block
            product = dot(cot_ref[:, place * cols : (place + 1) * cols], back, ((1,), (1,)))
            product = jnp.where(inside, product, 0.0)
            products = product if products is None else products + product
    values = jnp.sum(products, axis=0, keepdims=True)
    mine = iota((slots, rows), 1) % slots == iota((slots, rows), 0)
    owner = (expert_at(iota((rows, experts), 0) // (blocks * slots), experts) == iota((rows, experts), 1)).astype(F32)
    gate_grad_ref[...] = exact_dot(jnp.where(mine, values, 0.0), owner)
    for copy in copies:
        copy.wait()


def mix_rows(back, cotangent, picks, gates, halves, blocks):
    slots, experts = picks.shape
    tokens, width = cotangent.shape
    cols = width // (halves * blocks)
    rows = experts * blocks * slots
    return pl.pallas_call(
        mixed_kernel,
        in_specs=[vmem()] * 4,
        out_specs=[hbm(), vmem(), vmem()],
        out_shape=[shape_of(tokens, width), shape_of(slots, experts, dtype=F32), shape_of(blocks, tokens, rows)],
        scratch_shapes=[pltpu.VMEM((halves, blocks, tokens, cols), BF16), pltpu.SemaphoreType.DMA((halves, blocks))],
        compiler_params=params(16),
        cost_estimate=cost(8 * rows * tokens * width, 4 * tokens * width),
        name="mixed_rows",
    )(picks, gates, cotangent, back)


def token_grad_kernel(run, put_ref, back_ref, grad_ref, held_ref, sems):
    halves, blocks = held_ref.shape[:2]
    copies = []
    for half in range(halves):
        back = back_rows(back_ref, half, halves, run)
        for block in range(blocks):
            held_ref[half, block] = dot(put_ref[block], back).astype(BF16)
            copies.append(put_columns(held_ref, grad_ref, sems, half, block))
    for copy in copies:
        copy.wait()


def token_grads(back, put, halves, run):
    blocks, tokens, rows = put.shape
    cols = back.shape[1]
    width = halves * blocks * cols
    return pl.pallas_call(
        functools.partial(token_grad_kernel, run),
        in_specs=[vmem()] * 2,
        out_specs=hbm(),
        out_shape=shape_of(tokens, width),
        scratch_shapes=[pltpu.VMEM((halves, blocks, tokens, cols), BF16), pltpu.SemaphoreType.DMA((halves, blocks))],
        compiler_params=params(16),
        cost_estimate=cost(2 * rows * tokens * width, 2 * tokens * width),
        name="token_grads",
    )(put, back)


def to_owners(halves, experts, messages):
    planes = planes_of(experts)
    order = [
        half * experts + plane * (experts // planes) + place
        for place in range(experts // planes)
        for half in range(halves)
        for plane in range(planes)
    ]
    return lax.all_to_all(
        messages, EVERYONE, split_axis=0, concat_axis=0, tiled=True, axis_index_groups=[order]
    )


def to_experts(experts, messages):
    order = [expert_at(place, experts) for place in range(experts)]
    return lax.all_to_all(messages, "expert", split_axis=0, concat_axis=0, tiled=True, axis_index_groups=[order])


def dp_shares(own, halves):
    shares = [own] + [
        lax.ppermute(own, "dp", [(i, (i + shift) % halves) for i in range(halves)]) for shift in range(1, halves)
    ]
    return shares if halves <= 2 else [added([share.astype(F32) for share in shares])]


def body(halves, tokens, cotangent, picks, gates, w_gate, w_up, w_down):
    experts, slots = picks.shape[1:]
    scatter = functools.partial(to_owners, halves, experts)
    blocks = 2 if tokens.shape[1] // halves % 256 == 0 else 1
    picks_t = picks[0].T
    gates_t = gates[0].T
    messages_in = send_rows(tokens, (picks_t,), halves, blocks)
    arrived_in = scatter(messages_in)
    if halves == 2:
        own, other = pair_rows(cotangent, picks_t, gates_t, blocks, messages_in)
        other = lax.ppermute(other, "dp", [(0, 1), (1, 0)])
        arrived_up = to_experts(experts, join_rows(own, other, experts))
        place = functools.partial(split_place, halves=halves, planes=planes_of(experts))
    else:
        arrived_up = scatter(send_rows(cotangent, (picks_t, gates_t), halves, blocks))
        place = None
    own_gate, near_rows, rows_in = in_sums(arrived_in, w_gate, blocks, slots)
    gates_sum = dp_shares(own_gate, halves)
    (own_up,) = in_sums(near_rows, w_up, blocks, slots)
    ups_sum = dp_shares(own_up, halves)
    act, outputs = out_rows(gates_sum, ups_sum, w_down, blocks, slots)
    back_out = scatter(outputs)
    own_back, rows_up = back_sums(arrived_up, w_down, blocks, slots, place)
    backs_sum = dp_shares(own_back, halves)
    near_gate, near_up = bring((w_gate, w_up), own_back)
    grad_act, gradients = grad_rows(gates_sum, ups_sum, backs_sum, near_gate, near_up, blocks, slots)
    back_grad = scatter(gradients)
    grad_gate_w, grad_up_w, grad_down = weight_grads(rows_in, rows_up, act, grad_act)
    mixed, gate_grad, put = mix_rows(back_out, cotangent, picks_t, gates_t, halves, blocks)
    token_grad = token_grads(back_grad, put, halves, planes_of(experts) * blocks * slots)
    return mixed, token_grad, gate_grad.T[None], grad_gate_w, grad_up_w, grad_down


def solution(mesh):
    rows = P(("dp", "expert"), None)
    lists = P(("dp", "expert"), None, None)
    tall = P("expert", "dp", None)
    wide = P("expert", None, "dp")
    return jax.shard_map(
        functools.partial(body, mesh.shape["dp"]),
        mesh=mesh,
        in_specs=(rows, rows, lists, lists, tall, tall, wide),
        out_specs=(rows, rows, lists, tall, tall, wide),
        check_vma=False,
    )
```

```python
import functools

import jax
import jax.numpy as jnp
from jax import lax
from jax.experimental import pallas as pl
from jax.experimental.pallas import tpu as pltpu
from jax.sharding import PartitionSpec as P

F32 = jnp.float32
BF16 = jnp.bfloat16
MIB = 1024 * 1024
EVERYONE = ("dp", "expert")


def dot(left, right, dims=((1,), (0,)), precision=None):
    return lax.dot_general(left, right, (dims, ((), ())), precision=precision, preferred_element_type=F32)


def exact_dot(left, right, dims=((1,), (0,))):
    return dot(left, right, dims, lax.Precision.HIGHEST)


def iota(shape, axis):
    return lax.broadcasted_iota(jnp.int32, shape, axis)


def planes_of(experts):
    return experts // 4 if experts % 4 == 0 else 1


def expert_at(place, experts):
    planes = planes_of(experts)
    return place % planes * (experts // planes) + place // planes


def split_place(place, halves, planes):
    return (place // (halves * planes) * planes + place % planes) * halves + place // planes % halves


def one_hot(condition):
    return jnp.where(condition, 1.0, 0.0).astype(BF16)


def vmem():
    return pl.BlockSpec(memory_space=pltpu.VMEM)


def hbm():
    return pl.BlockSpec(memory_space=pltpu.HBM)


def in_hbm(value):
    return pltpu.with_memory_space_constraint(value, pltpu.HBM)


def shape_of(*sizes, dtype=BF16):
    return jax.ShapeDtypeStruct(sizes, dtype)


def hbm_shape(*sizes):
    return pltpu.HBM(sizes, BF16)


def params(mib=24):
    return pltpu.CompilerParams(vmem_limit_bytes=mib * MIB)


def cost(flops, moved):
    return pl.CostEstimate(flops=flops, bytes_accessed=moved, transcendentals=0)


def block_of(width, limit):
    best = 128
    for size in range(128, limit + 1, 128):
        if width % size == 0:
            best = size
    return best


def spread_column(values, blocks):
    slots, experts = values.shape
    rows = experts * blocks * slots
    owner = (expert_at(iota((rows, experts), 0) // (blocks * slots), experts) == iota((rows, experts), 1)).astype(F32)
    wide = exact_dot(owner, values, ((1,), (1,)))
    mine = iota((rows, slots), 0) % slots == iota((rows, slots), 1)
    return jnp.sum(jnp.where(mine, wide, 0.0), axis=1, keepdims=True)


def spread_row(values, blocks):
    slots, experts = values.shape
    rows = experts * blocks * slots
    owner = (expert_at(iota((experts, rows), 1) // (blocks * slots), experts) == iota((experts, rows), 0)).astype(F32)
    wide = exact_dot(values, owner)
    mine = iota((slots, rows), 1) % slots == iota((slots, rows), 0)
    return jnp.sum(jnp.where(mine, wide, 0.0), axis=0, keepdims=True)


def send_kernel(halves, blocks, scaled, *refs):
    count = 2 if scaled else 1
    lists, source_ref, out_ref = refs[:count], refs[count], refs[count + 1]
    held_ref, sems, list_sems = refs[count + 2 : count + 5]
    list_refs = refs[count + 5 :]
    rows, cols = out_ref.shape
    rows = rows // halves
    tokens = source_ref.shape[0]
    list_copies = [
        pltpu.make_async_copy(ref, target, list_sems.at[i]) for i, (ref, target) in enumerate(zip(lists, list_refs))
    ]
    copies = []
    for copy in list_copies:
        copy.start()
    for half in range(halves):
        for block in range(blocks):
            place = half * blocks + block
            copies.append(
                pltpu.make_async_copy(
                    source_ref.at[:, place * cols : (place + 1) * cols],
                    held_ref.at[half, block * tokens : (block + 1) * tokens],
                    sems.at[half, block],
                )
            )
            copies[-1].start()
    for copy in list_copies:
        copy.wait()
    slots, experts = list_refs[0].shape
    run = planes_of(experts) * blocks * slots
    chosen = spread_column(list_refs[0][...].astype(F32), blocks).astype(jnp.int32)
    target = chosen + iota((rows, 1), 0) % (blocks * slots) // slots * tokens
    take = one_hot(target == iota((rows, blocks * tokens), 1))
    scale = spread_column(list_refs[1][...], blocks) if scaled else None
    for half in range(halves):
        for block in range(blocks):
            copies[half * blocks + block].wait()
        picked = dot(take, held_ref[half])
        if scaled:
            picked = picked * scale
        picked = picked.astype(BF16)
        for place in range(rows // run):
            start = (place * halves + half) * run
            out_ref[start : start + run] = picked[place * run : (place + 1) * run]


def send_rows(source, lists, halves, blocks):
    slots, experts = lists[0].shape
    tokens, width = source.shape
    cols = width // (halves * blocks)
    rows = halves * experts * blocks * slots
    return pl.pallas_call(
        functools.partial(send_kernel, halves, blocks, len(lists) == 2),
        in_specs=[hbm()] * (len(lists) + 1),
        out_specs=vmem(),
        out_shape=shape_of(rows, cols),
        scratch_shapes=[
            pltpu.VMEM((halves, blocks * tokens, cols), BF16),
            pltpu.SemaphoreType.DMA((halves, blocks)),
            pltpu.SemaphoreType.DMA((2,)),
        ]
        + [pltpu.VMEM((slots, experts), value.dtype) for value in lists],
        compiler_params=params(16),
        cost_estimate=cost(2 * rows * cols * tokens * blocks, 2 * tokens * width + 2 * rows * cols),
        name="send_rows",
    )(*[in_hbm(value) for value in lists], in_hbm(source))


def same_place(device):
    return device


def sort_matrix(rows, blocks, slots, back, place=same_place):
    a = iota((rows, rows), 1 if back else 0)
    b = iota((rows, rows), 0 if back else 1)
    group = rows // blocks
    return one_hot(place(a % group // slots) * (blocks * slots) + a // group * slots + a % slots == b)


def sort_rows(messages_ref, rows_ref, slots):
    blocks, total = rows_ref.shape[:2]
    if blocks == 1:
        rows_ref[0] = messages_ref[...]
        return
    size = min(blocks * total, 256)
    group = size // blocks
    order = sort_matrix(size, blocks, slots, False)
    for part in range(total // group):
        ordered = dot(order, messages_ref[part * size : (part + 1) * size]).astype(BF16)
        for block in range(blocks):
            rows_ref[block, part * group : (part + 1) * group] = ordered[block * group : (block + 1) * group]


def unsort_rows(made, out_ref, slots, span=slice(None), place=same_place):
    blocks, total = len(made), made[0].shape[0]
    if blocks == 1 and place is same_place:
        out_ref[:, span] = made[0]
        return
    size = min(blocks * total, 256)
    group = size // blocks
    order = sort_matrix(size, blocks, slots, True, place)
    for part in range(total // group):
        stacked = jnp.concatenate([value[part * group : (part + 1) * group] for value in made], axis=0)
        out_ref[part * size : (part + 1) * size, span] = dot(order, stacked).astype(BF16)


def spans(ref, blocks):
    cols = ref // blocks
    return [slice(block * cols, (block + 1) * cols) for block in range(blocks)]


def added(terms):
    return functools.reduce(jnp.add, terms)


def pieces_of(width):
    if width % 256 or width <= 768:
        return [(0, width)]
    first = width // 2 // 256 * 256
    return [(0, first), (first, width - first)]


def thirds_of(height):
    size = height // 3 if height % 384 == 0 else height
    return [(start, size) for start in range(0, height, size)]


class Stream:
    def __init__(self, sems):
        self.sems, self.copies = sems, []

    def start(self, source, target):
        copy = pltpu.make_async_copy(source, target, self.sems.at[len(self.copies)])
        copy.start()
        self.copies.append(copy)
        return copy


def in_sums_kernel(slots, messages_ref, gate_ref, up_ref, out_ref, kept_ref, rows_ref, held_ref, acc_ref, sems):
    blocks, _, cols = rows_ref.shape
    hidden = gate_ref.shape[2]
    stream = Stream(sems)
    cuts = [(block, start, size) for block in range(blocks) for start, size in pieces_of(cols)]
    copies = []
    for block, start, size in cuts:
        span = slice(block * cols + start, block * cols + start + size)
        copies += [stream.start(ref.at[0, span], held_ref.at[i, span]) for i, ref in enumerate((gate_ref, up_ref))]
    sort_rows(messages_ref, rows_ref, slots)
    kept = stream.start(rows_ref, kept_ref)
    for number, (block, start, size) in enumerate(cuts):
        span = slice(block * cols + start, block * cols + start + size)
        for i in range(2):
            copies[2 * number + i].wait()
            term = dot(rows_ref[block, :, start : start + size], held_ref[i, span])
            acc_ref[i] = term if number == 0 else acc_ref[i] + term
    for i in range(2):
        out_ref[:, i * hidden : (i + 1) * hidden] = acc_ref[i].astype(BF16)
    kept.wait()


def in_sums(messages, w_gate, w_up, blocks, slots):
    part, hidden = w_gate.shape[1:]
    rows = messages.shape[0] // blocks
    cols = part // blocks
    return pl.pallas_call(
        functools.partial(in_sums_kernel, slots),
        in_specs=[vmem(), hbm(), hbm()],
        out_specs=[vmem(), hbm()],
        out_shape=[shape_of(rows, 2 * hidden), hbm_shape(blocks, rows, cols)],
        scratch_shapes=[
            pltpu.VMEM((blocks, rows, cols), BF16),
            pltpu.VMEM((2, part, hidden), BF16),
            pltpu.VMEM((2, rows, hidden), F32),
            pltpu.SemaphoreType.DMA((2 * blocks * len(pieces_of(cols)) + 1,)),
        ],
        compiler_params=params(),
        cost_estimate=cost(4 * rows * part * hidden, 4 * part * hidden),
        name="gate_up_sums",
    )(messages, in_hbm(w_gate), in_hbm(w_up))


def back_sums_kernel(slots, messages_ref, down_ref, out_ref, kept_ref, rows_ref, held_ref, sems):
    blocks, _, cols = rows_ref.shape
    stream = Stream(sems)
    spots = [slice(start, start + size) for start, size in thirds_of(down_ref.shape[1])]
    copies = [stream.start(down_ref.at[0, spot], held_ref.at[spot]) for spot in spots]
    sort_rows(messages_ref, rows_ref, slots)
    kept = stream.start(rows_ref, kept_ref)
    for spot, copy in zip(spots, copies):
        copy.wait()
        terms = [
            dot(rows_ref[b], held_ref[spot, span], ((1,), (1,))) for b, span in enumerate(spans(blocks * cols, blocks))
        ]
        out_ref[:, spot] = added(terms).astype(BF16)
    kept.wait()


def back_sums(messages, w_down, blocks, slots):
    hidden, part = w_down.shape[1:]
    rows = messages.shape[0] // blocks
    cols = part // blocks
    return pl.pallas_call(
        functools.partial(back_sums_kernel, slots),
        in_specs=[vmem(), hbm()],
        out_specs=[vmem(), hbm()],
        out_shape=[shape_of(rows, hidden), hbm_shape(blocks, rows, cols)],
        scratch_shapes=[
            pltpu.VMEM((blocks, rows, cols), BF16),
            pltpu.VMEM((hidden, part), BF16),
            pltpu.SemaphoreType.DMA((len(thirds_of(hidden)) + 1,)),
        ],
        compiler_params=params(),
        cost_estimate=cost(2 * rows * part * hidden, 2 * part * hidden),
        name="back_sums",
    )(messages, in_hbm(w_down))


def bring_kernel(count, *refs):
    sources, targets, sems = refs[1 : count + 1], refs[count + 1 : 2 * count + 1], refs[-1]
    copies = [pltpu.make_async_copy(s, t, sems.at[i]) for i, (s, t) in enumerate(zip(sources, targets))]
    for copy in copies:
        copy.start()
    for copy in copies:
        copy.wait()


def bring(values, after):
    return pl.pallas_call(
        functools.partial(bring_kernel, len(values)),
        in_specs=[pl.BlockSpec(memory_space=pl.ANY)] + [hbm()] * len(values),
        out_specs=[vmem()] * len(values),
        out_shape=[shape_of(*value.shape) for value in values],
        scratch_shapes=[pltpu.SemaphoreType.DMA((len(values),))],
        compiler_params=params(16),
        cost_estimate=cost(0, 2 * sum(value.size for value in values)),
        name="bring_weights",
    )(after, *[in_hbm(value) for value in values])


def row_parts(total):
    size = min(total, 128)
    return [slice(start, start + size) for start in range(0, total, size)]


def summed(refs, rows, span):
    return added([ref[rows, span].astype(F32) for ref in refs])


def out_rows_kernel(slots, blocks, place, count, *refs):
    shares, (down_ref, act_ref, out_ref) = refs[:count], refs[count:]
    hidden, part = down_ref.shape[1:]
    for rows in row_parts(act_ref.shape[0]):
        gate_sum = summed(shares, rows, slice(0, hidden))
        up_sum = summed(shares, rows, slice(hidden, 2 * hidden))
        act_ref[rows] = (gate_sum * jax.nn.sigmoid(gate_sum) * up_sum).astype(BF16)
    made = [dot(act_ref[...], down_ref[0, :, span]).astype(BF16) for span in spans(part, blocks)]
    unsort_rows(made, out_ref, slots, place=place)


def out_rows(shares, w_down, blocks, slots, place):
    hidden, part = w_down.shape[1:]
    rows = shares[0].shape[0]
    return pl.pallas_call(
        functools.partial(out_rows_kernel, slots, blocks, place, len(shares)),
        in_specs=[vmem()] * (len(shares) + 1),
        out_specs=[vmem()] * 2,
        out_shape=[shape_of(rows, hidden), shape_of(blocks * rows, part // blocks)],
        compiler_params=params(),
        cost_estimate=cost(2 * rows * part * hidden, 2 * part * hidden),
        name="output_rows",
    )(*shares, w_down)


def grad_rows_kernel(slots, blocks, count, *refs):
    shares, backs = refs[:count], refs[count : 2 * count]
    gate_ref, up_ref, kept_ref, out_ref, act_ref, sem = refs[2 * count :]
    part, hidden = gate_ref.shape[1:]
    cols = part // blocks
    for rows in row_parts(act_ref.shape[0]):
        gate_sum = summed(shares, rows, slice(0, hidden))
        up_sum = summed(shares, rows, slice(hidden, 2 * hidden))
        back_sum = summed(backs, rows, slice(0, hidden))
        sig = jax.nn.sigmoid(gate_sum)
        act_ref[rows, :hidden] = (back_sum * up_sum * sig * (1.0 + gate_sum * (1.0 - sig))).astype(BF16)
        act_ref[rows, hidden:] = (back_sum * (gate_sum * sig)).astype(BF16)
    kept = pltpu.make_async_copy(act_ref, kept_ref, sem)
    kept.start()
    for start, size in pieces_of(cols):
        made = []
        for block in range(blocks):
            span = slice(block * cols + start, block * cols + start + size)
            total = dot(act_ref[:, :hidden], gate_ref[0, span, :], ((1,), (1,)))
            total = total + dot(act_ref[:, hidden:], up_ref[0, span, :], ((1,), (1,)))
            made.append(total.astype(BF16))
        unsort_rows(made, out_ref, slots, slice(start, start + size))
    kept.wait()


def grad_rows(shares, backs, w_gate, w_up, blocks, slots):
    part, hidden = w_gate.shape[1:]
    rows = shares[0].shape[0]
    cols = part // blocks
    return pl.pallas_call(
        functools.partial(grad_rows_kernel, slots, blocks, len(shares)),
        in_specs=[vmem()] * (2 * len(shares) + 2),
        out_specs=[hbm(), vmem()],
        out_shape=[hbm_shape(rows, 2 * hidden), shape_of(blocks * rows, cols)],
        scratch_shapes=[pltpu.VMEM((rows, 2 * hidden), BF16), pltpu.SemaphoreType.DMA],
        compiler_params=params(32),
        cost_estimate=cost(4 * rows * part * hidden, 4 * part * hidden),
        name="gradient_rows",
    )(*shares, *backs, w_gate, w_up)


def weights_kernel(rows_in_ref, rows_up_ref, act_ref, grad_act_ref, gate_ref, up_ref, down_ref):
    hidden = gate_ref.shape[2]
    rows_in = rows_in_ref[0]
    gate_ref[0] = dot(rows_in, grad_act_ref[:, :hidden], ((0,), (0,))).astype(BF16)
    up_ref[0] = dot(rows_in, grad_act_ref[:, hidden:], ((0,), (0,))).astype(BF16)
    down_ref[0] = dot(act_ref[...], rows_up_ref[0], ((0,), (0,))).astype(BF16)


def weight_grads(rows_in, rows_up, act, grad_act):
    blocks, total, width = rows_in.shape
    part = blocks * width
    hidden = act.shape[1]
    cols = block_of(width, 640)
    steps = width // cols
    chunk = pl.BlockSpec((1, total, cols), lambda k, b: (k, 0, b))
    tall = pl.BlockSpec((1, cols, hidden), lambda k, b: (0, k * steps + b, 0))
    return pl.pallas_call(
        weights_kernel,
        grid=(blocks, steps),
        in_specs=[
            chunk,
            chunk,
            pl.BlockSpec((total, hidden), lambda k, b: (0, 0)),
            pl.BlockSpec((total, 2 * hidden), lambda k, b: (0, 0)),
        ],
        out_specs=[tall, tall, pl.BlockSpec((1, hidden, cols), lambda k, b: (0, 0, k * steps + b))],
        out_shape=[shape_of(1, part, hidden), shape_of(1, part, hidden), shape_of(1, hidden, part)],
        compiler_params=params(),
        cost_estimate=cost(6 * total * part * hidden, 6 * part * hidden),
        name="weight_grads",
    )(rows_in, rows_up, act, grad_act)


def back_rows(back_ref, half, halves, run):
    total = back_ref.shape[0]
    return jnp.concatenate([back_ref[start : start + run] for start in range(half * run, total, halves * run)], axis=0)


def put_columns(held_ref, target_ref, sems, half, block, start=None):
    blocks, _, cols = held_ref.shape[1:]
    start = (half * blocks + block) * cols if start is None else start
    copy = pltpu.make_async_copy(held_ref.at[half, block], target_ref.at[:, pl.ds(start, cols)], sems.at[half, block])
    copy.start()
    return copy


def mixed_kernel(crossed, picks_ref, gates_ref, cot_ref, *refs):
    back_refs, (mixed_ref, gate_grad_ref, put_ref, held_ref, sems) = refs[:-5], refs[-5:]
    slots, experts = picks_ref.shape
    halves, blocks, tokens, cols = held_ref.shape
    rows = experts * blocks * slots
    hit = spread_row(picks_ref[...].astype(F32), blocks).astype(jnp.int32) == iota((tokens, rows), 0)
    scale = spread_row(gates_ref[...], blocks)
    of_block = iota((tokens, rows), 1) % (blocks * slots) // slots
    if crossed:
        backs = [ref[...] for ref in back_refs]
        own = lax.axis_index("dp")
        places = [own, 1 - own]
    else:
        run = planes_of(experts) * blocks * slots
        backs = [back_rows(back_refs[0], half, halves, run) for half in range(halves)]
        places = list(range(halves))
    copies = []
    products = None
    for block in range(blocks):
        inside = hit & (of_block == block)
        put_ref[block] = one_hot(inside)
        rest = jnp.where(inside, scale, 0.0)
        pieces = []
        for _ in range(3):
            pieces.append(rest.astype(BF16))
            rest = rest - pieces[-1].astype(F32)
        for half in range(halves):
            back = backs[half]
            start = pl.multiple_of((places[half] * blocks + block) * cols, 128)
            held_ref[half, block] = added([dot(piece, back) for piece in pieces]).astype(BF16)
            copies.append(put_columns(held_ref, mixed_ref, sems, half, block, start))
            product = dot(cot_ref[:, pl.ds(start, cols)], back, ((1,), (1,)))
            product = jnp.where(inside, product, 0.0)
            products = product if products is None else products + product
    values = jnp.sum(products, axis=0, keepdims=True)
    mine = iota((slots, rows), 1) % slots == iota((slots, rows), 0)
    owner = (expert_at(iota((rows, experts), 0) // (blocks * slots), experts) == iota((rows, experts), 1)).astype(F32)
    gate_grad_ref[...] = exact_dot(jnp.where(mine, values, 0.0), owner)
    for copy in copies:
        copy.wait()


def mix_rows(backs, cotangent, picks, gates, halves, blocks):
    slots, experts = picks.shape
    tokens, width = cotangent.shape
    cols = width // (halves * blocks)
    rows = experts * blocks * slots
    return pl.pallas_call(
        functools.partial(mixed_kernel, len(backs) == 2),
        in_specs=[vmem()] * (3 + len(backs)),
        out_specs=[hbm(), vmem(), vmem()],
        out_shape=[shape_of(tokens, width), shape_of(slots, experts, dtype=F32), shape_of(blocks, tokens, rows)],
        scratch_shapes=[pltpu.VMEM((halves, blocks, tokens, cols), BF16), pltpu.SemaphoreType.DMA((halves, blocks))],
        compiler_params=params(16),
        cost_estimate=cost(8 * rows * tokens * width, 4 * tokens * width),
        name="mixed_rows",
    )(picks, gates, cotangent, *backs)


def part_kernel(joined_ref, own_ref, other_ref, sems):
    half = lax.axis_index("dp")
    copies = [
        pltpu.make_async_copy(joined_ref.at[:, half], own_ref, sems.at[0]),
        pltpu.make_async_copy(joined_ref.at[:, 1 - half], other_ref, sems.at[1]),
    ]
    for copy in copies:
        copy.start()
    for copy in copies:
        copy.wait()


def part_rows(joined, experts):
    rows, cols = joined.shape
    shape = (experts, rows // (2 * experts), cols)
    parted = pl.pallas_call(
        part_kernel,
        in_specs=[pl.BlockSpec(memory_space=pl.ANY)],
        out_specs=[pl.BlockSpec(memory_space=pl.ANY)] * 2,
        out_shape=[shape_of(*shape)] * 2,
        scratch_shapes=[pltpu.SemaphoreType.DMA((2,))],
        compiler_params=params(16),
        cost_estimate=cost(0, 4 * rows * cols),
        name="part_rows",
    )(joined.reshape(experts, 2, *shape[1:]))
    return [value.reshape(rows // 2, cols) for value in parted]


def token_grad_kernel(run, put_ref, back_ref, grad_ref, held_ref, sems):
    halves, blocks = held_ref.shape[:2]
    copies = []
    for half in range(halves):
        back = back_rows(back_ref, half, halves, run)
        for block in range(blocks):
            held_ref[half, block] = dot(put_ref[block], back).astype(BF16)
            copies.append(put_columns(held_ref, grad_ref, sems, half, block))
    for copy in copies:
        copy.wait()


def token_grads(back, put, halves, run):
    blocks, tokens, rows = put.shape
    cols = back.shape[1]
    width = halves * blocks * cols
    return pl.pallas_call(
        functools.partial(token_grad_kernel, run),
        in_specs=[vmem()] * 2,
        out_specs=hbm(),
        out_shape=shape_of(tokens, width),
        scratch_shapes=[pltpu.VMEM((halves, blocks, tokens, cols), BF16), pltpu.SemaphoreType.DMA((halves, blocks))],
        compiler_params=params(16),
        cost_estimate=cost(2 * rows * tokens * width, 2 * tokens * width),
        name="token_grads",
    )(put, back)


def to_owners(halves, experts, messages):
    planes = planes_of(experts)
    order = [
        half * experts + plane * (experts // planes) + place
        for place in range(experts // planes)
        for half in range(halves)
        for plane in range(planes)
    ]
    return lax.all_to_all(
        messages, EVERYONE, split_axis=0, concat_axis=0, tiled=True, axis_index_groups=[order]
    )


def to_experts(experts, messages):
    order = [expert_at(place, experts) for place in range(experts)]
    return lax.all_to_all(messages, "expert", split_axis=0, concat_axis=0, tiled=True, axis_index_groups=[order])


def dp_shares(own, halves):
    shares = [own] + [
        lax.ppermute(own, "dp", [(i, (i + shift) % halves) for i in range(halves)]) for shift in range(1, halves)
    ]
    return shares if halves <= 2 else [added([share.astype(F32) for share in shares])]


def body(halves, tokens, cotangent, picks, gates, w_gate, w_up, w_down):
    experts, slots = picks.shape[1:]
    scatter = functools.partial(to_owners, halves, experts)
    blocks = 2 if tokens.shape[1] // halves % 256 == 0 else 1
    picks_t = picks[0].T
    gates_t = gates[0].T
    arrived_in = scatter(send_rows(tokens, (picks_t,), halves, blocks))
    arrived_up = scatter(send_rows(cotangent, (picks_t, gates_t), halves, blocks))
    own_sums, rows_in = in_sums(arrived_in, w_gate, w_up, blocks, slots)
    shares = dp_shares(own_sums, halves)
    place = functools.partial(split_place, halves=2, planes=planes_of(experts)) if halves == 2 else same_place
    act, outputs = out_rows(shares, w_down, blocks, slots, place)
    back_out = to_experts(experts, outputs) if halves == 2 else scatter(outputs)
    own_back, rows_up = back_sums(arrived_up, w_down, blocks, slots)
    backs = dp_shares(own_back, halves)
    near_gate, near_up = bring((w_gate, w_up), own_back)
    grad_act, gradients = grad_rows(shares, backs, near_gate, near_up, blocks, slots)
    back_grad = scatter(gradients)
    grad_gate_w, grad_up_w, grad_down = weight_grads(rows_in, rows_up, act, grad_act)
    returned = [back_out]
    if halves == 2:
        own_out, other_out = part_rows(back_out, experts)
        returned = [own_out, lax.ppermute(other_out, "dp", [(0, 1), (1, 0)])]
    mixed, gate_grad, put = mix_rows(returned, cotangent, picks_t, gates_t, halves, blocks)
    token_grad = token_grads(back_grad, put, halves, planes_of(experts) * blocks * slots)
    return mixed, token_grad, gate_grad.T[None], grad_gate_w, grad_up_w, grad_down


def solution(mesh):
    rows = P(("dp", "expert"), None)
    lists = P(("dp", "expert"), None, None)
    tall = P("expert", "dp", None)
    wide = P("expert", None, "dp")
    return jax.shard_map(
        functools.partial(body, mesh.shape["dp"]),
        mesh=mesh,
        in_specs=(rows, rows, lists, lists, tall, tall, wide),
        out_specs=(rows, rows, lists, tall, tall, wide),
        check_vma=False,
    )
```

```python
import functools

import jax
import jax.numpy as jnp
from jax import lax
from jax.experimental import pallas as pl
from jax.experimental.pallas import tpu as pltpu
from jax.sharding import PartitionSpec as P

F32 = jnp.float32
BF16 = jnp.bfloat16
MIB = 1024 * 1024
EVERYONE = ("dp", "expert")


def dot(left, right, dims=((1,), (0,)), precision=None):
    return lax.dot_general(left, right, (dims, ((), ())), precision=precision, preferred_element_type=F32)


def exact_dot(left, right, dims=((1,), (0,))):
    return dot(left, right, dims, lax.Precision.HIGHEST)


def iota(shape, axis):
    return lax.broadcasted_iota(jnp.int32, shape, axis)


def planes_of(experts):
    return experts // 4 if experts % 4 == 0 else 1


def expert_at(place, experts):
    planes = planes_of(experts)
    return place % planes * (experts // planes) + place // planes


def split_place(place, halves, planes):
    return (place // (halves * planes) * planes + place % planes) * halves + place // planes % halves


def one_hot(condition):
    return jnp.where(condition, 1.0, 0.0).astype(BF16)


def vmem():
    return pl.BlockSpec(memory_space=pltpu.VMEM)


def hbm():
    return pl.BlockSpec(memory_space=pltpu.HBM)


def in_hbm(value):
    return pltpu.with_memory_space_constraint(value, pltpu.HBM)


def shape_of(*sizes, dtype=BF16):
    return jax.ShapeDtypeStruct(sizes, dtype)


def hbm_shape(*sizes):
    return pltpu.HBM(sizes, BF16)


def params(mib=24):
    return pltpu.CompilerParams(vmem_limit_bytes=mib * MIB)


def cost(flops, moved):
    return pl.CostEstimate(flops=flops, bytes_accessed=moved, transcendentals=0)


def block_of(width, limit):
    best = 128
    for size in range(128, limit + 1, 128):
        if width % size == 0:
            best = size
    return best


def spread_column(values, blocks):
    slots, experts = values.shape
    rows = experts * blocks * slots
    owner = (expert_at(iota((rows, experts), 0) // (blocks * slots), experts) == iota((rows, experts), 1)).astype(F32)
    wide = exact_dot(owner, values, ((1,), (1,)))
    mine = iota((rows, slots), 0) % slots == iota((rows, slots), 1)
    return jnp.sum(jnp.where(mine, wide, 0.0), axis=1, keepdims=True)


def spread_row(values, blocks):
    slots, experts = values.shape
    rows = experts * blocks * slots
    owner = (expert_at(iota((experts, rows), 1) // (blocks * slots), experts) == iota((experts, rows), 0)).astype(F32)
    wide = exact_dot(values, owner)
    mine = iota((slots, rows), 1) % slots == iota((slots, rows), 0)
    return jnp.sum(jnp.where(mine, wide, 0.0), axis=0, keepdims=True)


def send_kernel(halves, blocks, scaled, *refs):
    count = 2 if scaled else 1
    lists, source_ref, out_ref = refs[:count], refs[count], refs[count + 1]
    held_ref, made_ref, sems, list_sems, out_sems = refs[count + 2 : count + 7]
    list_refs = refs[count + 7 :]
    rows, cols = out_ref.shape
    rows = rows // halves
    tokens = source_ref.shape[0]
    list_copies = [
        pltpu.make_async_copy(ref, target, list_sems.at[i]) for i, (ref, target) in enumerate(zip(lists, list_refs))
    ]
    copies = []
    for copy in list_copies:
        copy.start()
    for half in range(halves):
        for block in range(blocks):
            place = half * blocks + block
            copies.append(
                pltpu.make_async_copy(
                    source_ref.at[:, place * cols : (place + 1) * cols],
                    held_ref.at[half, block * tokens : (block + 1) * tokens],
                    sems.at[half, block],
                )
            )
            copies[-1].start()
    for copy in list_copies:
        copy.wait()
    slots, experts = list_refs[0].shape
    run = planes_of(experts) * blocks * slots
    chosen = spread_column(list_refs[0][...].astype(F32), blocks).astype(jnp.int32)
    target = chosen + iota((rows, 1), 0) % (blocks * slots) // slots * tokens
    take = one_hot(target == iota((rows, blocks * tokens), 1))
    scale = spread_column(list_refs[1][...], blocks) if scaled else None
    out_copies = []
    for half in range(halves):
        for block in range(blocks):
            copies[half * blocks + block].wait()
        picked = dot(take, held_ref[half])
        if scaled:
            picked = picked * scale
        picked = picked.astype(BF16)
        for place in range(rows // run):
            start = (place * halves + half) * run
            made_ref[start : start + run] = picked[place * run : (place + 1) * run]
            out_copies.append(
                pltpu.make_async_copy(
                    made_ref.at[start : start + run], out_ref.at[start : start + run], out_sems.at[half, place]
                )
            )
            out_copies[-1].start()
    for copy in out_copies:
        copy.wait()


def pair_kernel(blocks, _, picks_ref, gates_ref, source_ref, own_ref, other_ref, held_ref, sems, list_sems, *list_refs):
    slots = picks_ref.shape[0]
    tokens = source_ref.shape[0]
    rows, cols = own_ref.shape
    half = lax.axis_index("dp")
    list_copies = [
        pltpu.make_async_copy(ref, target, list_sems.at[i])
        for i, (ref, target) in enumerate(zip((picks_ref, gates_ref), list_refs))
    ]
    for copy in list_copies:
        copy.start()
    copies = []
    for far in range(2):
        for block in range(blocks):
            start = (jnp.bitwise_xor(half, far) * blocks + block) * cols
            copies.append(
                pltpu.make_async_copy(
                    source_ref.at[:, pl.ds(pl.multiple_of(start, 128), cols)],
                    held_ref.at[far, block * tokens : (block + 1) * tokens],
                    sems.at[far, block],
                )
            )
            copies[-1].start()
    for copy in list_copies:
        copy.wait()
    chosen = spread_column(list_refs[0][...].astype(F32), blocks).astype(jnp.int32)
    target = chosen + iota((rows, 1), 0) % (blocks * slots) // slots * tokens
    take = one_hot(target == iota((rows, blocks * tokens), 1))
    scale = spread_column(list_refs[1][...], blocks)
    for far, out_ref in enumerate((own_ref, other_ref)):
        for block in range(blocks):
            copies[far * blocks + block].wait()
        out_ref[...] = (dot(take, held_ref[far]) * scale).astype(BF16)


def pair_rows(source, picks, gates, blocks, after):
    slots, experts = picks.shape
    tokens, width = source.shape
    cols = width // (2 * blocks)
    rows = experts * blocks * slots
    return pl.pallas_call(
        functools.partial(pair_kernel, blocks),
        in_specs=[hbm()] * 4,
        out_specs=[vmem()] * 2,
        out_shape=[shape_of(rows, cols)] * 2,
        scratch_shapes=[
            pltpu.VMEM((2, blocks * tokens, cols), BF16),
            pltpu.SemaphoreType.DMA((2, blocks)),
            pltpu.SemaphoreType.DMA((2,)),
            pltpu.VMEM((slots, experts), picks.dtype),
            pltpu.VMEM((slots, experts), gates.dtype),
        ],
        compiler_params=params(16),
        cost_estimate=cost(4 * rows * cols * tokens * blocks, 2 * tokens * width),
        name="pair_rows",
    )(in_hbm(after), in_hbm(picks), in_hbm(gates), in_hbm(source))


def join_kernel(own_ref, other_ref, out_ref, sems):
    half = lax.axis_index("dp")
    copies = [
        pltpu.make_async_copy(own_ref, out_ref.at[:, half], sems.at[0]),
        pltpu.make_async_copy(other_ref, out_ref.at[:, 1 - half], sems.at[1]),
    ]
    for copy in copies:
        copy.start()
    for copy in copies:
        copy.wait()


def join_rows(own, other, experts):
    rows, cols = own.shape
    shape = (experts, rows // experts, cols)
    joined = pl.pallas_call(
        join_kernel,
        in_specs=[pl.BlockSpec(memory_space=pl.ANY)] * 2,
        out_specs=hbm(),
        out_shape=hbm_shape(experts, 2, *shape[1:]),
        scratch_shapes=[pltpu.SemaphoreType.DMA((2,))],
        compiler_params=params(16),
        cost_estimate=cost(0, 8 * rows * cols),
        name="join_rows",
    )(own.reshape(shape), other.reshape(shape))
    return joined.reshape(2 * rows, cols)


def send_rows(source, lists, halves, blocks):
    slots, experts = lists[0].shape
    tokens, width = source.shape
    cols = width // (halves * blocks)
    rows = halves * experts * blocks * slots
    return pl.pallas_call(
        functools.partial(send_kernel, halves, blocks, len(lists) == 2),
        in_specs=[hbm()] * (len(lists) + 1),
        out_specs=hbm(),
        out_shape=hbm_shape(rows, cols),
        scratch_shapes=[
            pltpu.VMEM((halves, blocks * tokens, cols), BF16),
            pltpu.VMEM((rows, cols), BF16),
            pltpu.SemaphoreType.DMA((halves, blocks)),
            pltpu.SemaphoreType.DMA((2,)),
            pltpu.SemaphoreType.DMA((halves, experts // planes_of(experts))),
        ]
        + [pltpu.VMEM((slots, experts), value.dtype) for value in lists],
        compiler_params=params(16),
        cost_estimate=cost(2 * rows * cols * tokens * blocks, 2 * tokens * width + 2 * rows * cols),
        name="send_rows",
    )(*[in_hbm(value) for value in lists], in_hbm(source))


def same_place(device):
    return device


def sort_matrix(rows, blocks, slots, back, place=same_place):
    a = iota((rows, rows), 1 if back else 0)
    b = iota((rows, rows), 0 if back else 1)
    group = rows // blocks
    return one_hot(place(a % group // slots) * (blocks * slots) + a // group * slots + a % slots == b)


def sort_rows(messages_ref, rows_ref, slots, place=same_place):
    blocks, total = rows_ref.shape[:2]
    if blocks == 1 and place is same_place:
        rows_ref[0] = messages_ref[...]
        return
    size = min(blocks * total, 256)
    group = size // blocks
    order = sort_matrix(size, blocks, slots, False, place)
    for part in range(total // group):
        ordered = dot(order, messages_ref[part * size : (part + 1) * size]).astype(BF16)
        for block in range(blocks):
            rows_ref[block, part * group : (part + 1) * group] = ordered[block * group : (block + 1) * group]


def unsort_rows(made, out_ref, slots, span=slice(None), place=same_place):
    blocks, total = len(made), made[0].shape[0]
    if blocks == 1 and place is same_place:
        out_ref[:, span] = made[0]
        return
    size = min(blocks * total, 256)
    group = size // blocks
    order = sort_matrix(size, blocks, slots, True, place)
    for part in range(total // group):
        stacked = jnp.concatenate([value[part * group : (part + 1) * group] for value in made], axis=0)
        out_ref[part * size : (part + 1) * size, span] = dot(order, stacked).astype(BF16)


def spans(ref, blocks):
    cols = ref // blocks
    return [slice(block * cols, (block + 1) * cols) for block in range(blocks)]


def added(terms):
    return functools.reduce(jnp.add, terms)


def pieces_of(width):
    if width % 256 or width <= 768:
        return [(0, width)]
    first = width // 2 // 256 * 256
    return [(0, first), (first, width - first)]


def thirds_of(height):
    size = height // 3 if height % 384 == 0 else height
    return [(start, size) for start in range(0, height, size)]


class Stream:
    def __init__(self, sems):
        self.sems, self.copies = sems, []

    def start(self, source, target):
        copy = pltpu.make_async_copy(source, target, self.sems.at[len(self.copies)])
        copy.start()
        self.copies.append(copy)
        return copy


def in_sums_kernel(slots, messages_ref, gate_ref, up_ref, out_ref, kept_ref, rows_ref, held_ref, acc_ref, sems):
    blocks, _, cols = rows_ref.shape
    hidden = gate_ref.shape[2]
    stream = Stream(sems)
    cuts = [(block, start, size) for block in range(blocks) for start, size in pieces_of(cols)]
    copies = []
    for block, start, size in cuts:
        span = slice(block * cols + start, block * cols + start + size)
        copies += [stream.start(ref.at[0, span], held_ref.at[i, span]) for i, ref in enumerate((gate_ref, up_ref))]
    sort_rows(messages_ref, rows_ref, slots)
    kept = stream.start(rows_ref, kept_ref)
    for number, (block, start, size) in enumerate(cuts):
        span = slice(block * cols + start, block * cols + start + size)
        for i in range(2):
            copies[2 * number + i].wait()
            term = dot(rows_ref[block, :, start : start + size], held_ref[i, span])
            acc_ref[i] = term if number == 0 else acc_ref[i] + term
    for i in range(2):
        out_ref[:, i * hidden : (i + 1) * hidden] = acc_ref[i].astype(BF16)
    kept.wait()


def in_sums(messages, w_gate, w_up, blocks, slots):
    part, hidden = w_gate.shape[1:]
    rows = messages.shape[0] // blocks
    cols = part // blocks
    return pl.pallas_call(
        functools.partial(in_sums_kernel, slots),
        in_specs=[vmem(), hbm(), hbm()],
        out_specs=[vmem(), hbm()],
        out_shape=[shape_of(rows, 2 * hidden), hbm_shape(blocks, rows, cols)],
        scratch_shapes=[
            pltpu.VMEM((blocks, rows, cols), BF16),
            pltpu.VMEM((2, part, hidden), BF16),
            pltpu.VMEM((2, rows, hidden), F32),
            pltpu.SemaphoreType.DMA((2 * blocks * len(pieces_of(cols)) + 1,)),
        ],
        compiler_params=params(),
        cost_estimate=cost(4 * rows * part * hidden, 4 * part * hidden),
        name="gate_up_sums",
    )(messages, in_hbm(w_gate), in_hbm(w_up))


def back_sums_kernel(slots, place, messages_ref, down_ref, out_ref, kept_ref, rows_ref, held_ref, sems):
    blocks, _, cols = rows_ref.shape
    stream = Stream(sems)
    spots = [slice(start, start + size) for start, size in thirds_of(down_ref.shape[1])]
    copies = [stream.start(down_ref.at[0, spot], held_ref.at[spot]) for spot in spots]
    sort_rows(messages_ref, rows_ref, slots, place)
    kept = stream.start(rows_ref, kept_ref)
    for spot, copy in zip(spots, copies):
        copy.wait()
        terms = [
            dot(rows_ref[b], held_ref[spot, span], ((1,), (1,))) for b, span in enumerate(spans(blocks * cols, blocks))
        ]
        out_ref[:, spot] = added(terms).astype(BF16)
    kept.wait()


def back_sums(messages, w_down, blocks, slots, place):
    hidden, part = w_down.shape[1:]
    rows = messages.shape[0] // blocks
    cols = part // blocks
    return pl.pallas_call(
        functools.partial(back_sums_kernel, slots, place),
        in_specs=[vmem(), hbm()],
        out_specs=[vmem(), hbm()],
        out_shape=[shape_of(rows, hidden), hbm_shape(blocks, rows, cols)],
        scratch_shapes=[
            pltpu.VMEM((blocks, rows, cols), BF16),
            pltpu.VMEM((hidden, part), BF16),
            pltpu.SemaphoreType.DMA((len(thirds_of(hidden)) + 1,)),
        ],
        compiler_params=params(),
        cost_estimate=cost(2 * rows * part * hidden, 2 * part * hidden),
        name="back_sums",
    )(messages, in_hbm(w_down))


def bring_kernel(count, *refs):
    sources, targets, sems = refs[1 : count + 1], refs[count + 1 : 2 * count + 1], refs[-1]
    copies = [pltpu.make_async_copy(s, t, sems.at[i]) for i, (s, t) in enumerate(zip(sources, targets))]
    for copy in copies:
        copy.start()
    for copy in copies:
        copy.wait()


def bring(values, after):
    return pl.pallas_call(
        functools.partial(bring_kernel, len(values)),
        in_specs=[pl.BlockSpec(memory_space=pl.ANY)] + [hbm()] * len(values),
        out_specs=[vmem()] * len(values),
        out_shape=[shape_of(*value.shape) for value in values],
        scratch_shapes=[pltpu.SemaphoreType.DMA((len(values),))],
        compiler_params=params(16),
        cost_estimate=cost(0, 2 * sum(value.size for value in values)),
        name="bring_weights",
    )(after, *[in_hbm(value) for value in values])


def row_parts(total):
    size = min(total, 128)
    return [slice(start, start + size) for start in range(0, total, size)]


def summed(refs, rows, span):
    return added([ref[rows, span].astype(F32) for ref in refs])


def out_rows_kernel(slots, blocks, place, count, *refs):
    shares, (down_ref, act_ref, out_ref) = refs[:count], refs[count:]
    hidden, part = down_ref.shape[1:]
    for rows in row_parts(act_ref.shape[0]):
        gate_sum = summed(shares, rows, slice(0, hidden))
        up_sum = summed(shares, rows, slice(hidden, 2 * hidden))
        act_ref[rows] = (gate_sum * jax.nn.sigmoid(gate_sum) * up_sum).astype(BF16)
    made = [dot(act_ref[...], down_ref[0, :, span]).astype(BF16) for span in spans(part, blocks)]
    unsort_rows(made, out_ref, slots, place=place)


def out_rows(shares, w_down, blocks, slots, place):
    hidden, part = w_down.shape[1:]
    rows = shares[0].shape[0]
    return pl.pallas_call(
        functools.partial(out_rows_kernel, slots, blocks, place, len(shares)),
        in_specs=[vmem()] * (len(shares) + 1),
        out_specs=[vmem()] * 2,
        out_shape=[shape_of(rows, hidden), shape_of(blocks * rows, part // blocks)],
        compiler_params=params(),
        cost_estimate=cost(2 * rows * part * hidden, 2 * part * hidden),
        name="output_rows",
    )(*shares, w_down)


def grad_rows_kernel(slots, blocks, count, *refs):
    shares, backs = refs[:count], refs[count : 2 * count]
    gate_ref, up_ref, kept_ref, out_ref, act_ref, sem = refs[2 * count :]
    part, hidden = gate_ref.shape[1:]
    cols = part // blocks
    for rows in row_parts(act_ref.shape[0]):
        gate_sum = summed(shares, rows, slice(0, hidden))
        up_sum = summed(shares, rows, slice(hidden, 2 * hidden))
        back_sum = summed(backs, rows, slice(0, hidden))
        sig = jax.nn.sigmoid(gate_sum)
        act_ref[rows, :hidden] = (back_sum * up_sum * sig * (1.0 + gate_sum * (1.0 - sig))).astype(BF16)
        act_ref[rows, hidden:] = (back_sum * (gate_sum * sig)).astype(BF16)
    kept = pltpu.make_async_copy(act_ref, kept_ref, sem)
    kept.start()
    for start, size in pieces_of(cols):
        made = []
        for block in range(blocks):
            span = slice(block * cols + start, block * cols + start + size)
            total = dot(act_ref[:, :hidden], gate_ref[0, span, :], ((1,), (1,)))
            total = total + dot(act_ref[:, hidden:], up_ref[0, span, :], ((1,), (1,)))
            made.append(total.astype(BF16))
        unsort_rows(made, out_ref, slots, slice(start, start + size))
    kept.wait()


def grad_rows(shares, backs, w_gate, w_up, blocks, slots):
    part, hidden = w_gate.shape[1:]
    rows = shares[0].shape[0]
    cols = part // blocks
    return pl.pallas_call(
        functools.partial(grad_rows_kernel, slots, blocks, len(shares)),
        in_specs=[vmem()] * (2 * len(shares) + 2),
        out_specs=[hbm(), vmem()],
        out_shape=[hbm_shape(rows, 2 * hidden), shape_of(blocks * rows, cols)],
        scratch_shapes=[pltpu.VMEM((rows, 2 * hidden), BF16), pltpu.SemaphoreType.DMA],
        compiler_params=params(32),
        cost_estimate=cost(4 * rows * part * hidden, 4 * part * hidden),
        name="gradient_rows",
    )(*shares, *backs, w_gate, w_up)


def weights_kernel(rows_in_ref, rows_up_ref, act_ref, grad_act_ref, gate_ref, up_ref, down_ref):
    hidden = gate_ref.shape[2]
    rows_in = rows_in_ref[0]
    gate_ref[0] = dot(rows_in, grad_act_ref[:, :hidden], ((0,), (0,))).astype(BF16)
    up_ref[0] = dot(rows_in, grad_act_ref[:, hidden:], ((0,), (0,))).astype(BF16)
    down_ref[0] = dot(act_ref[...], rows_up_ref[0], ((0,), (0,))).astype(BF16)


def weight_grads(rows_in, rows_up, act, grad_act):
    blocks, total, width = rows_in.shape
    part = blocks * width
    hidden = act.shape[1]
    cols = block_of(width, 640)
    steps = width // cols
    chunk = pl.BlockSpec((1, total, cols), lambda k, b: (k, 0, b))
    tall = pl.BlockSpec((1, cols, hidden), lambda k, b: (0, k * steps + b, 0))
    return pl.pallas_call(
        weights_kernel,
        grid=(blocks, steps),
        in_specs=[
            chunk,
            chunk,
            pl.BlockSpec((total, hidden), lambda k, b: (0, 0)),
            pl.BlockSpec((total, 2 * hidden), lambda k, b: (0, 0)),
        ],
        out_specs=[tall, tall, pl.BlockSpec((1, hidden, cols), lambda k, b: (0, 0, k * steps + b))],
        out_shape=[shape_of(1, part, hidden), shape_of(1, part, hidden), shape_of(1, hidden, part)],
        compiler_params=params(),
        cost_estimate=cost(6 * total * part * hidden, 6 * part * hidden),
        name="weight_grads",
    )(*[in_hbm(value) for value in (rows_in, rows_up, act, grad_act)])


def back_rows(back_ref, half, halves, run):
    total = back_ref.shape[0]
    return jnp.concatenate([back_ref[start : start + run] for start in range(half * run, total, halves * run)], axis=0)


def put_columns(held_ref, target_ref, sems, half, block, start=None):
    blocks, _, cols = held_ref.shape[1:]
    start = (half * blocks + block) * cols if start is None else start
    copy = pltpu.make_async_copy(held_ref.at[half, block], target_ref.at[:, pl.ds(start, cols)], sems.at[half, block])
    copy.start()
    return copy


def mixed_kernel(picks_ref, gates_ref, cot_ref, back_ref, mixed_ref, gate_grad_ref, put_ref, held_ref, sems):
    slots, experts = picks_ref.shape
    halves, blocks, tokens, cols = held_ref.shape
    rows = experts * blocks * slots
    hit = spread_row(picks_ref[...].astype(F32), blocks).astype(jnp.int32) == iota((tokens, rows), 0)
    scale = spread_row(gates_ref[...], blocks)
    of_block = iota((tokens, rows), 1) % (blocks * slots) // slots
    run = planes_of(experts) * blocks * slots
    backs = [back_rows(back_ref, half, halves, run) for half in range(halves)]
    copies = []
    products = None
    for block in range(blocks):
        inside = hit & (of_block == block)
        put_ref[block] = one_hot(inside)
        rest = jnp.where(inside, scale, 0.0)
        pieces = []
        for _ in range(3):
            pieces.append(rest.astype(BF16))
            rest = rest - pieces[-1].astype(F32)
        for half in range(halves):
            back = backs[half]
            held_ref[half, block] = added([dot(piece, back) for piece in pieces]).astype(BF16)
            copies.append(put_columns(held_ref, mixed_ref, sems, half, block))
            place = half * blocks + block
            product = dot(cot_ref[:, place * cols : (place + 1) * cols], back, ((1,), (1,)))
            product = jnp.where(inside, product, 0.0)
            products = product if products is None else products + product
    values = jnp.sum(products, axis=0, keepdims=True)
    mine = iota((slots, rows), 1) % slots == iota((slots, rows), 0)
    owner = (expert_at(iota((rows, experts), 0) // (blocks * slots), experts) == iota((rows, experts), 1)).astype(F32)
    gate_grad_ref[...] = exact_dot(jnp.where(mine, values, 0.0), owner)
    for copy in copies:
        copy.wait()


def mix_rows(back, cotangent, picks, gates, halves, blocks):
    slots, experts = picks.shape
    tokens, width = cotangent.shape
    cols = width // (halves * blocks)
    rows = experts * blocks * slots
    return pl.pallas_call(
        mixed_kernel,
        in_specs=[vmem()] * 4,
        out_specs=[hbm(), vmem(), vmem()],
        out_shape=[shape_of(tokens, width), shape_of(slots, experts, dtype=F32), shape_of(blocks, tokens, rows)],
        scratch_shapes=[pltpu.VMEM((halves, blocks, tokens, cols), BF16), pltpu.SemaphoreType.DMA((halves, blocks))],
        compiler_params=params(16),
        cost_estimate=cost(8 * rows * tokens * width, 4 * tokens * width),
        name="mixed_rows",
    )(picks, gates, cotangent, back)


def mix_half(half, put_ref, pieces_ref, cot_ref, back_ref, target_ref, held_ref, sems):
    blocks, tokens, cols = held_ref.shape
    back = back_ref[...]
    copies = []
    products = None
    for block in range(blocks):
        start = pl.multiple_of((half * blocks + block) * cols, 128)
        held_ref[block] = added([dot(pieces_ref[block, i], back) for i in range(3)]).astype(BF16)
        copies.append(pltpu.make_async_copy(held_ref.at[block], target_ref.at[:, pl.ds(start, cols)], sems.at[block]))
        copies[-1].start()
        product = dot(cot_ref[:, pl.ds(start, cols)], back, ((1,), (1,))) * put_ref[block].astype(F32)
        products = product if products is None else products + product
    return jnp.sum(products, axis=0, keepdims=True), copies


def near_kernel(picks_ref, gates_ref, cot_ref, back_ref, mixed_ref, put_ref, pieces_ref, sums_ref, held_ref, sems):
    slots = picks_ref.shape[0]
    blocks, tokens, rows = put_ref.shape
    hit = spread_row(picks_ref[...].astype(F32), blocks).astype(jnp.int32) == iota((tokens, rows), 0)
    scale = spread_row(gates_ref[...], blocks)
    of_block = iota((tokens, rows), 1) % (blocks * slots) // slots
    for block in range(blocks):
        inside = hit & (of_block == block)
        put_ref[block] = one_hot(inside)
        rest = jnp.where(inside, scale, 0.0)
        for i in range(3):
            piece = rest.astype(BF16)
            pieces_ref[block, i] = piece
            rest = rest - piece.astype(F32)
    half = lax.axis_index("dp")
    sums_ref[...], copies = mix_half(half, put_ref, pieces_ref, cot_ref, back_ref, mixed_ref, held_ref, sems)
    for copy in copies:
        copy.wait()


def far_kernel(
    slots, put_ref, pieces_ref, sums_ref, cot_ref, back_ref, _, mixed_ref, gate_grad_ref, held_ref, sems
):
    blocks, _, rows = put_ref.shape
    experts = gate_grad_ref.shape[1]
    half = 1 - lax.axis_index("dp")
    values, copies = mix_half(half, put_ref, pieces_ref, cot_ref, back_ref, mixed_ref, held_ref, sems)
    values = values + sums_ref[...]
    mine = iota((slots, rows), 1) % slots == iota((slots, rows), 0)
    owner = (expert_at(iota((rows, experts), 0) // (blocks * slots), experts) == iota((rows, experts), 1)).astype(F32)
    gate_grad_ref[...] = exact_dot(jnp.where(mine, values, 0.0), owner)
    for copy in copies:
        copy.wait()


def mix_halves(own, other, cotangent, picks, gates, blocks):
    slots, experts = picks.shape
    tokens, width = cotangent.shape
    rows, cols = own.shape
    scratch = [pltpu.VMEM((blocks, tokens, cols), BF16), pltpu.SemaphoreType.DMA((blocks,))]
    work = cost(4 * rows * tokens * width, 2 * tokens * width)
    mixed, put, pieces, sums = pl.pallas_call(
        near_kernel,
        in_specs=[vmem()] * 4,
        out_specs=[hbm()] + [vmem()] * 3,
        out_shape=[
            hbm_shape(tokens, width),
            shape_of(blocks, tokens, rows),
            shape_of(blocks, 3, tokens, rows),
            shape_of(1, rows, dtype=F32),
        ],
        scratch_shapes=scratch,
        compiler_params=params(16),
        cost_estimate=work,
        name="mixed_near",
    )(picks, gates, cotangent, own)
    mixed, gate_grad = pl.pallas_call(
        functools.partial(far_kernel, slots),
        in_specs=[vmem()] * 5 + [hbm()],
        out_specs=[hbm(), vmem()],
        out_shape=[hbm_shape(tokens, width), shape_of(slots, experts, dtype=F32)],
        scratch_shapes=scratch,
        input_output_aliases={5: 0},
        compiler_params=params(16),
        cost_estimate=work,
        name="mixed_far",
    )(put, pieces, sums, cotangent, other, in_hbm(mixed))
    return mixed, gate_grad, put


def part_kernel(joined_ref, own_ref, other_ref, sems):
    half = lax.axis_index("dp")
    copies = [
        pltpu.make_async_copy(joined_ref.at[:, half], own_ref, sems.at[0]),
        pltpu.make_async_copy(joined_ref.at[:, 1 - half], other_ref, sems.at[1]),
    ]
    for copy in copies:
        copy.start()
    for copy in copies:
        copy.wait()


def part_rows(joined, experts):
    rows, cols = joined.shape
    shape = (experts, rows // (2 * experts), cols)
    parted = pl.pallas_call(
        part_kernel,
        in_specs=[pl.BlockSpec(memory_space=pl.ANY)],
        out_specs=[pl.BlockSpec(memory_space=pl.ANY)] * 2,
        out_shape=[shape_of(*shape)] * 2,
        scratch_shapes=[pltpu.SemaphoreType.DMA((2,))],
        compiler_params=params(16),
        cost_estimate=cost(0, 4 * rows * cols),
        name="part_rows",
    )(joined.reshape(experts, 2, *shape[1:]))
    return [value.reshape(rows // 2, cols) for value in parted]


def token_grad_kernel(run, put_ref, back_ref, grad_ref, held_ref, sems):
    halves, blocks = held_ref.shape[:2]
    copies = []
    for half in range(halves):
        back = back_rows(back_ref, half, halves, run)
        for block in range(blocks):
            held_ref[half, block] = dot(put_ref[block], back).astype(BF16)
            copies.append(put_columns(held_ref, grad_ref, sems, half, block))
    for copy in copies:
        copy.wait()


def token_grads(back, put, halves, run):
    blocks, tokens, rows = put.shape
    cols = back.shape[1]
    width = halves * blocks * cols
    return pl.pallas_call(
        functools.partial(token_grad_kernel, run),
        in_specs=[vmem()] * 2,
        out_specs=hbm(),
        out_shape=shape_of(tokens, width),
        scratch_shapes=[pltpu.VMEM((halves, blocks, tokens, cols), BF16), pltpu.SemaphoreType.DMA((halves, blocks))],
        compiler_params=params(16),
        cost_estimate=cost(2 * rows * tokens * width, 2 * tokens * width),
        name="token_grads",
    )(put, back)


def to_owners(halves, experts, messages):
    planes = planes_of(experts)
    order = [
        half * experts + plane * (experts // planes) + place
        for place in range(experts // planes)
        for half in range(halves)
        for plane in range(planes)
    ]
    return lax.all_to_all(
        messages, EVERYONE, split_axis=0, concat_axis=0, tiled=True, axis_index_groups=[order]
    )


def to_experts(experts, messages):
    order = [expert_at(place, experts) for place in range(experts)]
    return lax.all_to_all(messages, "expert", split_axis=0, concat_axis=0, tiled=True, axis_index_groups=[order])


def dp_shares(own, halves):
    shares = [own] + [
        lax.ppermute(own, "dp", [(i, (i + shift) % halves) for i in range(halves)]) for shift in range(1, halves)
    ]
    return shares if halves <= 2 else [added([share.astype(F32) for share in shares])]


def body(halves, tokens, cotangent, picks, gates, w_gate, w_up, w_down):
    experts, slots = picks.shape[1:]
    scatter = functools.partial(to_owners, halves, experts)
    blocks = 2 if tokens.shape[1] // halves % 256 == 0 else 1
    picks_t = picks[0].T
    gates_t = gates[0].T
    messages_in = send_rows(tokens, (picks_t,), halves, blocks)
    arrived_in = scatter(messages_in)
    if halves == 2:
        own, other = pair_rows(cotangent, picks_t, gates_t, blocks, messages_in)
        other = lax.ppermute(other, "dp", [(0, 1), (1, 0)])
        arrived_up = to_experts(experts, join_rows(own, other, experts))
    else:
        arrived_up = scatter(send_rows(cotangent, (picks_t, gates_t), halves, blocks))
    own_sums, rows_in = in_sums(arrived_in, w_gate, w_up, blocks, slots)
    shares = dp_shares(own_sums, halves)
    place = functools.partial(split_place, halves=2, planes=planes_of(experts)) if halves == 2 else same_place
    act, outputs = out_rows(shares, w_down, blocks, slots, place)
    back_out = to_experts(experts, outputs) if halves == 2 else scatter(outputs)
    own_back, rows_up = back_sums(arrived_up, w_down, blocks, slots, place)
    backs = dp_shares(own_back, halves)
    near_gate, near_up = bring((w_gate, w_up), own_back)
    grad_act, gradients = grad_rows(shares, backs, near_gate, near_up, blocks, slots)
    back_grad = scatter(gradients)
    grad_gate_w, grad_up_w, grad_down = weight_grads(rows_in, rows_up, act, grad_act)
    if halves == 2:
        own_out, other_out = part_rows(back_out, experts)
        other_out = lax.ppermute(other_out, "dp", [(0, 1), (1, 0)])
        mixed, gate_grad, put = mix_halves(own_out, other_out, cotangent, picks_t, gates_t, blocks)
    else:
        mixed, gate_grad, put = mix_rows(back_out, cotangent, picks_t, gates_t, halves, blocks)
    token_grad = token_grads(back_grad, put, halves, planes_of(experts) * blocks * slots)
    return mixed, token_grad, gate_grad.T[None], grad_gate_w, grad_up_w, grad_down


def solution(mesh):
    rows = P(("dp", "expert"), None)
    lists = P(("dp", "expert"), None, None)
    tall = P("expert", "dp", None)
    wide = P("expert", None, "dp")
    return jax.shard_map(
        functools.partial(body, mesh.shape["dp"]),
        mesh=mesh,
        in_specs=(rows, rows, lists, lists, tall, tall, wide),
        out_specs=(rows, rows, lists, tall, tall, wide),
        check_vma=False,
    )
```

```python
import functools

import jax
import jax.numpy as jnp
from jax import lax
from jax.experimental import pallas as pl
from jax.experimental.pallas import tpu as pltpu
from jax.sharding import PartitionSpec as P

F32 = jnp.float32
BF16 = jnp.bfloat16
MIB = 1024 * 1024
EVERYONE = ("dp", "expert")


def dot(left, right, dims=((1,), (0,)), precision=None):
    return lax.dot_general(left, right, (dims, ((), ())), precision=precision, preferred_element_type=F32)


def exact_dot(left, right, dims=((1,), (0,))):
    return dot(left, right, dims, lax.Precision.HIGHEST)


def iota(shape, axis):
    return lax.broadcasted_iota(jnp.int32, shape, axis)


def planes_of(experts):
    return experts // 4 if experts % 4 == 0 else 1


def expert_at(place, experts):
    planes = planes_of(experts)
    return place % planes * (experts // planes) + place // planes


def split_place(place, halves, planes):
    return (place // (halves * planes) * planes + place % planes) * halves + place // planes % halves


def one_hot(condition):
    return jnp.where(condition, 1.0, 0.0).astype(BF16)


def vmem():
    return pl.BlockSpec(memory_space=pltpu.VMEM)


def hbm():
    return pl.BlockSpec(memory_space=pltpu.HBM)


def in_hbm(value):
    return pltpu.with_memory_space_constraint(value, pltpu.HBM)


def shape_of(*sizes, dtype=BF16):
    return jax.ShapeDtypeStruct(sizes, dtype)


def hbm_shape(*sizes):
    return pltpu.HBM(sizes, BF16)


def params(mib=24):
    return pltpu.CompilerParams(vmem_limit_bytes=mib * MIB)


def cost(flops, moved):
    return pl.CostEstimate(flops=flops, bytes_accessed=moved, transcendentals=0)


def block_of(width, limit):
    best = 128
    for size in range(128, limit + 1, 128):
        if width % size == 0:
            best = size
    return best


def spread_column(values, blocks):
    slots, experts = values.shape
    rows = experts * blocks * slots
    owner = (expert_at(iota((rows, experts), 0) // (blocks * slots), experts) == iota((rows, experts), 1)).astype(F32)
    wide = exact_dot(owner, values, ((1,), (1,)))
    mine = iota((rows, slots), 0) % slots == iota((rows, slots), 1)
    return jnp.sum(jnp.where(mine, wide, 0.0), axis=1, keepdims=True)


def spread_row(values, blocks):
    slots, experts = values.shape
    rows = experts * blocks * slots
    owner = (expert_at(iota((experts, rows), 1) // (blocks * slots), experts) == iota((experts, rows), 0)).astype(F32)
    wide = exact_dot(values, owner)
    mine = iota((slots, rows), 1) % slots == iota((slots, rows), 0)
    return jnp.sum(jnp.where(mine, wide, 0.0), axis=0, keepdims=True)


def send_kernel(halves, blocks, scaled, *refs):
    count = 2 if scaled else 1
    lists, source_ref, out_ref = refs[:count], refs[count], refs[count + 1]
    held_ref, made_ref, sems, list_sems, out_sems = refs[count + 2 : count + 7]
    list_refs = refs[count + 7 :]
    rows, cols = out_ref.shape
    rows = rows // halves
    tokens = source_ref.shape[0]
    list_copies = [
        pltpu.make_async_copy(ref, target, list_sems.at[i]) for i, (ref, target) in enumerate(zip(lists, list_refs))
    ]
    copies = []
    for copy in list_copies:
        copy.start()
    for half in range(halves):
        for block in range(blocks):
            place = half * blocks + block
            copies.append(
                pltpu.make_async_copy(
                    source_ref.at[:, place * cols : (place + 1) * cols],
                    held_ref.at[half, block * tokens : (block + 1) * tokens],
                    sems.at[half, block],
                )
            )
            copies[-1].start()
    for copy in list_copies:
        copy.wait()
    slots, experts = list_refs[0].shape
    run = planes_of(experts) * blocks * slots
    chosen = spread_column(list_refs[0][...].astype(F32), blocks).astype(jnp.int32)
    target = chosen + iota((rows, 1), 0) % (blocks * slots) // slots * tokens
    take = one_hot(target == iota((rows, blocks * tokens), 1))
    scale = spread_column(list_refs[1][...], blocks) if scaled else None
    out_copies = []
    for half in range(halves):
        for block in range(blocks):
            copies[half * blocks + block].wait()
        picked = dot(take, held_ref[half])
        if scaled:
            picked = picked * scale
        picked = picked.astype(BF16)
        for place in range(rows // run):
            start = (place * halves + half) * run
            made_ref[start : start + run] = picked[place * run : (place + 1) * run]
            out_copies.append(
                pltpu.make_async_copy(
                    made_ref.at[start : start + run], out_ref.at[start : start + run], out_sems.at[half, place]
                )
            )
            out_copies[-1].start()
    for copy in out_copies:
        copy.wait()


def pair_kernel(blocks, _, picks_ref, gates_ref, source_ref, own_ref, other_ref, held_ref, sems, list_sems, *list_refs):
    slots = picks_ref.shape[0]
    tokens = source_ref.shape[0]
    rows, cols = own_ref.shape
    half = lax.axis_index("dp")
    list_copies = [
        pltpu.make_async_copy(ref, target, list_sems.at[i])
        for i, (ref, target) in enumerate(zip((picks_ref, gates_ref), list_refs))
    ]
    for copy in list_copies:
        copy.start()
    copies = []
    for far in range(2):
        for block in range(blocks):
            start = (jnp.bitwise_xor(half, far) * blocks + block) * cols
            copies.append(
                pltpu.make_async_copy(
                    source_ref.at[:, pl.ds(pl.multiple_of(start, 128), cols)],
                    held_ref.at[far, block * tokens : (block + 1) * tokens],
                    sems.at[far, block],
                )
            )
            copies[-1].start()
    for copy in list_copies:
        copy.wait()
    chosen = spread_column(list_refs[0][...].astype(F32), blocks).astype(jnp.int32)
    target = chosen + iota((rows, 1), 0) % (blocks * slots) // slots * tokens
    take = one_hot(target == iota((rows, blocks * tokens), 1))
    scale = spread_column(list_refs[1][...], blocks)
    for far, out_ref in enumerate((own_ref, other_ref)):
        for block in range(blocks):
            copies[far * blocks + block].wait()
        out_ref[...] = (dot(take, held_ref[far]) * scale).astype(BF16)


def pair_rows(source, picks, gates, blocks, after):
    slots, experts = picks.shape
    tokens, width = source.shape
    cols = width // (2 * blocks)
    rows = experts * blocks * slots
    return pl.pallas_call(
        functools.partial(pair_kernel, blocks),
        in_specs=[hbm()] * 4,
        out_specs=[vmem()] * 2,
        out_shape=[shape_of(rows, cols)] * 2,
        scratch_shapes=[
            pltpu.VMEM((2, blocks * tokens, cols), BF16),
            pltpu.SemaphoreType.DMA((2, blocks)),
            pltpu.SemaphoreType.DMA((2,)),
            pltpu.VMEM((slots, experts), picks.dtype),
            pltpu.VMEM((slots, experts), gates.dtype),
        ],
        compiler_params=params(16),
        cost_estimate=cost(4 * rows * cols * tokens * blocks, 2 * tokens * width),
        name="pair_rows",
    )(in_hbm(after), in_hbm(picks), in_hbm(gates), in_hbm(source))


def join_kernel(own_ref, other_ref, out_ref, sems):
    half = lax.axis_index("dp")
    copies = [
        pltpu.make_async_copy(own_ref, out_ref.at[:, half], sems.at[0]),
        pltpu.make_async_copy(other_ref, out_ref.at[:, 1 - half], sems.at[1]),
    ]
    for copy in copies:
        copy.start()
    for copy in copies:
        copy.wait()


def join_rows(own, other, experts):
    rows, cols = own.shape
    shape = (experts, rows // experts, cols)
    joined = pl.pallas_call(
        join_kernel,
        in_specs=[pl.BlockSpec(memory_space=pl.ANY)] * 2,
        out_specs=hbm(),
        out_shape=hbm_shape(experts, 2, *shape[1:]),
        scratch_shapes=[pltpu.SemaphoreType.DMA((2,))],
        compiler_params=params(16),
        cost_estimate=cost(0, 8 * rows * cols),
        name="join_rows",
    )(own.reshape(shape), other.reshape(shape))
    return joined.reshape(2 * rows, cols)


def send_rows(source, lists, halves, blocks):
    slots, experts = lists[0].shape
    tokens, width = source.shape
    cols = width // (halves * blocks)
    rows = halves * experts * blocks * slots
    return pl.pallas_call(
        functools.partial(send_kernel, halves, blocks, len(lists) == 2),
        in_specs=[hbm()] * (len(lists) + 1),
        out_specs=hbm(),
        out_shape=hbm_shape(rows, cols),
        scratch_shapes=[
            pltpu.VMEM((halves, blocks * tokens, cols), BF16),
            pltpu.VMEM((rows, cols), BF16),
            pltpu.SemaphoreType.DMA((halves, blocks)),
            pltpu.SemaphoreType.DMA((2,)),
            pltpu.SemaphoreType.DMA((halves, experts // planes_of(experts))),
        ]
        + [pltpu.VMEM((slots, experts), value.dtype) for value in lists],
        compiler_params=params(16),
        cost_estimate=cost(2 * rows * cols * tokens * blocks, 2 * tokens * width + 2 * rows * cols),
        name="send_rows",
    )(*[in_hbm(value) for value in lists], in_hbm(source))


def same_place(device):
    return device


def sort_matrix(rows, blocks, slots, back, place=same_place):
    a = iota((rows, rows), 1 if back else 0)
    b = iota((rows, rows), 0 if back else 1)
    group = rows // blocks
    return one_hot(place(a % group // slots) * (blocks * slots) + a // group * slots + a % slots == b)


def sort_rows(messages_ref, rows_ref, slots, place=same_place):
    blocks, total = rows_ref.shape[:2]
    if blocks == 1 and place is same_place:
        rows_ref[0] = messages_ref[...]
        return
    size = min(blocks * total, 256)
    group = size // blocks
    order = sort_matrix(size, blocks, slots, False, place)
    for part in range(total // group):
        ordered = dot(order, messages_ref[part * size : (part + 1) * size]).astype(BF16)
        for block in range(blocks):
            rows_ref[block, part * group : (part + 1) * group] = ordered[block * group : (block + 1) * group]


def unsort_rows(made, out_ref, slots, span=slice(None), place=same_place):
    blocks, total = len(made), made[0].shape[0]
    if blocks == 1 and place is same_place:
        out_ref[:, span] = made[0]
        return
    size = min(blocks * total, 256)
    group = size // blocks
    order = sort_matrix(size, blocks, slots, True, place)
    for part in range(total // group):
        stacked = jnp.concatenate([value[part * group : (part + 1) * group] for value in made], axis=0)
        out_ref[part * size : (part + 1) * size, span] = dot(order, stacked).astype(BF16)


def spans(ref, blocks):
    cols = ref // blocks
    return [slice(block * cols, (block + 1) * cols) for block in range(blocks)]


def added(terms):
    return functools.reduce(jnp.add, terms)


def pieces_of(width):
    if width % 256 or width <= 768:
        return [(0, width)]
    first = width // 2 // 256 * 256
    return [(0, first), (first, width - first)]


class Stream:
    def __init__(self, sems):
        self.sems, self.copies = sems, []

    def start(self, source, target):
        copy = pltpu.make_async_copy(source, target, self.sems.at[len(self.copies)])
        copy.start()
        self.copies.append(copy)
        return copy


def in_sums_kernel(slots, messages_ref, gate_ref, up_ref, out_ref, kept_ref, rows_ref, held_ref, acc_ref, sems):
    blocks, _, cols = rows_ref.shape
    hidden = gate_ref.shape[2]
    stream = Stream(sems)
    cuts = [(block, start, size) for block in range(blocks) for start, size in pieces_of(cols)]
    copies = []
    for block, start, size in cuts:
        span = slice(block * cols + start, block * cols + start + size)
        copies += [stream.start(ref.at[0, span], held_ref.at[i, span]) for i, ref in enumerate((gate_ref, up_ref))]
    sort_rows(messages_ref, rows_ref, slots)
    kept = stream.start(rows_ref, kept_ref)
    for number, (block, start, size) in enumerate(cuts):
        span = slice(block * cols + start, block * cols + start + size)
        for i in range(2):
            copies[2 * number + i].wait()
            term = dot(rows_ref[block, :, start : start + size], held_ref[i, span])
            acc_ref[i] = term if number == 0 else acc_ref[i] + term
    for i in range(2):
        out_ref[:, i * hidden : (i + 1) * hidden] = acc_ref[i].astype(BF16)
    kept.wait()


def in_sums(messages, w_gate, w_up, blocks, slots):
    part, hidden = w_gate.shape[1:]
    rows = messages.shape[0] // blocks
    cols = part // blocks
    return pl.pallas_call(
        functools.partial(in_sums_kernel, slots),
        in_specs=[vmem(), hbm(), hbm()],
        out_specs=[vmem(), hbm()],
        out_shape=[shape_of(rows, 2 * hidden), hbm_shape(blocks, rows, cols)],
        scratch_shapes=[
            pltpu.VMEM((blocks, rows, cols), BF16),
            pltpu.VMEM((2, part, hidden), BF16),
            pltpu.VMEM((2, rows, hidden), F32),
            pltpu.SemaphoreType.DMA((2 * blocks * len(pieces_of(cols)) + 1,)),
        ],
        compiler_params=params(),
        cost_estimate=cost(4 * rows * part * hidden, 4 * part * hidden),
        name="gate_up_sums",
    )(messages, in_hbm(w_gate), in_hbm(w_up))


def back_sums_kernel(slots, place, messages_ref, down_ref, out_ref, kept_ref, rows_ref, held_ref, acc_ref, sems):
    blocks, _, cols = rows_ref.shape
    stream = Stream(sems)
    cuts = [(block, start, size) for block in range(blocks) for start, size in pieces_of(cols)]
    copies = []
    for block, start, size in cuts:
        span = slice(block * cols + start, block * cols + start + size)
        copies.append(stream.start(down_ref.at[0, :, span], held_ref.at[:, span]))
    sort_rows(messages_ref, rows_ref, slots, place)
    kept = stream.start(rows_ref, kept_ref)
    for number, (block, start, size) in enumerate(cuts):
        span = slice(block * cols + start, block * cols + start + size)
        copies[number].wait()
        term = dot(rows_ref[block, :, start : start + size], held_ref[:, span], ((1,), (1,)))
        acc_ref[...] = term if number == 0 else acc_ref[...] + term
    out_ref[...] = acc_ref[...].astype(BF16)
    kept.wait()


def back_sums(messages, w_down, blocks, slots, place):
    hidden, part = w_down.shape[1:]
    rows = messages.shape[0] // blocks
    cols = part // blocks
    return pl.pallas_call(
        functools.partial(back_sums_kernel, slots, place),
        in_specs=[vmem(), hbm()],
        out_specs=[vmem(), hbm()],
        out_shape=[shape_of(rows, hidden), hbm_shape(blocks, rows, cols)],
        scratch_shapes=[
            pltpu.VMEM((blocks, rows, cols), BF16),
            pltpu.VMEM((hidden, part), BF16),
            pltpu.VMEM((rows, hidden), F32),
            pltpu.SemaphoreType.DMA((blocks * len(pieces_of(cols)) + 1,)),
        ],
        compiler_params=params(),
        cost_estimate=cost(2 * rows * part * hidden, 2 * part * hidden),
        name="back_sums",
    )(messages, in_hbm(w_down))


def bring_kernel(count, *refs):
    sources, targets, sems = refs[1 : count + 1], refs[count + 1 : 2 * count + 1], refs[-1]
    copies = [pltpu.make_async_copy(s, t, sems.at[i]) for i, (s, t) in enumerate(zip(sources, targets))]
    for copy in copies:
        copy.start()
    for copy in copies:
        copy.wait()


def bring(values, after):
    return pl.pallas_call(
        functools.partial(bring_kernel, len(values)),
        in_specs=[pl.BlockSpec(memory_space=pl.ANY)] + [hbm()] * len(values),
        out_specs=[vmem()] * len(values),
        out_shape=[shape_of(*value.shape) for value in values],
        scratch_shapes=[pltpu.SemaphoreType.DMA((len(values),))],
        compiler_params=params(16),
        cost_estimate=cost(0, 2 * sum(value.size for value in values)),
        name="bring_weights",
    )(after, *[in_hbm(value) for value in values])


def row_parts(total):
    size = min(total, 128)
    return [slice(start, start + size) for start in range(0, total, size)]


def summed(refs, rows, span):
    return added([ref[rows, span].astype(F32) for ref in refs])


def out_rows_kernel(slots, blocks, place, count, *refs):
    shares, (down_ref, act_ref, out_ref) = refs[:count], refs[count:]
    hidden, part = down_ref.shape[1:]
    for rows in row_parts(act_ref.shape[0]):
        gate_sum = summed(shares, rows, slice(0, hidden))
        up_sum = summed(shares, rows, slice(hidden, 2 * hidden))
        act_ref[rows] = (gate_sum * jax.nn.sigmoid(gate_sum) * up_sum).astype(BF16)
    made = [dot(act_ref[...], down_ref[0, :, span]).astype(BF16) for span in spans(part, blocks)]
    unsort_rows(made, out_ref, slots, place=place)


def out_rows(shares, w_down, blocks, slots, place):
    hidden, part = w_down.shape[1:]
    rows = shares[0].shape[0]
    return pl.pallas_call(
        functools.partial(out_rows_kernel, slots, blocks, place, len(shares)),
        in_specs=[vmem()] * (len(shares) + 1),
        out_specs=[vmem()] * 2,
        out_shape=[shape_of(rows, hidden), shape_of(blocks * rows, part // blocks)],
        compiler_params=params(),
        cost_estimate=cost(2 * rows * part * hidden, 2 * part * hidden),
        name="output_rows",
    )(*shares, w_down)


def grad_rows_kernel(slots, blocks, count, *refs):
    shares, backs = refs[:count], refs[count : 2 * count]
    gate_ref, up_ref, kept_ref, out_ref, act_ref, sem = refs[2 * count :]
    part, hidden = gate_ref.shape[1:]
    cols = part // blocks
    for rows in row_parts(act_ref.shape[0]):
        gate_sum = summed(shares, rows, slice(0, hidden))
        up_sum = summed(shares, rows, slice(hidden, 2 * hidden))
        back_sum = summed(backs, rows, slice(0, hidden))
        sig = jax.nn.sigmoid(gate_sum)
        act_ref[rows, :hidden] = (back_sum * up_sum * sig * (1.0 + gate_sum * (1.0 - sig))).astype(BF16)
        act_ref[rows, hidden:] = (back_sum * (gate_sum * sig)).astype(BF16)
    kept = pltpu.make_async_copy(act_ref, kept_ref, sem)
    kept.start()
    for start, size in pieces_of(cols):
        made = []
        for block in range(blocks):
            span = slice(block * cols + start, block * cols + start + size)
            total = dot(act_ref[:, :hidden], gate_ref[0, span, :], ((1,), (1,)))
            total = total + dot(act_ref[:, hidden:], up_ref[0, span, :], ((1,), (1,)))
            made.append(total.astype(BF16))
        unsort_rows(made, out_ref, slots, slice(start, start + size))
    kept.wait()


def grad_rows(shares, backs, w_gate, w_up, blocks, slots):
    part, hidden = w_gate.shape[1:]
    rows = shares[0].shape[0]
    cols = part // blocks
    return pl.pallas_call(
        functools.partial(grad_rows_kernel, slots, blocks, len(shares)),
        in_specs=[vmem()] * (2 * len(shares) + 2),
        out_specs=[hbm(), vmem()],
        out_shape=[hbm_shape(rows, 2 * hidden), shape_of(blocks * rows, cols)],
        scratch_shapes=[pltpu.VMEM((rows, 2 * hidden), BF16), pltpu.SemaphoreType.DMA],
        compiler_params=params(32),
        cost_estimate=cost(4 * rows * part * hidden, 4 * part * hidden),
        name="gradient_rows",
    )(*shares, *backs, w_gate, w_up)


def weights_kernel(rows_in_ref, rows_up_ref, act_ref, grad_act_ref, gate_ref, up_ref, down_ref):
    hidden = gate_ref.shape[2]
    rows_in = rows_in_ref[0]
    gate_ref[0] = dot(rows_in, grad_act_ref[:, :hidden], ((0,), (0,))).astype(BF16)
    up_ref[0] = dot(rows_in, grad_act_ref[:, hidden:], ((0,), (0,))).astype(BF16)
    down_ref[0] = dot(act_ref[...], rows_up_ref[0], ((0,), (0,))).astype(BF16)


def weight_grads(rows_in, rows_up, act, grad_act):
    blocks, total, width = rows_in.shape
    part = blocks * width
    hidden = act.shape[1]
    cols = block_of(width, 640)
    steps = width // cols
    chunk = pl.BlockSpec((1, total, cols), lambda k, b: (k, 0, b))
    tall = pl.BlockSpec((1, cols, hidden), lambda k, b: (0, k * steps + b, 0))
    return pl.pallas_call(
        weights_kernel,
        grid=(blocks, steps),
        in_specs=[
            chunk,
            chunk,
            pl.BlockSpec((total, hidden), lambda k, b: (0, 0)),
            pl.BlockSpec((total, 2 * hidden), lambda k, b: (0, 0)),
        ],
        out_specs=[tall, tall, pl.BlockSpec((1, hidden, cols), lambda k, b: (0, 0, k * steps + b))],
        out_shape=[shape_of(1, part, hidden), shape_of(1, part, hidden), shape_of(1, hidden, part)],
        compiler_params=params(),
        cost_estimate=cost(6 * total * part * hidden, 6 * part * hidden),
        name="weight_grads",
    )(*[in_hbm(value) for value in (rows_in, rows_up, act, grad_act)])


def back_rows(back_ref, half, halves, run):
    total = back_ref.shape[0]
    return jnp.concatenate([back_ref[start : start + run] for start in range(half * run, total, halves * run)], axis=0)


def put_columns(held_ref, target_ref, sems, half, block, start=None):
    blocks, _, cols = held_ref.shape[1:]
    start = (half * blocks + block) * cols if start is None else start
    copy = pltpu.make_async_copy(held_ref.at[half, block], target_ref.at[:, pl.ds(start, cols)], sems.at[half, block])
    copy.start()
    return copy


def mixed_kernel(picks_ref, gates_ref, cot_ref, back_ref, mixed_ref, gate_grad_ref, put_ref, held_ref, sems):
    slots, experts = picks_ref.shape
    halves, blocks, tokens, cols = held_ref.shape
    rows = experts * blocks * slots
    hit = spread_row(picks_ref[...].astype(F32), blocks).astype(jnp.int32) == iota((tokens, rows), 0)
    scale = spread_row(gates_ref[...], blocks)
    of_block = iota((tokens, rows), 1) % (blocks * slots) // slots
    run = planes_of(experts) * blocks * slots
    backs = [back_rows(back_ref, half, halves, run) for half in range(halves)]
    copies = []
    products = None
    for block in range(blocks):
        inside = hit & (of_block == block)
        put_ref[block] = one_hot(inside)
        rest = jnp.where(inside, scale, 0.0)
        pieces = []
        for _ in range(3):
            pieces.append(rest.astype(BF16))
            rest = rest - pieces[-1].astype(F32)
        for half in range(halves):
            back = backs[half]
            held_ref[half, block] = added([dot(piece, back) for piece in pieces]).astype(BF16)
            copies.append(put_columns(held_ref, mixed_ref, sems, half, block))
            place = half * blocks + block
            product = dot(cot_ref[:, place * cols : (place + 1) * cols], back, ((1,), (1,)))
            product = jnp.where(inside, product, 0.0)
            products = product if products is None else products + product
    values = jnp.sum(products, axis=0, keepdims=True)
    mine = iota((slots, rows), 1) % slots == iota((slots, rows), 0)
    owner = (expert_at(iota((rows, experts), 0) // (blocks * slots), experts) == iota((rows, experts), 1)).astype(F32)
    gate_grad_ref[...] = exact_dot(jnp.where(mine, values, 0.0), owner)
    for copy in copies:
        copy.wait()


def mix_rows(back, cotangent, picks, gates, halves, blocks):
    slots, experts = picks.shape
    tokens, width = cotangent.shape
    cols = width // (halves * blocks)
    rows = experts * blocks * slots
    return pl.pallas_call(
        mixed_kernel,
        in_specs=[vmem()] * 4,
        out_specs=[hbm(), vmem(), vmem()],
        out_shape=[shape_of(tokens, width), shape_of(slots, experts, dtype=F32), shape_of(blocks, tokens, rows)],
        scratch_shapes=[pltpu.VMEM((halves, blocks, tokens, cols), BF16), pltpu.SemaphoreType.DMA((halves, blocks))],
        compiler_params=params(16),
        cost_estimate=cost(8 * rows * tokens * width, 4 * tokens * width),
        name="mixed_rows",
    )(picks, gates, cotangent, back)


def mix_half(half, put_ref, pieces_ref, cot_ref, back_ref, target_ref, held_ref, sems):
    blocks, tokens, cols = held_ref.shape
    back = back_ref[...]
    copies = []
    products = None
    for block in range(blocks):
        start = pl.multiple_of((half * blocks + block) * cols, 128)
        held_ref[block] = added([dot(pieces_ref[block, i], back) for i in range(3)]).astype(BF16)
        copies.append(pltpu.make_async_copy(held_ref.at[block], target_ref.at[:, pl.ds(start, cols)], sems.at[block]))
        copies[-1].start()
        product = dot(cot_ref[:, pl.ds(start, cols)], back, ((1,), (1,))) * put_ref[block].astype(F32)
        products = product if products is None else products + product
    return jnp.sum(products, axis=0, keepdims=True), copies


def near_kernel(picks_ref, gates_ref, cot_ref, back_ref, mixed_ref, put_ref, pieces_ref, sums_ref, held_ref, sems):
    slots = picks_ref.shape[0]
    blocks, tokens, rows = put_ref.shape
    hit = spread_row(picks_ref[...].astype(F32), blocks).astype(jnp.int32) == iota((tokens, rows), 0)
    scale = spread_row(gates_ref[...], blocks)
    of_block = iota((tokens, rows), 1) % (blocks * slots) // slots
    for block in range(blocks):
        inside = hit & (of_block == block)
        put_ref[block] = one_hot(inside)
        rest = jnp.where(inside, scale, 0.0)
        for i in range(3):
            piece = rest.astype(BF16)
            pieces_ref[block, i] = piece
            rest = rest - piece.astype(F32)
    half = lax.axis_index("dp")
    sums_ref[...], copies = mix_half(half, put_ref, pieces_ref, cot_ref, back_ref, mixed_ref, held_ref, sems)
    for copy in copies:
        copy.wait()


def far_kernel(
    slots, put_ref, pieces_ref, sums_ref, cot_ref, back_ref, _, mixed_ref, gate_grad_ref, held_ref, sems
):
    blocks, _, rows = put_ref.shape
    experts = gate_grad_ref.shape[1]
    half = 1 - lax.axis_index("dp")
    values, copies = mix_half(half, put_ref, pieces_ref, cot_ref, back_ref, mixed_ref, held_ref, sems)
    values = values + sums_ref[...]
    mine = iota((slots, rows), 1) % slots == iota((slots, rows), 0)
    owner = (expert_at(iota((rows, experts), 0) // (blocks * slots), experts) == iota((rows, experts), 1)).astype(F32)
    gate_grad_ref[...] = exact_dot(jnp.where(mine, values, 0.0), owner)
    for copy in copies:
        copy.wait()


def mix_halves(own, other, cotangent, picks, gates, blocks):
    slots, experts = picks.shape
    tokens, width = cotangent.shape
    rows, cols = own.shape
    scratch = [pltpu.VMEM((blocks, tokens, cols), BF16), pltpu.SemaphoreType.DMA((blocks,))]
    work = cost(4 * rows * tokens * width, 2 * tokens * width)
    mixed, put, pieces, sums = pl.pallas_call(
        near_kernel,
        in_specs=[vmem()] * 4,
        out_specs=[hbm()] + [vmem()] * 3,
        out_shape=[
            hbm_shape(tokens, width),
            shape_of(blocks, tokens, rows),
            shape_of(blocks, 3, tokens, rows),
            shape_of(1, rows, dtype=F32),
        ],
        scratch_shapes=scratch,
        compiler_params=params(16),
        cost_estimate=work,
        name="mixed_near",
    )(picks, gates, cotangent, own)
    mixed, gate_grad = pl.pallas_call(
        functools.partial(far_kernel, slots),
        in_specs=[vmem()] * 5 + [hbm()],
        out_specs=[hbm(), vmem()],
        out_shape=[hbm_shape(tokens, width), shape_of(slots, experts, dtype=F32)],
        scratch_shapes=scratch,
        input_output_aliases={5: 0},
        compiler_params=params(16),
        cost_estimate=work,
        name="mixed_far",
    )(put, pieces, sums, cotangent, other, in_hbm(mixed))
    return mixed, gate_grad, put


def part_kernel(joined_ref, own_ref, other_ref, sems):
    half = lax.axis_index("dp")
    copies = [
        pltpu.make_async_copy(joined_ref.at[:, half], own_ref, sems.at[0]),
        pltpu.make_async_copy(joined_ref.at[:, 1 - half], other_ref, sems.at[1]),
    ]
    for copy in copies:
        copy.start()
    for copy in copies:
        copy.wait()


def part_rows(joined, experts):
    rows, cols = joined.shape
    shape = (experts, rows // (2 * experts), cols)
    parted = pl.pallas_call(
        part_kernel,
        in_specs=[pl.BlockSpec(memory_space=pl.ANY)],
        out_specs=[pl.BlockSpec(memory_space=pl.ANY)] * 2,
        out_shape=[shape_of(*shape)] * 2,
        scratch_shapes=[pltpu.SemaphoreType.DMA((2,))],
        compiler_params=params(16),
        cost_estimate=cost(0, 4 * rows * cols),
        name="part_rows",
    )(joined.reshape(experts, 2, *shape[1:]))
    return [value.reshape(rows // 2, cols) for value in parted]


def token_grad_kernel(run, _, put_ref, back_ref, grad_ref, held_ref, sems):
    halves, blocks = held_ref.shape[:2]
    copies = []
    for half in range(halves):
        back = back_rows(back_ref, half, halves, run)
        for block in range(blocks):
            held_ref[half, block] = dot(put_ref[block], back).astype(BF16)
            copies.append(put_columns(held_ref, grad_ref, sems, half, block))
    for copy in copies:
        copy.wait()


def token_grads(back, put, halves, run, after):
    blocks, tokens, rows = put.shape
    cols = back.shape[1]
    width = halves * blocks * cols
    return pl.pallas_call(
        functools.partial(token_grad_kernel, run),
        in_specs=[pl.BlockSpec(memory_space=pl.ANY)] + [vmem()] * 2,
        out_specs=hbm(),
        out_shape=shape_of(tokens, width),
        scratch_shapes=[pltpu.VMEM((halves, blocks, tokens, cols), BF16), pltpu.SemaphoreType.DMA((halves, blocks))],
        compiler_params=params(16),
        cost_estimate=cost(2 * rows * tokens * width, 2 * tokens * width),
        name="token_grads",
    )(after, put, back)


def to_owners(halves, experts, messages):
    planes = planes_of(experts)
    order = [
        half * experts + plane * (experts // planes) + place
        for place in range(experts // planes)
        for half in range(halves)
        for plane in range(planes)
    ]
    return lax.all_to_all(
        messages, EVERYONE, split_axis=0, concat_axis=0, tiled=True, axis_index_groups=[order]
    )


def to_experts(experts, messages):
    order = [expert_at(place, experts) for place in range(experts)]
    return lax.all_to_all(messages, "expert", split_axis=0, concat_axis=0, tiled=True, axis_index_groups=[order])


def dp_shares(own, halves):
    shares = [own] + [
        lax.ppermute(own, "dp", [(i, (i + shift) % halves) for i in range(halves)]) for shift in range(1, halves)
    ]
    return shares if halves <= 2 else [added([share.astype(F32) for share in shares])]


def body(halves, tokens, cotangent, picks, gates, w_gate, w_up, w_down):
    experts, slots = picks.shape[1:]
    scatter = functools.partial(to_owners, halves, experts)
    blocks = 2 if tokens.shape[1] // halves % 256 == 0 else 1
    picks_t = picks[0].T
    gates_t = gates[0].T
    messages_in = send_rows(tokens, (picks_t,), halves, blocks)
    arrived_in = scatter(messages_in)
    if halves == 2:
        own, other = pair_rows(cotangent, picks_t, gates_t, blocks, messages_in)
        other = lax.ppermute(other, "dp", [(0, 1), (1, 0)])
        arrived_up = to_experts(experts, join_rows(own, other, experts))
    else:
        arrived_up = scatter(send_rows(cotangent, (picks_t, gates_t), halves, blocks))
    own_sums, rows_in = in_sums(arrived_in, w_gate, w_up, blocks, slots)
    shares = dp_shares(own_sums, halves)
    place = functools.partial(split_place, halves=2, planes=planes_of(experts)) if halves == 2 else same_place
    act, outputs = out_rows(shares, w_down, blocks, slots, place)
    back_out = to_experts(experts, outputs) if halves == 2 else scatter(outputs)
    own_back, rows_up = back_sums(arrived_up, w_down, blocks, slots, place)
    backs = dp_shares(own_back, halves)
    near_gate, near_up = bring((w_gate, w_up), own_back)
    grad_act, gradients = grad_rows(shares, backs, near_gate, near_up, blocks, slots)
    back_grad = scatter(gradients)
    grad_gate_w, grad_up_w, grad_down = weight_grads(rows_in, rows_up, act, grad_act)
    if halves == 2:
        own_out, other_out = part_rows(back_out, experts)
        other_out = lax.ppermute(other_out, "dp", [(0, 1), (1, 0)])
        mixed, gate_grad, put = mix_halves(own_out, other_out, cotangent, picks_t, gates_t, blocks)
    else:
        mixed, gate_grad, put = mix_rows(back_out, cotangent, picks_t, gates_t, halves, blocks)
    token_grad = token_grads(back_grad, put, halves, planes_of(experts) * blocks * slots, gate_grad)
    return mixed, token_grad, gate_grad.T[None], grad_gate_w, grad_up_w, grad_down


def solution(mesh):
    rows = P(("dp", "expert"), None)
    lists = P(("dp", "expert"), None, None)
    tall = P("expert", "dp", None)
    wide = P("expert", None, "dp")
    return jax.shard_map(
        functools.partial(body, mesh.shape["dp"]),
        mesh=mesh,
        in_specs=(rows, rows, lists, lists, tall, tall, wide),
        out_specs=(rows, rows, lists, tall, tall, wide),
        check_vma=False,
    )
```

```python
import functools

import jax
import jax.numpy as jnp
from jax import lax
from jax.experimental import pallas as pl
from jax.experimental.pallas import tpu as pltpu
from jax.sharding import PartitionSpec as P

F32 = jnp.float32
BF16 = jnp.bfloat16
MIB = 1024 * 1024
EVERYONE = ("dp", "expert")


def dot(left, right, dims=((1,), (0,)), precision=None):
    return lax.dot_general(left, right, (dims, ((), ())), precision=precision, preferred_element_type=F32)


def exact_dot(left, right, dims=((1,), (0,))):
    return dot(left, right, dims, lax.Precision.HIGHEST)


def iota(shape, axis):
    return lax.broadcasted_iota(jnp.int32, shape, axis)


def planes_of(experts):
    return experts // 4 if experts % 4 == 0 else 1


def expert_at(place, experts):
    planes = planes_of(experts)
    return place % planes * (experts // planes) + place // planes


def split_place(place, halves, planes):
    return (place // (halves * planes) * planes + place % planes) * halves + place // planes % halves


def one_hot(condition):
    return jnp.where(condition, 1.0, 0.0).astype(BF16)


def vmem():
    return pl.BlockSpec(memory_space=pltpu.VMEM)


def hbm():
    return pl.BlockSpec(memory_space=pltpu.HBM)


def in_hbm(value):
    return pltpu.with_memory_space_constraint(value, pltpu.HBM)


def shape_of(*sizes, dtype=BF16):
    return jax.ShapeDtypeStruct(sizes, dtype)


def hbm_shape(*sizes):
    return pltpu.HBM(sizes, BF16)


def params(mib=24):
    return pltpu.CompilerParams(vmem_limit_bytes=mib * MIB)


def cost(flops, moved):
    return pl.CostEstimate(flops=flops, bytes_accessed=moved, transcendentals=0)


def block_of(width, limit):
    best = 128
    for size in range(128, limit + 1, 128):
        if width % size == 0:
            best = size
    return best


def spread_column(values, blocks, plain=False):
    slots, experts = values.shape
    rows = experts * blocks * slots
    owner = (expert_at(iota((rows, experts), 0) // (blocks * slots), experts) == iota((rows, experts), 1)).astype(F32)
    if plain:
        wide = dot(owner.astype(BF16), values.astype(BF16), ((1,), (1,)))
    else:
        wide = exact_dot(owner, values, ((1,), (1,)))
    mine = iota((rows, slots), 0) % slots == iota((rows, slots), 1)
    return jnp.sum(jnp.where(mine, wide, 0.0), axis=1, keepdims=True)


def spread_row(values, blocks):
    slots, experts = values.shape
    rows = experts * blocks * slots
    owner = (expert_at(iota((experts, rows), 1) // (blocks * slots), experts) == iota((experts, rows), 0)).astype(F32)
    wide = exact_dot(values, owner)
    mine = iota((slots, rows), 1) % slots == iota((slots, rows), 0)
    return jnp.sum(jnp.where(mine, wide, 0.0), axis=0, keepdims=True)


def send_kernel(halves, blocks, scaled, *refs):
    count = 2 if scaled else 1
    lists, source_ref, out_ref = refs[:count], refs[count], refs[count + 1]
    held_ref, made_ref, sems, list_sems, out_sems = refs[count + 2 : count + 7]
    list_refs = refs[count + 7 :]
    rows, cols = out_ref.shape
    rows = rows // halves
    tokens = source_ref.shape[0]
    list_copies = [
        pltpu.make_async_copy(ref, target, list_sems.at[i]) for i, (ref, target) in enumerate(zip(lists, list_refs))
    ]
    copies = []
    for copy in list_copies:
        copy.start()
    for half in range(halves):
        for block in range(blocks):
            place = half * blocks + block
            copies.append(
                pltpu.make_async_copy(
                    source_ref.at[:, place * cols : (place + 1) * cols],
                    held_ref.at[half, block * tokens : (block + 1) * tokens],
                    sems.at[half, block],
                )
            )
            copies[-1].start()
    for copy in list_copies:
        copy.wait()
    slots, experts = list_refs[0].shape
    run = planes_of(experts) * blocks * slots
    chosen = spread_column(list_refs[0][...].astype(F32), blocks, tokens <= 256).astype(jnp.int32)
    target = chosen + iota((rows, 1), 0) % (blocks * slots) // slots * tokens
    take = one_hot(target == iota((rows, blocks * tokens), 1))
    scale = spread_column(list_refs[1][...], blocks) if scaled else None
    out_copies = []
    for half in range(halves):
        for block in range(blocks):
            copies[half * blocks + block].wait()
        picked = dot(take, held_ref[half])
        if scaled:
            picked = picked * scale
        picked = picked.astype(BF16)
        for place in range(rows // run):
            start = (place * halves + half) * run
            made_ref[start : start + run] = picked[place * run : (place + 1) * run]
            out_copies.append(
                pltpu.make_async_copy(
                    made_ref.at[start : start + run], out_ref.at[start : start + run], out_sems.at[half, place]
                )
            )
            out_copies[-1].start()
    for copy in out_copies:
        copy.wait()


def pair_kernel(blocks, _, picks_ref, gates_ref, source_ref, own_ref, other_ref, held_ref, sems, list_sems, *list_refs):
    slots = picks_ref.shape[0]
    tokens = source_ref.shape[0]
    rows, cols = own_ref.shape
    half = lax.axis_index("dp")
    list_copies = [
        pltpu.make_async_copy(ref, target, list_sems.at[i])
        for i, (ref, target) in enumerate(zip((picks_ref, gates_ref), list_refs))
    ]
    for copy in list_copies:
        copy.start()
    copies = []
    for far in range(2):
        for block in range(blocks):
            start = (jnp.bitwise_xor(half, far) * blocks + block) * cols
            copies.append(
                pltpu.make_async_copy(
                    source_ref.at[:, pl.ds(pl.multiple_of(start, 128), cols)],
                    held_ref.at[far, block * tokens : (block + 1) * tokens],
                    sems.at[far, block],
                )
            )
            copies[-1].start()
    for copy in list_copies:
        copy.wait()
    chosen = spread_column(list_refs[0][...].astype(F32), blocks, tokens <= 256).astype(jnp.int32)
    target = chosen + iota((rows, 1), 0) % (blocks * slots) // slots * tokens
    take = one_hot(target == iota((rows, blocks * tokens), 1))
    scale = spread_column(list_refs[1][...], blocks)
    for far, out_ref in enumerate((own_ref, other_ref)):
        for block in range(blocks):
            copies[far * blocks + block].wait()
        out_ref[...] = (dot(take, held_ref[far]) * scale).astype(BF16)


def pair_rows(source, picks, gates, blocks, after):
    slots, experts = picks.shape
    tokens, width = source.shape
    cols = width // (2 * blocks)
    rows = experts * blocks * slots
    return pl.pallas_call(
        functools.partial(pair_kernel, blocks),
        in_specs=[hbm()] * 4,
        out_specs=[vmem()] * 2,
        out_shape=[shape_of(rows, cols)] * 2,
        scratch_shapes=[
            pltpu.VMEM((2, blocks * tokens, cols), BF16),
            pltpu.SemaphoreType.DMA((2, blocks)),
            pltpu.SemaphoreType.DMA((2,)),
            pltpu.VMEM((slots, experts), picks.dtype),
            pltpu.VMEM((slots, experts), gates.dtype),
        ],
        compiler_params=params(16),
        cost_estimate=cost(4 * rows * cols * tokens * blocks, 2 * tokens * width),
        name="pair_rows",
    )(in_hbm(after), in_hbm(picks), in_hbm(gates), in_hbm(source))


def join_kernel(own_ref, other_ref, out_ref, sems):
    half = lax.axis_index("dp")
    copies = [
        pltpu.make_async_copy(own_ref, out_ref.at[:, half], sems.at[0]),
        pltpu.make_async_copy(other_ref, out_ref.at[:, 1 - half], sems.at[1]),
    ]
    for copy in copies:
        copy.start()
    for copy in copies:
        copy.wait()


def join_rows(own, other, experts):
    rows, cols = own.shape
    shape = (experts, rows // experts, cols)
    joined = pl.pallas_call(
        join_kernel,
        in_specs=[pl.BlockSpec(memory_space=pl.ANY)] * 2,
        out_specs=hbm(),
        out_shape=hbm_shape(experts, 2, *shape[1:]),
        scratch_shapes=[pltpu.SemaphoreType.DMA((2,))],
        compiler_params=params(16),
        cost_estimate=cost(0, 8 * rows * cols),
        name="join_rows",
    )(own.reshape(shape), other.reshape(shape))
    return joined.reshape(2 * rows, cols)


def send_rows(source, lists, halves, blocks):
    slots, experts = lists[0].shape
    tokens, width = source.shape
    cols = width // (halves * blocks)
    rows = halves * experts * blocks * slots
    return pl.pallas_call(
        functools.partial(send_kernel, halves, blocks, len(lists) == 2),
        in_specs=[hbm()] * (len(lists) + 1),
        out_specs=hbm(),
        out_shape=hbm_shape(rows, cols),
        scratch_shapes=[
            pltpu.VMEM((halves, blocks * tokens, cols), BF16),
            pltpu.VMEM((rows, cols), BF16),
            pltpu.SemaphoreType.DMA((halves, blocks)),
            pltpu.SemaphoreType.DMA((2,)),
            pltpu.SemaphoreType.DMA((halves, experts // planes_of(experts))),
        ]
        + [pltpu.VMEM((slots, experts), value.dtype) for value in lists],
        compiler_params=params(16),
        cost_estimate=cost(2 * rows * cols * tokens * blocks, 2 * tokens * width + 2 * rows * cols),
        name="send_rows",
    )(*[in_hbm(value) for value in lists], in_hbm(source))


def same_place(device):
    return device


def sort_matrix(rows, blocks, slots, back, place=same_place):
    a = iota((rows, rows), 1 if back else 0)
    b = iota((rows, rows), 0 if back else 1)
    group = rows // blocks
    return one_hot(place(a % group // slots) * (blocks * slots) + a // group * slots + a % slots == b)


def sort_rows(messages_ref, rows_ref, slots, place=same_place):
    blocks, total = rows_ref.shape[:2]
    if blocks == 1 and place is same_place:
        rows_ref[0] = messages_ref[...]
        return
    size = min(blocks * total, 256)
    group = size // blocks
    order = sort_matrix(size, blocks, slots, False, place)
    for part in range(total // group):
        ordered = dot(order, messages_ref[part * size : (part + 1) * size]).astype(BF16)
        for block in range(blocks):
            rows_ref[block, part * group : (part + 1) * group] = ordered[block * group : (block + 1) * group]


def unsort_rows(made, out_ref, slots, span=slice(None), place=same_place):
    blocks, total = len(made), made[0].shape[0]
    if blocks == 1 and place is same_place:
        out_ref[:, span] = made[0]
        return
    size = min(blocks * total, 256)
    group = size // blocks
    order = sort_matrix(size, blocks, slots, True, place)
    for part in range(total // group):
        stacked = jnp.concatenate([value[part * group : (part + 1) * group] for value in made], axis=0)
        out_ref[part * size : (part + 1) * size, span] = dot(order, stacked).astype(BF16)


def spans(ref, blocks):
    cols = ref // blocks
    return [slice(block * cols, (block + 1) * cols) for block in range(blocks)]


def added(terms):
    return functools.reduce(jnp.add, terms)


def pieces_of(width):
    if width % 256 or width <= 768:
        return [(0, width)]
    first = width // 2 // 256 * 256
    return [(0, first), (first, width - first)]


class Stream:
    def __init__(self, sems):
        self.sems, self.copies = sems, []

    def start(self, source, target):
        copy = pltpu.make_async_copy(source, target, self.sems.at[len(self.copies)])
        copy.start()
        self.copies.append(copy)
        return copy


def in_sums_kernel(slots, messages_ref, gate_ref, up_ref, out_ref, kept_ref, rows_ref, held_ref, acc_ref, sems):
    blocks, _, cols = rows_ref.shape
    hidden = gate_ref.shape[2]
    stream = Stream(sems)
    cuts = [(block, start, size) for block in range(blocks) for start, size in pieces_of(cols)]
    copies = []
    for block, start, size in cuts:
        span = slice(block * cols + start, block * cols + start + size)
        copies += [stream.start(ref.at[0, span], held_ref.at[i, span]) for i, ref in enumerate((gate_ref, up_ref))]
    sort_rows(messages_ref, rows_ref, slots)
    kept = stream.start(rows_ref, kept_ref)
    for number, (block, start, size) in enumerate(cuts):
        span = slice(block * cols + start, block * cols + start + size)
        for i in range(2):
            copies[2 * number + i].wait()
            term = dot(rows_ref[block, :, start : start + size], held_ref[i, span])
            acc_ref[i] = term if number == 0 else acc_ref[i] + term
    for i in range(2):
        out_ref[:, i * hidden : (i + 1) * hidden] = acc_ref[i].astype(BF16)
    kept.wait()


def in_sums(messages, w_gate, w_up, blocks, slots):
    part, hidden = w_gate.shape[1:]
    rows = messages.shape[0] // blocks
    cols = part // blocks
    return pl.pallas_call(
        functools.partial(in_sums_kernel, slots),
        in_specs=[vmem(), hbm(), hbm()],
        out_specs=[vmem(), hbm()],
        out_shape=[shape_of(rows, 2 * hidden), hbm_shape(blocks, rows, cols)],
        scratch_shapes=[
            pltpu.VMEM((blocks, rows, cols), BF16),
            pltpu.VMEM((2, part, hidden), BF16),
            pltpu.VMEM((2, rows, hidden), F32),
            pltpu.SemaphoreType.DMA((2 * blocks * len(pieces_of(cols)) + 1,)),
        ],
        compiler_params=params(),
        cost_estimate=cost(4 * rows * part * hidden, 4 * part * hidden),
        name="gate_up_sums",
    )(messages, in_hbm(w_gate), in_hbm(w_up))


def back_sums_kernel(slots, place, messages_ref, down_ref, out_ref, kept_ref, rows_ref, held_ref, acc_ref, sems):
    blocks, _, cols = rows_ref.shape
    stream = Stream(sems)
    cuts = [(block, start, size) for block in range(blocks) for start, size in pieces_of(cols)]
    copies = []
    for block, start, size in cuts:
        span = slice(block * cols + start, block * cols + start + size)
        copies.append(stream.start(down_ref.at[0, :, span], held_ref.at[:, span]))
    sort_rows(messages_ref, rows_ref, slots, place)
    kept = stream.start(rows_ref, kept_ref)
    for number, (block, start, size) in enumerate(cuts):
        span = slice(block * cols + start, block * cols + start + size)
        copies[number].wait()
        term = dot(rows_ref[block, :, start : start + size], held_ref[:, span], ((1,), (1,)))
        acc_ref[...] = term if number == 0 else acc_ref[...] + term
    out_ref[...] = acc_ref[...].astype(BF16)
    kept.wait()


def back_sums(messages, w_down, blocks, slots, place):
    hidden, part = w_down.shape[1:]
    rows = messages.shape[0] // blocks
    cols = part // blocks
    return pl.pallas_call(
        functools.partial(back_sums_kernel, slots, place),
        in_specs=[vmem(), hbm()],
        out_specs=[vmem(), hbm()],
        out_shape=[shape_of(rows, hidden), hbm_shape(blocks, rows, cols)],
        scratch_shapes=[
            pltpu.VMEM((blocks, rows, cols), BF16),
            pltpu.VMEM((hidden, part), BF16),
            pltpu.VMEM((rows, hidden), F32),
            pltpu.SemaphoreType.DMA((blocks * len(pieces_of(cols)) + 1,)),
        ],
        compiler_params=params(),
        cost_estimate=cost(2 * rows * part * hidden, 2 * part * hidden),
        name="back_sums",
    )(messages, in_hbm(w_down))


def bring_kernel(count, *refs):
    sources, targets, sems = refs[1 : count + 1], refs[count + 1 : 2 * count + 1], refs[-1]
    copies = [pltpu.make_async_copy(s, t, sems.at[i]) for i, (s, t) in enumerate(zip(sources, targets))]
    for copy in copies:
        copy.start()
    for copy in copies:
        copy.wait()


def bring(values, after):
    return pl.pallas_call(
        functools.partial(bring_kernel, len(values)),
        in_specs=[pl.BlockSpec(memory_space=pl.ANY)] + [hbm()] * len(values),
        out_specs=[vmem()] * len(values),
        out_shape=[shape_of(*value.shape) for value in values],
        scratch_shapes=[pltpu.SemaphoreType.DMA((len(values),))],
        compiler_params=params(16),
        cost_estimate=cost(0, 2 * sum(value.size for value in values)),
        name="bring_weights",
    )(after, *[in_hbm(value) for value in values])


def row_parts(total):
    size = min(total, 128)
    return [slice(start, start + size) for start in range(0, total, size)]


def summed(refs, rows, span):
    return added([ref[rows, span].astype(F32) for ref in refs])


def out_rows_kernel(slots, blocks, place, count, *refs):
    shares, (down_ref, act_ref, out_ref) = refs[:count], refs[count:]
    hidden, part = down_ref.shape[1:]
    for rows in row_parts(act_ref.shape[0]):
        gate_sum = summed(shares, rows, slice(0, hidden))
        up_sum = summed(shares, rows, slice(hidden, 2 * hidden))
        act_ref[rows] = (gate_sum * jax.nn.sigmoid(gate_sum) * up_sum).astype(BF16)
    made = [dot(act_ref[...], down_ref[0, :, span]).astype(BF16) for span in spans(part, blocks)]
    unsort_rows(made, out_ref, slots, place=place)


def out_rows(shares, w_down, blocks, slots, place):
    hidden, part = w_down.shape[1:]
    rows = shares[0].shape[0]
    return pl.pallas_call(
        functools.partial(out_rows_kernel, slots, blocks, place, len(shares)),
        in_specs=[vmem()] * (len(shares) + 1),
        out_specs=[vmem()] * 2,
        out_shape=[shape_of(rows, hidden), shape_of(blocks * rows, part // blocks)],
        compiler_params=params(),
        cost_estimate=cost(2 * rows * part * hidden, 2 * part * hidden),
        name="output_rows",
    )(*shares, w_down)


def grad_rows_kernel(slots, blocks, count, *refs):
    shares, backs = refs[:count], refs[count : 2 * count]
    gate_ref, up_ref, kept_ref, out_ref, act_ref, sem = refs[2 * count :]
    part, hidden = gate_ref.shape[1:]
    cols = part // blocks
    for rows in row_parts(act_ref.shape[0]):
        gate_sum = summed(shares, rows, slice(0, hidden))
        up_sum = summed(shares, rows, slice(hidden, 2 * hidden))
        back_sum = summed(backs, rows, slice(0, hidden))
        sig = jax.nn.sigmoid(gate_sum)
        act_ref[rows, :hidden] = (back_sum * up_sum * sig * (1.0 + gate_sum * (1.0 - sig))).astype(BF16)
        act_ref[rows, hidden:] = (back_sum * (gate_sum * sig)).astype(BF16)
    kept = pltpu.make_async_copy(act_ref, kept_ref, sem)
    kept.start()
    for start, size in pieces_of(cols):
        made = []
        for block in range(blocks):
            span = slice(block * cols + start, block * cols + start + size)
            total = dot(act_ref[:, :hidden], gate_ref[0, span, :], ((1,), (1,)))
            total = total + dot(act_ref[:, hidden:], up_ref[0, span, :], ((1,), (1,)))
            made.append(total.astype(BF16))
        unsort_rows(made, out_ref, slots, slice(start, start + size))
    kept.wait()


def grad_rows(shares, backs, w_gate, w_up, blocks, slots):
    part, hidden = w_gate.shape[1:]
    rows = shares[0].shape[0]
    cols = part // blocks
    return pl.pallas_call(
        functools.partial(grad_rows_kernel, slots, blocks, len(shares)),
        in_specs=[vmem()] * (2 * len(shares) + 2),
        out_specs=[hbm(), vmem()],
        out_shape=[hbm_shape(rows, 2 * hidden), shape_of(blocks * rows, cols)],
        scratch_shapes=[pltpu.VMEM((rows, 2 * hidden), BF16), pltpu.SemaphoreType.DMA],
        compiler_params=params(32),
        cost_estimate=cost(4 * rows * part * hidden, 4 * part * hidden),
        name="gradient_rows",
    )(*shares, *backs, w_gate, w_up)


def weights_kernel(rows_in_ref, rows_up_ref, act_ref, grad_act_ref, gate_ref, up_ref, down_ref):
    hidden = gate_ref.shape[2]
    rows_in = rows_in_ref[0]
    gate_ref[0] = dot(rows_in, grad_act_ref[:, :hidden], ((0,), (0,))).astype(BF16)
    up_ref[0] = dot(rows_in, grad_act_ref[:, hidden:], ((0,), (0,))).astype(BF16)
    down_ref[0] = dot(act_ref[...], rows_up_ref[0], ((0,), (0,))).astype(BF16)


def weight_grads(rows_in, rows_up, act, grad_act):
    blocks, total, width = rows_in.shape
    part = blocks * width
    hidden = act.shape[1]
    cols = block_of(width, 640)
    steps = width // cols
    chunk = pl.BlockSpec((1, total, cols), lambda k, b: (k, 0, b))
    tall = pl.BlockSpec((1, cols, hidden), lambda k, b: (0, k * steps + b, 0))
    return pl.pallas_call(
        weights_kernel,
        grid=(blocks, steps),
        in_specs=[
            chunk,
            chunk,
            pl.BlockSpec((total, hidden), lambda k, b: (0, 0)),
            pl.BlockSpec((total, 2 * hidden), lambda k, b: (0, 0)),
        ],
        out_specs=[tall, tall, pl.BlockSpec((1, hidden, cols), lambda k, b: (0, 0, k * steps + b))],
        out_shape=[shape_of(1, part, hidden), shape_of(1, part, hidden), shape_of(1, hidden, part)],
        compiler_params=params(),
        cost_estimate=cost(6 * total * part * hidden, 6 * part * hidden),
        name="weight_grads",
    )(*[in_hbm(value) for value in (rows_in, rows_up, act, grad_act)])


def back_rows(back_ref, half, halves, run):
    total = back_ref.shape[0]
    return jnp.concatenate([back_ref[start : start + run] for start in range(half * run, total, halves * run)], axis=0)


def put_columns(held_ref, target_ref, sems, half, block, start=None):
    blocks, _, cols = held_ref.shape[1:]
    start = (half * blocks + block) * cols if start is None else start
    copy = pltpu.make_async_copy(held_ref.at[half, block], target_ref.at[:, pl.ds(start, cols)], sems.at[half, block])
    copy.start()
    return copy


def mixed_kernel(picks_ref, gates_ref, cot_ref, back_ref, mixed_ref, gate_grad_ref, put_ref, held_ref, sems):
    slots, experts = picks_ref.shape
    halves, blocks, tokens, cols = held_ref.shape
    rows = experts * blocks * slots
    hit = spread_row(picks_ref[...].astype(F32), blocks).astype(jnp.int32) == iota((tokens, rows), 0)
    scale = spread_row(gates_ref[...], blocks)
    of_block = iota((tokens, rows), 1) % (blocks * slots) // slots
    run = planes_of(experts) * blocks * slots
    backs = [back_rows(back_ref, half, halves, run) for half in range(halves)]
    copies = []
    products = None
    for block in range(blocks):
        inside = hit & (of_block == block)
        put_ref[block] = one_hot(inside)
        rest = jnp.where(inside, scale, 0.0)
        pieces = []
        for _ in range(3):
            pieces.append(rest.astype(BF16))
            rest = rest - pieces[-1].astype(F32)
        for half in range(halves):
            back = backs[half]
            held_ref[half, block] = added([dot(piece, back) for piece in pieces]).astype(BF16)
            copies.append(put_columns(held_ref, mixed_ref, sems, half, block))
            place = half * blocks + block
            product = dot(cot_ref[:, place * cols : (place + 1) * cols], back, ((1,), (1,)))
            product = jnp.where(inside, product, 0.0)
            products = product if products is None else products + product
    values = jnp.sum(products, axis=0, keepdims=True)
    mine = iota((slots, rows), 1) % slots == iota((slots, rows), 0)
    owner = (expert_at(iota((rows, experts), 0) // (blocks * slots), experts) == iota((rows, experts), 1)).astype(F32)
    gate_grad_ref[...] = exact_dot(jnp.where(mine, values, 0.0), owner)
    for copy in copies:
        copy.wait()


def mix_rows(back, cotangent, picks, gates, halves, blocks):
    slots, experts = picks.shape
    tokens, width = cotangent.shape
    cols = width // (halves * blocks)
    rows = experts * blocks * slots
    return pl.pallas_call(
        mixed_kernel,
        in_specs=[vmem()] * 4,
        out_specs=[hbm(), vmem(), vmem()],
        out_shape=[shape_of(tokens, width), shape_of(slots, experts, dtype=F32), shape_of(blocks, tokens, rows)],
        scratch_shapes=[pltpu.VMEM((halves, blocks, tokens, cols), BF16), pltpu.SemaphoreType.DMA((halves, blocks))],
        compiler_params=params(16),
        cost_estimate=cost(8 * rows * tokens * width, 4 * tokens * width),
        name="mixed_rows",
    )(picks, gates, cotangent, back)


def mix_half(half, put_ref, pieces_ref, cot_ref, back_ref, target_ref, held_ref, sems):
    blocks, tokens, cols = held_ref.shape
    back = back_ref[...]
    copies = []
    products = None
    for block in range(blocks):
        start = pl.multiple_of((half * blocks + block) * cols, 128)
        held_ref[block] = added([dot(pieces_ref[block, i], back) for i in range(3)]).astype(BF16)
        copies.append(pltpu.make_async_copy(held_ref.at[block], target_ref.at[:, pl.ds(start, cols)], sems.at[block]))
        copies[-1].start()
        product = dot(cot_ref[:, pl.ds(start, cols)], back, ((1,), (1,))) * put_ref[block].astype(F32)
        products = product if products is None else products + product
    return jnp.sum(products, axis=0, keepdims=True), copies


def near_kernel(picks_ref, gates_ref, cot_ref, back_ref, mixed_ref, put_ref, pieces_ref, sums_ref, held_ref, sems):
    slots = picks_ref.shape[0]
    blocks, tokens, rows = put_ref.shape
    hit = spread_row(picks_ref[...].astype(F32), blocks).astype(jnp.int32) == iota((tokens, rows), 0)
    scale = spread_row(gates_ref[...], blocks)
    of_block = iota((tokens, rows), 1) % (blocks * slots) // slots
    for block in range(blocks):
        inside = hit & (of_block == block)
        put_ref[block] = one_hot(inside)
        rest = jnp.where(inside, scale, 0.0)
        for i in range(3):
            piece = rest.astype(BF16)
            pieces_ref[block, i] = piece
            rest = rest - piece.astype(F32)
    half = lax.axis_index("dp")
    sums_ref[...], copies = mix_half(half, put_ref, pieces_ref, cot_ref, back_ref, mixed_ref, held_ref, sems)
    for copy in copies:
        copy.wait()


def far_kernel(
    slots, put_ref, pieces_ref, sums_ref, cot_ref, back_ref, _, mixed_ref, gate_grad_ref, held_ref, sems
):
    blocks, _, rows = put_ref.shape
    experts = gate_grad_ref.shape[1]
    half = 1 - lax.axis_index("dp")
    values, copies = mix_half(half, put_ref, pieces_ref, cot_ref, back_ref, mixed_ref, held_ref, sems)
    values = values + sums_ref[...]
    mine = iota((slots, rows), 1) % slots == iota((slots, rows), 0)
    owner = (expert_at(iota((rows, experts), 0) // (blocks * slots), experts) == iota((rows, experts), 1)).astype(F32)
    gate_grad_ref[...] = exact_dot(jnp.where(mine, values, 0.0), owner)
    for copy in copies:
        copy.wait()


def mix_halves(own, other, cotangent, picks, gates, blocks):
    slots, experts = picks.shape
    tokens, width = cotangent.shape
    rows, cols = own.shape
    scratch = [pltpu.VMEM((blocks, tokens, cols), BF16), pltpu.SemaphoreType.DMA((blocks,))]
    work = cost(4 * rows * tokens * width, 2 * tokens * width)
    mixed, put, pieces, sums = pl.pallas_call(
        near_kernel,
        in_specs=[vmem()] * 4,
        out_specs=[hbm()] + [vmem()] * 3,
        out_shape=[
            hbm_shape(tokens, width),
            shape_of(blocks, tokens, rows),
            shape_of(blocks, 3, tokens, rows),
            shape_of(1, rows, dtype=F32),
        ],
        scratch_shapes=scratch,
        compiler_params=params(16),
        cost_estimate=work,
        name="mixed_near",
    )(picks, gates, cotangent, own)
    mixed, gate_grad = pl.pallas_call(
        functools.partial(far_kernel, slots),
        in_specs=[vmem()] * 5 + [hbm()],
        out_specs=[hbm(), vmem()],
        out_shape=[hbm_shape(tokens, width), shape_of(slots, experts, dtype=F32)],
        scratch_shapes=scratch,
        input_output_aliases={5: 0},
        compiler_params=params(16),
        cost_estimate=work,
        name="mixed_far",
    )(put, pieces, sums, cotangent, other, in_hbm(mixed))
    return mixed, gate_grad, put


def part_kernel(joined_ref, own_ref, other_ref, sems):
    half = lax.axis_index("dp")
    copies = [
        pltpu.make_async_copy(joined_ref.at[:, half], own_ref, sems.at[0]),
        pltpu.make_async_copy(joined_ref.at[:, 1 - half], other_ref, sems.at[1]),
    ]
    for copy in copies:
        copy.start()
    for copy in copies:
        copy.wait()


def part_rows(joined, experts):
    rows, cols = joined.shape
    shape = (experts, rows // (2 * experts), cols)
    parted = pl.pallas_call(
        part_kernel,
        in_specs=[pl.BlockSpec(memory_space=pl.ANY)],
        out_specs=[pl.BlockSpec(memory_space=pl.ANY)] * 2,
        out_shape=[shape_of(*shape)] * 2,
        scratch_shapes=[pltpu.SemaphoreType.DMA((2,))],
        compiler_params=params(16),
        cost_estimate=cost(0, 4 * rows * cols),
        name="part_rows",
    )(joined.reshape(experts, 2, *shape[1:]))
    return [value.reshape(rows // 2, cols) for value in parted]


def token_grad_kernel(run, _, put_ref, back_ref, grad_ref, held_ref, sems):
    halves, blocks = held_ref.shape[:2]
    copies = []
    for half in range(halves):
        back = back_rows(back_ref, half, halves, run)
        for block in range(blocks):
            held_ref[half, block] = dot(put_ref[block], back).astype(BF16)
            copies.append(put_columns(held_ref, grad_ref, sems, half, block))
    for copy in copies:
        copy.wait()


def token_grads(back, put, halves, run, after):
    blocks, tokens, rows = put.shape
    cols = back.shape[1]
    width = halves * blocks * cols
    return pl.pallas_call(
        functools.partial(token_grad_kernel, run),
        in_specs=[hbm()] + [vmem()] * 2,
        out_specs=hbm(),
        out_shape=shape_of(tokens, width),
        scratch_shapes=[pltpu.VMEM((halves, blocks, tokens, cols), BF16), pltpu.SemaphoreType.DMA((halves, blocks))],
        compiler_params=params(16),
        cost_estimate=cost(2 * rows * tokens * width, 2 * tokens * width),
        name="token_grads",
    )(in_hbm(after), put, back)


def to_owners(halves, experts, messages):
    planes = planes_of(experts)
    order = [
        half * experts + plane * (experts // planes) + place
        for place in range(experts // planes)
        for half in range(halves)
        for plane in range(planes)
    ]
    return lax.all_to_all(
        messages, EVERYONE, split_axis=0, concat_axis=0, tiled=True, axis_index_groups=[order]
    )


def to_experts(experts, messages):
    order = [expert_at(place, experts) for place in range(experts)]
    return lax.all_to_all(messages, "expert", split_axis=0, concat_axis=0, tiled=True, axis_index_groups=[order])


def dp_shares(own, halves):
    shares = [own] + [
        lax.ppermute(own, "dp", [(i, (i + shift) % halves) for i in range(halves)]) for shift in range(1, halves)
    ]
    return shares if halves <= 2 else [added([share.astype(F32) for share in shares])]


def body(halves, tokens, cotangent, picks, gates, w_gate, w_up, w_down):
    experts, slots = picks.shape[1:]
    scatter = functools.partial(to_owners, halves, experts)
    blocks = 2 if tokens.shape[1] // halves % 256 == 0 else 1
    picks_t = picks[0].T
    gates_t = gates[0].T
    messages_in = send_rows(tokens, (picks_t,), halves, blocks)
    arrived_in = scatter(messages_in)
    if halves == 2:
        own, other = pair_rows(cotangent, picks_t, gates_t, blocks, messages_in)
        other = lax.ppermute(other, "dp", [(0, 1), (1, 0)])
        arrived_up = to_experts(experts, join_rows(own, other, experts))
    else:
        arrived_up = scatter(send_rows(cotangent, (picks_t, gates_t), halves, blocks))
    own_sums, rows_in = in_sums(arrived_in, w_gate, w_up, blocks, slots)
    shares = dp_shares(own_sums, halves)
    place = functools.partial(split_place, halves=2, planes=planes_of(experts)) if halves == 2 else same_place
    act, outputs = out_rows(shares, w_down, blocks, slots, place)
    back_out = to_experts(experts, outputs) if halves == 2 else scatter(outputs)
    own_back, rows_up = back_sums(arrived_up, w_down, blocks, slots, place)
    backs = dp_shares(own_back, halves)
    near_gate, near_up = bring((w_gate, w_up), own_back)
    grad_act, gradients = grad_rows(shares, backs, near_gate, near_up, blocks, slots)
    back_grad = scatter(gradients)
    grad_gate_w, grad_up_w, grad_down = weight_grads(rows_in, rows_up, act, grad_act)
    if halves == 2:
        own_out, other_out = part_rows(back_out, experts)
        other_out = lax.ppermute(other_out, "dp", [(0, 1), (1, 0)])
        mixed, gate_grad, put = mix_halves(own_out, other_out, cotangent, picks_t, gates_t, blocks)
    else:
        mixed, gate_grad, put = mix_rows(back_out, cotangent, picks_t, gates_t, halves, blocks)
    token_grad = token_grads(back_grad, put, halves, planes_of(experts) * blocks * slots, gate_grad)
    return mixed, token_grad, gate_grad.T[None], grad_gate_w, grad_up_w, grad_down


def solution(mesh):
    rows = P(("dp", "expert"), None)
    lists = P(("dp", "expert"), None, None)
    tall = P("expert", "dp", None)
    wide = P("expert", None, "dp")
    return jax.shard_map(
        functools.partial(body, mesh.shape["dp"]),
        mesh=mesh,
        in_specs=(rows, rows, lists, lists, tall, tall, wide),
        out_specs=(rows, rows, lists, tall, tall, wide),
        check_vma=False,
    )
```

```python
import functools

import jax
import jax.numpy as jnp
from jax import lax
from jax.experimental import pallas as pl
from jax.experimental.pallas import tpu as pltpu
from jax.sharding import PartitionSpec as P

F32 = jnp.float32
BF16 = jnp.bfloat16
MIB = 1024 * 1024
EVERYONE = ("dp", "expert")


def dot(left, right, dims=((1,), (0,)), precision=None):
    return lax.dot_general(left, right, (dims, ((), ())), precision=precision, preferred_element_type=F32)


def exact_dot(left, right, dims=((1,), (0,))):
    return dot(left, right, dims, lax.Precision.HIGHEST)


def iota(shape, axis):
    return lax.broadcasted_iota(jnp.int32, shape, axis)


def planes_of(experts):
    return experts // 4 if experts % 4 == 0 else 1


def expert_at(place, experts):
    planes = planes_of(experts)
    return place % planes * (experts // planes) + place // planes


def split_place(place, halves, planes):
    return (place // (halves * planes) * planes + place % planes) * halves + place // planes % halves


def one_hot(condition):
    return jnp.where(condition, 1.0, 0.0).astype(BF16)


def vmem():
    return pl.BlockSpec(memory_space=pltpu.VMEM)


def hbm():
    return pl.BlockSpec(memory_space=pltpu.HBM)


def in_hbm(value):
    return pltpu.with_memory_space_constraint(value, pltpu.HBM)


def shape_of(*sizes, dtype=BF16):
    return jax.ShapeDtypeStruct(sizes, dtype)


def hbm_shape(*sizes):
    return pltpu.HBM(sizes, BF16)


def params(mib=24):
    return pltpu.CompilerParams(vmem_limit_bytes=mib * MIB)


def cost(flops, moved):
    return pl.CostEstimate(flops=flops, bytes_accessed=moved, transcendentals=0)


def block_of(width, limit):
    best = 128
    for size in range(128, limit + 1, 128):
        if width % size == 0:
            best = size
    return best


def spread_column(values, blocks, plain=False):
    slots, experts = values.shape
    rows = experts * blocks * slots
    owner = (expert_at(iota((rows, experts), 0) // (blocks * slots), experts) == iota((rows, experts), 1)).astype(F32)
    if plain:
        wide = dot(owner.astype(BF16), values.astype(BF16), ((1,), (1,)))
    else:
        wide = exact_dot(owner, values, ((1,), (1,)))
    mine = iota((rows, slots), 0) % slots == iota((rows, slots), 1)
    return jnp.sum(jnp.where(mine, wide, 0.0), axis=1, keepdims=True)


def spread_row(values, blocks):
    slots, experts = values.shape
    rows = experts * blocks * slots
    owner = (expert_at(iota((experts, rows), 1) // (blocks * slots), experts) == iota((experts, rows), 0)).astype(F32)
    wide = exact_dot(values, owner)
    mine = iota((slots, rows), 1) % slots == iota((slots, rows), 0)
    return jnp.sum(jnp.where(mine, wide, 0.0), axis=0, keepdims=True)


def send_kernel(halves, blocks, scaled, *refs):
    count = 2 if scaled else 1
    lists, source_ref, out_ref = refs[:count], refs[count], refs[count + 1]
    held_ref, made_ref, sems, list_sems, out_sems = refs[count + 2 : count + 7]
    list_refs = refs[count + 7 :]
    rows, cols = out_ref.shape
    rows = rows // halves
    tokens = source_ref.shape[0]
    list_copies = [
        pltpu.make_async_copy(ref, target, list_sems.at[i]) for i, (ref, target) in enumerate(zip(lists, list_refs))
    ]
    copies = []
    for copy in list_copies:
        copy.start()
    for half in range(halves):
        for block in range(blocks):
            place = half * blocks + block
            copies.append(
                pltpu.make_async_copy(
                    source_ref.at[:, place * cols : (place + 1) * cols],
                    held_ref.at[half, block * tokens : (block + 1) * tokens],
                    sems.at[half, block],
                )
            )
            copies[-1].start()
    for copy in list_copies:
        copy.wait()
    slots, experts = list_refs[0].shape
    run = planes_of(experts) * blocks * slots
    chosen = spread_column(list_refs[0][...].astype(F32), blocks, tokens <= 256).astype(jnp.int32)
    target = chosen + iota((rows, 1), 0) % (blocks * slots) // slots * tokens
    take = one_hot(target == iota((rows, blocks * tokens), 1))
    scale = spread_column(list_refs[1][...], blocks) if scaled else None
    out_copies = []
    for half in range(halves):
        for block in range(blocks):
            copies[half * blocks + block].wait()
        picked = dot(take, held_ref[half])
        if scaled:
            picked = picked * scale
        picked = picked.astype(BF16)
        for place in range(rows // run):
            start = (place * halves + half) * run
            made_ref[start : start + run] = picked[place * run : (place + 1) * run]
            out_copies.append(
                pltpu.make_async_copy(
                    made_ref.at[start : start + run], out_ref.at[start : start + run], out_sems.at[half, place]
                )
            )
            out_copies[-1].start()
    for copy in out_copies:
        copy.wait()


def side_kernel(blocks, far, _, picks_ref, gates_ref, source_ref, out_ref, held_ref, sems, list_sems, *list_refs):
    slots = picks_ref.shape[0]
    tokens = source_ref.shape[0]
    rows, cols = out_ref.shape
    half = lax.axis_index("dp")
    list_copies = [
        pltpu.make_async_copy(ref, target, list_sems.at[i])
        for i, (ref, target) in enumerate(zip((picks_ref, gates_ref), list_refs))
    ]
    for copy in list_copies:
        copy.start()
    copies = []
    for block in range(blocks):
        start = (jnp.bitwise_xor(half, far) * blocks + block) * cols
        copies.append(
            pltpu.make_async_copy(
                source_ref.at[:, pl.ds(pl.multiple_of(start, 128), cols)],
                held_ref.at[block * tokens : (block + 1) * tokens],
                sems.at[block],
            )
        )
        copies[-1].start()
    for copy in list_copies:
        copy.wait()
    chosen = spread_column(list_refs[0][...].astype(F32), blocks, tokens <= 256).astype(jnp.int32)
    target = chosen + iota((rows, 1), 0) % (blocks * slots) // slots * tokens
    take = one_hot(target == iota((rows, blocks * tokens), 1))
    scale = spread_column(list_refs[1][...], blocks)
    for copy in copies:
        copy.wait()
    out_ref[...] = (dot(take, held_ref[...]) * scale).astype(BF16)


def side_rows(source, picks, gates, blocks, far, after):
    slots, experts = picks.shape
    tokens, width = source.shape
    cols = width // (2 * blocks)
    rows = experts * blocks * slots
    return pl.pallas_call(
        functools.partial(side_kernel, blocks, far),
        in_specs=[hbm()] * 4,
        out_specs=vmem(),
        out_shape=shape_of(rows, cols),
        scratch_shapes=[
            pltpu.VMEM((blocks * tokens, cols), BF16),
            pltpu.SemaphoreType.DMA((blocks,)),
            pltpu.SemaphoreType.DMA((2,)),
            pltpu.VMEM((slots, experts), picks.dtype),
            pltpu.VMEM((slots, experts), gates.dtype),
        ],
        compiler_params=params(16),
        cost_estimate=cost(2 * rows * cols * tokens * blocks, tokens * width),
        name="side_rows",
    )(in_hbm(after), in_hbm(picks), in_hbm(gates), in_hbm(source))


def join_kernel(own_ref, other_ref, out_ref, sems):
    half = lax.axis_index("dp")
    copies = [
        pltpu.make_async_copy(own_ref, out_ref.at[:, half], sems.at[0]),
        pltpu.make_async_copy(other_ref, out_ref.at[:, 1 - half], sems.at[1]),
    ]
    for copy in copies:
        copy.start()
    for copy in copies:
        copy.wait()


def join_rows(own, other, experts):
    rows, cols = own.shape
    shape = (experts, rows // experts, cols)
    joined = pl.pallas_call(
        join_kernel,
        in_specs=[pl.BlockSpec(memory_space=pl.ANY)] * 2,
        out_specs=hbm(),
        out_shape=hbm_shape(experts, 2, *shape[1:]),
        scratch_shapes=[pltpu.SemaphoreType.DMA((2,))],
        compiler_params=params(16),
        cost_estimate=cost(0, 8 * rows * cols),
        name="join_rows",
    )(own.reshape(shape), other.reshape(shape))
    return joined.reshape(2 * rows, cols)


def send_rows(source, lists, halves, blocks):
    slots, experts = lists[0].shape
    tokens, width = source.shape
    cols = width // (halves * blocks)
    rows = halves * experts * blocks * slots
    return pl.pallas_call(
        functools.partial(send_kernel, halves, blocks, len(lists) == 2),
        in_specs=[hbm()] * (len(lists) + 1),
        out_specs=hbm(),
        out_shape=hbm_shape(rows, cols),
        scratch_shapes=[
            pltpu.VMEM((halves, blocks * tokens, cols), BF16),
            pltpu.VMEM((rows, cols), BF16),
            pltpu.SemaphoreType.DMA((halves, blocks)),
            pltpu.SemaphoreType.DMA((2,)),
            pltpu.SemaphoreType.DMA((halves, experts // planes_of(experts))),
        ]
        + [pltpu.VMEM((slots, experts), value.dtype) for value in lists],
        compiler_params=params(16),
        cost_estimate=cost(2 * rows * cols * tokens * blocks, 2 * tokens * width + 2 * rows * cols),
        name="send_rows",
    )(*[in_hbm(value) for value in lists], in_hbm(source))


def same_place(device):
    return device


def sort_matrix(rows, blocks, slots, back, place=same_place):
    a = iota((rows, rows), 1 if back else 0)
    b = iota((rows, rows), 0 if back else 1)
    group = rows // blocks
    return one_hot(place(a % group // slots) * (blocks * slots) + a // group * slots + a % slots == b)


def sort_rows(messages_ref, rows_ref, slots, place=same_place):
    blocks, total = rows_ref.shape[:2]
    if blocks == 1 and place is same_place:
        rows_ref[0] = messages_ref[...]
        return
    size = min(blocks * total, 256)
    group = size // blocks
    order = sort_matrix(size, blocks, slots, False, place)
    for part in range(total // group):
        ordered = dot(order, messages_ref[part * size : (part + 1) * size]).astype(BF16)
        for block in range(blocks):
            rows_ref[block, part * group : (part + 1) * group] = ordered[block * group : (block + 1) * group]


def unsort_rows(made, out_ref, slots, span=slice(None), place=same_place):
    blocks, total = len(made), made[0].shape[0]
    if blocks == 1 and place is same_place:
        out_ref[:, span] = made[0]
        return
    size = min(blocks * total, 256)
    group = size // blocks
    order = sort_matrix(size, blocks, slots, True, place)
    for part in range(total // group):
        stacked = jnp.concatenate([value[part * group : (part + 1) * group] for value in made], axis=0)
        out_ref[part * size : (part + 1) * size, span] = dot(order, stacked).astype(BF16)


def spans(ref, blocks):
    cols = ref // blocks
    return [slice(block * cols, (block + 1) * cols) for block in range(blocks)]


def added(terms):
    return functools.reduce(jnp.add, terms)


def pieces_of(width):
    if width % 256 or width <= 768:
        return [(0, width)]
    first = width // 2 // 256 * 256
    return [(0, first), (first, width - first)]


class Stream:
    def __init__(self, sems):
        self.sems, self.copies = sems, []

    def start(self, source, target):
        copy = pltpu.make_async_copy(source, target, self.sems.at[len(self.copies)])
        copy.start()
        self.copies.append(copy)
        return copy


def in_sums_kernel(slots, messages_ref, gate_ref, up_ref, out_ref, kept_ref, rows_ref, held_ref, acc_ref, sems):
    blocks, _, cols = rows_ref.shape
    hidden = gate_ref.shape[2]
    stream = Stream(sems)
    cuts = [(block, start, size) for block in range(blocks) for start, size in pieces_of(cols)]
    copies = []
    for block, start, size in cuts:
        span = slice(block * cols + start, block * cols + start + size)
        copies += [stream.start(ref.at[0, span], held_ref.at[i, span]) for i, ref in enumerate((gate_ref, up_ref))]
    sort_rows(messages_ref, rows_ref, slots)
    kept = stream.start(rows_ref, kept_ref)
    for number, (block, start, size) in enumerate(cuts):
        span = slice(block * cols + start, block * cols + start + size)
        for i in range(2):
            copies[2 * number + i].wait()
            term = dot(rows_ref[block, :, start : start + size], held_ref[i, span])
            acc_ref[i] = term if number == 0 else acc_ref[i] + term
    for i in range(2):
        out_ref[:, i * hidden : (i + 1) * hidden] = acc_ref[i].astype(BF16)
    kept.wait()


def in_sums(messages, w_gate, w_up, blocks, slots):
    part, hidden = w_gate.shape[1:]
    rows = messages.shape[0] // blocks
    cols = part // blocks
    return pl.pallas_call(
        functools.partial(in_sums_kernel, slots),
        in_specs=[vmem(), hbm(), hbm()],
        out_specs=[vmem(), hbm()],
        out_shape=[shape_of(rows, 2 * hidden), hbm_shape(blocks, rows, cols)],
        scratch_shapes=[
            pltpu.VMEM((blocks, rows, cols), BF16),
            pltpu.VMEM((2, part, hidden), BF16),
            pltpu.VMEM((2, rows, hidden), F32),
            pltpu.SemaphoreType.DMA((2 * blocks * len(pieces_of(cols)) + 1,)),
        ],
        compiler_params=params(),
        cost_estimate=cost(4 * rows * part * hidden, 4 * part * hidden),
        name="gate_up_sums",
    )(messages, in_hbm(w_gate), in_hbm(w_up))


def back_sums_kernel(slots, place, messages_ref, down_ref, out_ref, kept_ref, rows_ref, held_ref, acc_ref, sems):
    blocks, _, cols = rows_ref.shape
    stream = Stream(sems)
    cuts = [(block, start, size) for block in range(blocks) for start, size in pieces_of(cols)]
    copies = []
    for block, start, size in cuts:
        span = slice(block * cols + start, block * cols + start + size)
        copies.append(stream.start(down_ref.at[0, :, span], held_ref.at[:, span]))
    sort_rows(messages_ref, rows_ref, slots, place)
    kept = stream.start(rows_ref, kept_ref)
    for number, (block, start, size) in enumerate(cuts):
        span = slice(block * cols + start, block * cols + start + size)
        copies[number].wait()
        term = dot(rows_ref[block, :, start : start + size], held_ref[:, span], ((1,), (1,)))
        acc_ref[...] = term if number == 0 else acc_ref[...] + term
    out_ref[...] = acc_ref[...].astype(BF16)
    kept.wait()


def back_sums(messages, w_down, blocks, slots, place):
    hidden, part = w_down.shape[1:]
    rows = messages.shape[0] // blocks
    cols = part // blocks
    return pl.pallas_call(
        functools.partial(back_sums_kernel, slots, place),
        in_specs=[vmem(), hbm()],
        out_specs=[vmem(), hbm()],
        out_shape=[shape_of(rows, hidden), hbm_shape(blocks, rows, cols)],
        scratch_shapes=[
            pltpu.VMEM((blocks, rows, cols), BF16),
            pltpu.VMEM((hidden, part), BF16),
            pltpu.VMEM((rows, hidden), F32),
            pltpu.SemaphoreType.DMA((blocks * len(pieces_of(cols)) + 1,)),
        ],
        compiler_params=params(),
        cost_estimate=cost(2 * rows * part * hidden, 2 * part * hidden),
        name="back_sums",
    )(messages, in_hbm(w_down))


def bring_kernel(count, *refs):
    sources, targets, sems = refs[1 : count + 1], refs[count + 1 : 2 * count + 1], refs[-1]
    copies = [pltpu.make_async_copy(s, t, sems.at[i]) for i, (s, t) in enumerate(zip(sources, targets))]
    for copy in copies:
        copy.start()
    for copy in copies:
        copy.wait()


def bring(values, after):
    return pl.pallas_call(
        functools.partial(bring_kernel, len(values)),
        in_specs=[pl.BlockSpec(memory_space=pl.ANY)] + [hbm()] * len(values),
        out_specs=[vmem()] * len(values),
        out_shape=[shape_of(*value.shape) for value in values],
        scratch_shapes=[pltpu.SemaphoreType.DMA((len(values),))],
        compiler_params=params(16),
        cost_estimate=cost(0, 2 * sum(value.size for value in values)),
        name="bring_weights",
    )(after, *[in_hbm(value) for value in values])


def row_parts(total):
    size = min(total, 128)
    return [slice(start, start + size) for start in range(0, total, size)]


def summed(refs, rows, span):
    return added([ref[rows, span].astype(F32) for ref in refs])


def out_rows_kernel(slots, blocks, place, count, *refs):
    shares, (down_ref, act_ref, out_ref) = refs[:count], refs[count:]
    hidden, part = down_ref.shape[1:]
    for rows in row_parts(act_ref.shape[0]):
        gate_sum = summed(shares, rows, slice(0, hidden))
        up_sum = summed(shares, rows, slice(hidden, 2 * hidden))
        act_ref[rows] = (gate_sum * jax.nn.sigmoid(gate_sum) * up_sum).astype(BF16)
    made = [dot(act_ref[...], down_ref[0, :, span]).astype(BF16) for span in spans(part, blocks)]
    unsort_rows(made, out_ref, slots, place=place)


def out_rows(shares, w_down, blocks, slots, place):
    hidden, part = w_down.shape[1:]
    rows = shares[0].shape[0]
    return pl.pallas_call(
        functools.partial(out_rows_kernel, slots, blocks, place, len(shares)),
        in_specs=[vmem()] * (len(shares) + 1),
        out_specs=[vmem()] * 2,
        out_shape=[shape_of(rows, hidden), shape_of(blocks * rows, part // blocks)],
        compiler_params=params(),
        cost_estimate=cost(2 * rows * part * hidden, 2 * part * hidden),
        name="output_rows",
    )(*shares, w_down)


def grad_rows_kernel(slots, blocks, count, *refs):
    shares, backs = refs[:count], refs[count : 2 * count]
    gate_ref, up_ref, kept_ref, out_ref, act_ref, sem = refs[2 * count :]
    part, hidden = gate_ref.shape[1:]
    cols = part // blocks
    for rows in row_parts(act_ref.shape[0]):
        gate_sum = summed(shares, rows, slice(0, hidden))
        up_sum = summed(shares, rows, slice(hidden, 2 * hidden))
        back_sum = summed(backs, rows, slice(0, hidden))
        sig = jax.nn.sigmoid(gate_sum)
        act_ref[rows, :hidden] = (back_sum * up_sum * sig * (1.0 + gate_sum * (1.0 - sig))).astype(BF16)
        act_ref[rows, hidden:] = (back_sum * (gate_sum * sig)).astype(BF16)
    kept = pltpu.make_async_copy(act_ref, kept_ref, sem)
    kept.start()
    for start, size in pieces_of(cols):
        made = []
        for block in range(blocks):
            span = slice(block * cols + start, block * cols + start + size)
            total = dot(act_ref[:, :hidden], gate_ref[0, span, :], ((1,), (1,)))
            total = total + dot(act_ref[:, hidden:], up_ref[0, span, :], ((1,), (1,)))
            made.append(total.astype(BF16))
        unsort_rows(made, out_ref, slots, slice(start, start + size))
    kept.wait()


def grad_rows(shares, backs, w_gate, w_up, blocks, slots):
    part, hidden = w_gate.shape[1:]
    rows = shares[0].shape[0]
    cols = part // blocks
    return pl.pallas_call(
        functools.partial(grad_rows_kernel, slots, blocks, len(shares)),
        in_specs=[vmem()] * (2 * len(shares) + 2),
        out_specs=[hbm(), vmem()],
        out_shape=[hbm_shape(rows, 2 * hidden), shape_of(blocks * rows, cols)],
        scratch_shapes=[pltpu.VMEM((rows, 2 * hidden), BF16), pltpu.SemaphoreType.DMA],
        compiler_params=params(32),
        cost_estimate=cost(4 * rows * part * hidden, 4 * part * hidden),
        name="gradient_rows",
    )(*shares, *backs, w_gate, w_up)


def weights_kernel(rows_in_ref, rows_up_ref, act_ref, grad_act_ref, gate_ref, up_ref, down_ref):
    hidden = gate_ref.shape[2]
    rows_in = rows_in_ref[0]
    gate_ref[0] = dot(rows_in, grad_act_ref[:, :hidden], ((0,), (0,))).astype(BF16)
    up_ref[0] = dot(rows_in, grad_act_ref[:, hidden:], ((0,), (0,))).astype(BF16)
    down_ref[0] = dot(act_ref[...], rows_up_ref[0], ((0,), (0,))).astype(BF16)


def weight_grads(rows_in, rows_up, act, grad_act):
    blocks, total, width = rows_in.shape
    part = blocks * width
    hidden = act.shape[1]
    cols = block_of(width, 640)
    steps = width // cols
    chunk = pl.BlockSpec((1, total, cols), lambda k, b: (k, 0, b))
    tall = pl.BlockSpec((1, cols, hidden), lambda k, b: (0, k * steps + b, 0))
    return pl.pallas_call(
        weights_kernel,
        grid=(blocks, steps),
        in_specs=[
            chunk,
            chunk,
            pl.BlockSpec((total, hidden), lambda k, b: (0, 0)),
            pl.BlockSpec((total, 2 * hidden), lambda k, b: (0, 0)),
        ],
        out_specs=[tall, tall, pl.BlockSpec((1, hidden, cols), lambda k, b: (0, 0, k * steps + b))],
        out_shape=[shape_of(1, part, hidden), shape_of(1, part, hidden), shape_of(1, hidden, part)],
        compiler_params=params(),
        cost_estimate=cost(6 * total * part * hidden, 6 * part * hidden),
        name="weight_grads",
    )(*[in_hbm(value) for value in (rows_in, rows_up, act, grad_act)])


def back_rows(back_ref, half, halves, run):
    total = back_ref.shape[0]
    return jnp.concatenate([back_ref[start : start + run] for start in range(half * run, total, halves * run)], axis=0)


def put_columns(held_ref, target_ref, sems, half, block, start=None):
    blocks, _, cols = held_ref.shape[1:]
    start = (half * blocks + block) * cols if start is None else start
    copy = pltpu.make_async_copy(held_ref.at[half, block], target_ref.at[:, pl.ds(start, cols)], sems.at[half, block])
    copy.start()
    return copy


def mixed_kernel(picks_ref, gates_ref, cot_ref, back_ref, mixed_ref, gate_grad_ref, put_ref, held_ref, sems):
    slots, experts = picks_ref.shape
    halves, blocks, tokens, cols = held_ref.shape
    rows = experts * blocks * slots
    hit = spread_row(picks_ref[...].astype(F32), blocks).astype(jnp.int32) == iota((tokens, rows), 0)
    scale = spread_row(gates_ref[...], blocks)
    of_block = iota((tokens, rows), 1) % (blocks * slots) // slots
    run = planes_of(experts) * blocks * slots
    backs = [back_rows(back_ref, half, halves, run) for half in range(halves)]
    copies = []
    products = None
    for block in range(blocks):
        inside = hit & (of_block == block)
        put_ref[block] = one_hot(inside)
        rest = jnp.where(inside, scale, 0.0)
        pieces = []
        for _ in range(3):
            pieces.append(rest.astype(BF16))
            rest = rest - pieces[-1].astype(F32)
        for half in range(halves):
            back = backs[half]
            held_ref[half, block] = added([dot(piece, back) for piece in pieces]).astype(BF16)
            copies.append(put_columns(held_ref, mixed_ref, sems, half, block))
            place = half * blocks + block
            product = dot(cot_ref[:, place * cols : (place + 1) * cols], back, ((1,), (1,)))
            product = jnp.where(inside, product, 0.0)
            products = product if products is None else products + product
    values = jnp.sum(products, axis=0, keepdims=True)
    mine = iota((slots, rows), 1) % slots == iota((slots, rows), 0)
    owner = (expert_at(iota((rows, experts), 0) // (blocks * slots), experts) == iota((rows, experts), 1)).astype(F32)
    gate_grad_ref[...] = exact_dot(jnp.where(mine, values, 0.0), owner)
    for copy in copies:
        copy.wait()


def mix_rows(back, cotangent, picks, gates, halves, blocks):
    slots, experts = picks.shape
    tokens, width = cotangent.shape
    cols = width // (halves * blocks)
    rows = experts * blocks * slots
    return pl.pallas_call(
        mixed_kernel,
        in_specs=[vmem()] * 4,
        out_specs=[hbm(), vmem(), vmem()],
        out_shape=[shape_of(tokens, width), shape_of(slots, experts, dtype=F32), shape_of(blocks, tokens, rows)],
        scratch_shapes=[pltpu.VMEM((halves, blocks, tokens, cols), BF16), pltpu.SemaphoreType.DMA((halves, blocks))],
        compiler_params=params(16),
        cost_estimate=cost(8 * rows * tokens * width, 4 * tokens * width),
        name="mixed_rows",
    )(picks, gates, cotangent, back)


def mix_half(half, put_ref, pieces_ref, cot_ref, back_ref, target_ref, held_ref, sems):
    blocks, tokens, cols = held_ref.shape
    back = back_ref[...]
    copies = []
    products = None
    for block in range(blocks):
        start = pl.multiple_of((half * blocks + block) * cols, 128)
        held_ref[block] = added([dot(pieces_ref[block, i], back) for i in range(3)]).astype(BF16)
        copies.append(pltpu.make_async_copy(held_ref.at[block], target_ref.at[:, pl.ds(start, cols)], sems.at[block]))
        copies[-1].start()
        product = dot(cot_ref[:, pl.ds(start, cols)], back, ((1,), (1,))) * put_ref[block].astype(F32)
        products = product if products is None else products + product
    return jnp.sum(products, axis=0, keepdims=True), copies


def near_kernel(picks_ref, gates_ref, cot_ref, back_ref, mixed_ref, put_ref, pieces_ref, sums_ref, held_ref, sems):
    slots = picks_ref.shape[0]
    blocks, tokens, rows = put_ref.shape
    hit = spread_row(picks_ref[...].astype(F32), blocks).astype(jnp.int32) == iota((tokens, rows), 0)
    scale = spread_row(gates_ref[...], blocks)
    of_block = iota((tokens, rows), 1) % (blocks * slots) // slots
    for block in range(blocks):
        inside = hit & (of_block == block)
        put_ref[block] = one_hot(inside)
        rest = jnp.where(inside, scale, 0.0)
        for i in range(3):
            piece = rest.astype(BF16)
            pieces_ref[block, i] = piece
            rest = rest - piece.astype(F32)
    half = lax.axis_index("dp")
    sums_ref[...], copies = mix_half(half, put_ref, pieces_ref, cot_ref, back_ref, mixed_ref, held_ref, sems)
    for copy in copies:
        copy.wait()


def far_kernel(
    slots, put_ref, pieces_ref, sums_ref, cot_ref, back_ref, _, mixed_ref, gate_grad_ref, held_ref, sems
):
    blocks, _, rows = put_ref.shape
    experts = gate_grad_ref.shape[1]
    half = 1 - lax.axis_index("dp")
    values, copies = mix_half(half, put_ref, pieces_ref, cot_ref, back_ref, mixed_ref, held_ref, sems)
    values = values + sums_ref[...]
    mine = iota((slots, rows), 1) % slots == iota((slots, rows), 0)
    owner = (expert_at(iota((rows, experts), 0) // (blocks * slots), experts) == iota((rows, experts), 1)).astype(F32)
    gate_grad_ref[...] = exact_dot(jnp.where(mine, values, 0.0), owner)
    for copy in copies:
        copy.wait()


def mix_halves(own, other, cotangent, picks, gates, blocks):
    slots, experts = picks.shape
    tokens, width = cotangent.shape
    rows, cols = own.shape
    scratch = [pltpu.VMEM((blocks, tokens, cols), BF16), pltpu.SemaphoreType.DMA((blocks,))]
    work = cost(4 * rows * tokens * width, 2 * tokens * width)
    mixed, put, pieces, sums = pl.pallas_call(
        near_kernel,
        in_specs=[vmem()] * 4,
        out_specs=[hbm()] + [vmem()] * 3,
        out_shape=[
            hbm_shape(tokens, width),
            shape_of(blocks, tokens, rows),
            shape_of(blocks, 3, tokens, rows),
            shape_of(1, rows, dtype=F32),
        ],
        scratch_shapes=scratch,
        compiler_params=params(16),
        cost_estimate=work,
        name="mixed_near",
    )(picks, gates, cotangent, own)
    mixed, gate_grad = pl.pallas_call(
        functools.partial(far_kernel, slots),
        in_specs=[vmem()] * 5 + [hbm()],
        out_specs=[hbm(), vmem()],
        out_shape=[hbm_shape(tokens, width), shape_of(slots, experts, dtype=F32)],
        scratch_shapes=scratch,
        input_output_aliases={5: 0},
        compiler_params=params(16),
        cost_estimate=work,
        name="mixed_far",
    )(put, pieces, sums, cotangent, other, in_hbm(mixed))
    return mixed, gate_grad, put


def part_kernel(joined_ref, own_ref, other_ref, sems):
    half = lax.axis_index("dp")
    copies = [
        pltpu.make_async_copy(joined_ref.at[:, half], own_ref, sems.at[0]),
        pltpu.make_async_copy(joined_ref.at[:, 1 - half], other_ref, sems.at[1]),
    ]
    for copy in copies:
        copy.start()
    for copy in copies:
        copy.wait()


def part_rows(joined, experts):
    rows, cols = joined.shape
    shape = (experts, rows // (2 * experts), cols)
    parted = pl.pallas_call(
        part_kernel,
        in_specs=[pl.BlockSpec(memory_space=pl.ANY)],
        out_specs=[pl.BlockSpec(memory_space=pl.ANY)] * 2,
        out_shape=[shape_of(*shape)] * 2,
        scratch_shapes=[pltpu.SemaphoreType.DMA((2,))],
        compiler_params=params(16),
        cost_estimate=cost(0, 4 * rows * cols),
        name="part_rows",
    )(joined.reshape(experts, 2, *shape[1:]))
    return [value.reshape(rows // 2, cols) for value in parted]


def token_grad_kernel(run, _, put_ref, back_ref, grad_ref, held_ref, sems):
    halves, blocks = held_ref.shape[:2]
    copies = []
    for half in range(halves):
        back = back_rows(back_ref, half, halves, run)
        for block in range(blocks):
            held_ref[half, block] = dot(put_ref[block], back).astype(BF16)
            copies.append(put_columns(held_ref, grad_ref, sems, half, block))
    for copy in copies:
        copy.wait()


def token_grads(back, put, halves, run, after):
    blocks, tokens, rows = put.shape
    cols = back.shape[1]
    width = halves * blocks * cols
    return pl.pallas_call(
        functools.partial(token_grad_kernel, run),
        in_specs=[hbm()] + [vmem()] * 2,
        out_specs=hbm(),
        out_shape=shape_of(tokens, width),
        scratch_shapes=[pltpu.VMEM((halves, blocks, tokens, cols), BF16), pltpu.SemaphoreType.DMA((halves, blocks))],
        compiler_params=params(16),
        cost_estimate=cost(2 * rows * tokens * width, 2 * tokens * width),
        name="token_grads",
    )(in_hbm(after), put, back)


def to_owners(halves, experts, messages):
    planes = planes_of(experts)
    order = [
        half * experts + plane * (experts // planes) + place
        for place in range(experts // planes)
        for half in range(halves)
        for plane in range(planes)
    ]
    return lax.all_to_all(
        messages, EVERYONE, split_axis=0, concat_axis=0, tiled=True, axis_index_groups=[order]
    )


def to_experts(experts, messages):
    order = [expert_at(place, experts) for place in range(experts)]
    return lax.all_to_all(messages, "expert", split_axis=0, concat_axis=0, tiled=True, axis_index_groups=[order])


def dp_shares(own, halves):
    shares = [own] + [
        lax.ppermute(own, "dp", [(i, (i + shift) % halves) for i in range(halves)]) for shift in range(1, halves)
    ]
    return shares if halves <= 2 else [added([share.astype(F32) for share in shares])]


def body(halves, tokens, cotangent, picks, gates, w_gate, w_up, w_down):
    experts, slots = picks.shape[1:]
    scatter = functools.partial(to_owners, halves, experts)
    blocks = 2 if tokens.shape[1] // halves % 256 == 0 else 1
    picks_t = picks[0].T
    gates_t = gates[0].T
    messages_in = send_rows(tokens, (picks_t,), halves, blocks)
    arrived_in = scatter(messages_in)
    if halves == 2:
        leaving = side_rows(cotangent, picks_t, gates_t, blocks, 1, messages_in)
        other = lax.ppermute(leaving, "dp", [(0, 1), (1, 0)])
        own = side_rows(cotangent, picks_t, gates_t, blocks, 0, messages_in)
        arrived_up = to_experts(experts, join_rows(own, other, experts))
    else:
        arrived_up = scatter(send_rows(cotangent, (picks_t, gates_t), halves, blocks))
    own_sums, rows_in = in_sums(arrived_in, w_gate, w_up, blocks, slots)
    shares = dp_shares(own_sums, halves)
    place = functools.partial(split_place, halves=2, planes=planes_of(experts)) if halves == 2 else same_place
    act, outputs = out_rows(shares, w_down, blocks, slots, place)
    back_out = to_experts(experts, outputs) if halves == 2 else scatter(outputs)
    own_back, rows_up = back_sums(arrived_up, w_down, blocks, slots, place)
    backs = dp_shares(own_back, halves)
    near_gate, near_up = bring((w_gate, w_up), own_back)
    grad_act, gradients = grad_rows(shares, backs, near_gate, near_up, blocks, slots)
    back_grad = scatter(gradients)
    grad_gate_w, grad_up_w, grad_down = weight_grads(rows_in, rows_up, act, grad_act)
    if halves == 2:
        own_out, other_out = part_rows(back_out, experts)
        other_out = lax.ppermute(other_out, "dp", [(0, 1), (1, 0)])
        mixed, gate_grad, put = mix_halves(own_out, other_out, cotangent, picks_t, gates_t, blocks)
    else:
        mixed, gate_grad, put = mix_rows(back_out, cotangent, picks_t, gates_t, halves, blocks)
    token_grad = token_grads(back_grad, put, halves, planes_of(experts) * blocks * slots, gate_grad)
    return mixed, token_grad, gate_grad.T[None], grad_gate_w, grad_up_w, grad_down


def solution(mesh):
    rows = P(("dp", "expert"), None)
    lists = P(("dp", "expert"), None, None)
    tall = P("expert", "dp", None)
    wide = P("expert", None, "dp")
    return jax.shard_map(
        functools.partial(body, mesh.shape["dp"]),
        mesh=mesh,
        in_specs=(rows, rows, lists, lists, tall, tall, wide),
        out_specs=(rows, rows, lists, tall, tall, wide),
        check_vma=False,
    )
```
